512 devices in a mesh: tiles: 256 (over x, z, y_hi, core), dp: 2 (over y_lo).
Axes of the slice: x: 4, y: 8 (y_hi: 4, y_lo: 2; y = y_hi * 2 + y_lo), z: 8, core: 2. Of those that a mesh axis runs over, the one named last changes fastest.
Arguments:
- fields: bfloat16 [2, 768, 16, 16, 256], P('dp', 'tiles'), may hold values from -6 to 6
- grad_out: bfloat16 [2, 768, 16, 16, 256], P('dp', 'tiles'), may hold values from -6 to 6
- block_count: int32 [256], P('tiles'), may hold values from 1 to 3, as said below
- ocean: int32 [768], P('tiles'), may hold values from 0 to 1, as said below
- kernel: bfloat16 [7, 7, 256], replicated, may hold values from -0.875 to 0.875
- ln_gain: float32 [256], replicated, may hold values from 0.1 to 1.9
- w_in: bfloat16 [256, 1024], replicated, may hold values from -0.375 to 0.375
- w_out: bfloat16 [1024, 256], replicated, may hold values from -0.1875 to 0.1875
- layer_scale: float32 [256], replicated, may hold values from 0.3 to 1.5
Outputs:
- state_next: bfloat16 [2, 768, 16, 16, 256], P('dp', 'tiles')
- grad_fields: bfloat16 [2, 768, 16, 16, 256], P('dp', 'tiles')
- grad_kernel: float32 [7, 7, 256], replicated
- grad_gain: float32 [256], replicated
- grad_w_in: float32 [256, 1024], replicated
- grad_w_out: float32 [1024, 256], replicated
- grad_scale: float32 [256], replicated
The draws below stay inside these ranges and needn't reach their ends.
Inputs may be any that keep to these rules, and one draw needn't show every extreme that they name: Index i of tiles owns block_count[i] consecutive cycle tiles in its first slots, in the cycle order of the first step; index i and index i + H (i < H, H half the number of entries) own equally many; some index owns 3 and some index owns one. 1 marks an ocean tile; the first and the last cycle tile that each index of tiles owns are ocean.
All inputs are finite; a program needn't handle non-finite values.
Results may differ from the reference program's by a relative error of at most 0.0066.
Values may be sent and summed in bfloat16 or wider, within the bound.
A program may use at most 64 MiB of HBM per device.

```python
import math
import jax
import jax.numpy as jnp
from jax import lax

C = 256
HID = 1024
KSIZE = 7
TILE = 16
SLOTS = 3
SAMPLES = 2
SLOT_TOTAL = 768
CELLS = 393216


def cycle_counts(key):
    key = jax.random.fold_in(key, 11)
    half_cycle = SLOT_TOTAL // SLOTS // 2
    owned_counts = jax.random.randint(jax.random.fold_in(key, 1), (half_cycle,), 1, SLOTS + 1)
    shuffled = jax.random.permutation(jax.random.fold_in(key, 2), half_cycle)
    owned_counts = owned_counts.at[shuffled[0]].set(SLOTS).at[shuffled[1]].set(1)
    return jnp.concatenate([owned_counts, owned_counts]).astype(jnp.int32)


def draw_block_count(key, part):
    return cycle_counts(key)


def draw_ocean(key, part):
    owned_counts = cycle_counts(key)
    key = jax.random.fold_in(key, 12)
    flags = (jax.random.randint(key, (SLOT_TOTAL,), 0, 4) < 3).astype(jnp.int32)
    slot_ids = jnp.arange(SLOT_TOTAL, dtype=jnp.int32)
    position = slot_ids % SLOTS
    owner_count = owned_counts[slot_ids // SLOTS]
    run_end = jnp.logical_or(position == 0, position == owner_count - 1)
    return jnp.where(run_end, 1, flags).astype(jnp.int32)


def levels(key, shape, split, smallest, largest):
    level = 1.0
    for dim, parts in split:
        heights = jax.random.uniform(jax.random.fold_in(jax.random.fold_in(key, 6), dim), (parts,), jnp.float32, smallest / len(split), largest / len(split))
        level = level * jnp.repeat(jnp.exp(heights), shape[dim] // parts).reshape((-1,) + (1,) * (len(shape) - 1 - dim))
    return level


def bell_draw(key, extent, width, bound, shards=(), held_as=jnp.bfloat16):
    drawn = width * jax.random.normal(key, extent, jnp.float32)
    if shards:
        drawn = drawn * levels(key, extent, shards, -0.22, 0.18)
    return jnp.clip(drawn, -bound, bound).astype(held_as)


def setup_inputs(seed: int = 0) -> dict:
    arg_keys = jax.random.split(jax.random.key(seed), 10)
    return {
        "fields": bell_draw(arg_keys[0], (SAMPLES, SLOT_TOTAL, TILE, TILE, C), 1.0, 6.0, ((0, 2), (1, 256))),
        "grad_out": bell_draw(arg_keys[1], (SAMPLES, SLOT_TOTAL, TILE, TILE, C), 1.0, 6.0, ((0, 2), (1, 256))),
        "block_count": draw_block_count(jax.random.fold_in(arg_keys[9], 71), 0),
        "ocean": draw_ocean(jax.random.fold_in(arg_keys[9], 71), 0),
        "kernel": bell_draw(arg_keys[4], (KSIZE, KSIZE, C), (KSIZE * KSIZE) ** -0.5, 0.875),
        "ln_gain": jnp.clip(1.0 + 0.18 * jax.random.normal(arg_keys[5], (C,), jnp.float32), 0.1, 1.9),
        "w_in": bell_draw(arg_keys[6], (C, HID), C ** -0.5, 0.375),
        "w_out": bell_draw(arg_keys[7], (HID, C), HID ** -0.5, 0.1875),
        "layer_scale": jnp.clip(jnp.exp(jax.random.uniform(arg_keys[8], (C,), jnp.float32, math.log(0.3), math.log(1.5))), 0.3, 1.5),
    }


EPS = 1e-06

def gelu_tanh(inputs):
    return jax.nn.gelu(inputs, approximate=True)

def depthwise(padded, kernel_f, tile_rows, tile_cols):
    running = jnp.zeros(padded.shape[:-3] + (tile_rows, tile_cols, padded.shape[-1]), jnp.float32)
    for row_shift in range(KSIZE):
        for col_shift in range(KSIZE):
            window = padded[..., row_shift:row_shift + tile_rows, col_shift:col_shift + tile_cols, :]
            running = running + kernel_f[row_shift, col_shift] * window.astype(jnp.float32)
    return running

def kernel_terms(conv_grad, padded, tile_rows, tile_cols):
    grad_f = conv_grad.astype(jnp.float32)
    leading = tuple(range(grad_f.ndim - 1))
    stacked = []
    for row_shift in range(KSIZE):
        taps = []
        for col_shift in range(KSIZE):
            window = padded[..., row_shift:row_shift + tile_rows, col_shift:col_shift + tile_cols, :]
            taps.append(lax.optimization_barrier(jnp.sum(grad_f * window.astype(jnp.float32), axis=leading)))
        stacked.append(jnp.stack(taps))
    return jnp.stack(stacked)

def spread(conv_grad, kernel_f, tile_rows, tile_cols):
    reach = KSIZE - 1
    widths = [(0, 0)] * (conv_grad.ndim - 3) + [(reach, reach), (reach, reach), (0, 0)]
    grad_f = jnp.pad(conv_grad.astype(jnp.float32), widths)
    running = jnp.zeros(conv_grad.shape[:-3] + (tile_rows + reach, tile_cols + reach, conv_grad.shape[-1]), jnp.float32)
    for row_shift in range(KSIZE):
        for col_shift in range(KSIZE):
            window = grad_f[..., reach - row_shift:reach - row_shift + tile_rows + reach, reach - col_shift:reach - col_shift + tile_cols + reach, :]
            running = running + kernel_f[row_shift, col_shift] * window
    return running

def make_block(ln_gain, w_in, w_out, layer_scale):

    def block_step(totals, inputs):
        convolved, skip_rows, cell_mask, tangent = inputs
        row_mean = lax.optimization_barrier(jnp.mean(convolved, axis=-1, keepdims=True))
        centred = convolved - row_mean
        variance = lax.optimization_barrier(jnp.mean(centred * centred, axis=-1, keepdims=True))
        inverse = lax.rsqrt(variance + EPS)
        yhat = centred * inverse
        normed = (yhat * ln_gain).astype(jnp.bfloat16)
        preact = jnp.dot(normed, w_in, preferred_element_type=jnp.float32)
        activated = gelu_tanh(preact).astype(jnp.bfloat16)
        projected = jnp.dot(activated, w_out, preferred_element_type=jnp.float32)
        tangent_f = tangent.astype(jnp.float32)
        state = (cell_mask * (skip_rows.astype(jnp.float32) + layer_scale * projected)).astype(jnp.bfloat16)
        dproj = (cell_mask * layer_scale * tangent_f).astype(jnp.bfloat16)
        scale_part = lax.optimization_barrier(jnp.sum(cell_mask * tangent_f * projected, axis=0))
        w_out_part = lax.dot_general(activated, dproj, (((0,), (0,)), ((), ())), preferred_element_type=jnp.float32)
        dactivated = lax.dot_general(dproj, w_out, (((1,), (1,)), ((), ())), preferred_element_type=jnp.float32)
        unused, pullback = jax.vjp(gelu_tanh, preact)
        dpreact = pullback(dactivated)[0].astype(jnp.bfloat16)
        w_in_part = lax.dot_general(normed, dpreact, (((0,), (0,)), ((), ())), preferred_element_type=jnp.float32)
        dnormed = lax.dot_general(dpreact, w_in, (((1,), (1,)), ((), ())), preferred_element_type=jnp.float32)
        gain_part = lax.optimization_barrier(jnp.sum(dnormed * yhat, axis=0))
        dhat = dnormed * ln_gain
        conv_grad = inverse * (dhat - lax.optimization_barrier(jnp.mean(dhat, axis=-1, keepdims=True)) - yhat * lax.optimization_barrier(jnp.mean(dhat * yhat, axis=-1, keepdims=True)))
        totals = (totals[0] + gain_part, totals[1] + w_in_part, totals[2] + w_out_part, totals[3] + scale_part)
        return (totals, (state, conv_grad.astype(jnp.bfloat16)))
    return block_step

def pad_tiles(masked, west_slot, east_slot, partner_slot, half_kernel):
    tile_rows = masked.shape[1]
    extended = jnp.concatenate([masked[west_slot][:, :, -half_kernel:], masked, masked[east_slot][:, :, :half_kernel]], axis=2)
    north_rows = extended[partner_slot][:, tile_rows - half_kernel:][:, ::-1, ::-1]
    south_rows = jnp.zeros((masked.shape[0], half_kernel, extended.shape[2], masked.shape[3]), masked.dtype)
    return jnp.concatenate([south_rows, extended, north_rows], axis=1)

def unpad_tiles(dpadded, west_slot, east_slot, partner_slot, half_kernel):
    tile_rows = dpadded.shape[1] - 2 * half_kernel
    tile_cols = dpadded.shape[2] - 2 * half_kernel
    north_rows = dpadded[:, tile_rows + half_kernel:]
    dextended = dpadded[:, half_kernel:tile_rows + half_kernel]
    dextended = dextended.at[:, tile_rows - half_kernel:].add(north_rows[partner_slot][:, ::-1, ::-1])
    core_grad = dextended[:, :, half_kernel:tile_cols + half_kernel]
    core_grad = core_grad.at[:, :, :half_kernel].add(dextended[west_slot][:, :, tile_cols + half_kernel:])
    core_grad = core_grad.at[:, :, tile_cols - half_kernel:].add(dextended[east_slot][:, :, :half_kernel])
    return core_grad

def reference(fields, grad_out, block_count, ocean, kernel, ln_gain, w_in, w_out, layer_scale):
    samples, total_slots, tile_rows, tile_cols, channels = fields.shape
    half_kernel = KSIZE // 2
    blocks = total_slots // SLOTS
    half_blocks = blocks // 2
    cycle_order = jnp.concatenate([jnp.arange(half_blocks, dtype=jnp.int32), jnp.arange(blocks - 1, half_blocks - 1, -1, dtype=jnp.int32)]).astype(jnp.int32)
    counts_by_rank = block_count[cycle_order]
    starts_by_rank = (jnp.cumsum(counts_by_rank) - counts_by_rank).astype(jnp.int32)
    starts = jnp.zeros((blocks,), jnp.int32).at[cycle_order].set(starts_by_rank)
    slot_ids = jnp.arange(total_slots, dtype=jnp.int32)
    owner_index = slot_ids // SLOTS
    position = slot_ids % SLOTS
    cycle_tiles = jnp.sum(block_count).astype(jnp.int32)
    valid = position < block_count[owner_index]
    live = jnp.logical_and(valid, ocean > 0)
    tile_id = jnp.where(valid, starts[owner_index] + position, 0).astype(jnp.int32)
    target = jnp.where(valid, tile_id, total_slots).astype(jnp.int32)
    slot_of_tile = jnp.zeros((total_slots + 1,), jnp.int32).at[target].set(slot_ids)
    west_slot = slot_of_tile[(tile_id + cycle_tiles - 1) % cycle_tiles]
    east_slot = slot_of_tile[(tile_id + 1) % cycle_tiles]
    partner_slot = slot_of_tile[cycle_tiles - 1 - tile_id]
    slot_mask = live.astype(jnp.float32)
    kernel_f = kernel.astype(jnp.float32)
    block_step = make_block(ln_gain, w_in, w_out, layer_scale)
    block_rows = SLOTS * tile_rows * tile_cols

    def one_sample(sample_pair):
        sample_field, tangent = sample_pair
        masked = sample_field * slot_mask.astype(jnp.bfloat16)[:, None, None, None]
        padded = pad_tiles(masked, west_slot, east_slot, partner_slot, half_kernel)
        convolved = depthwise(padded, kernel_f, tile_rows, tile_cols)
        cell_mask = jnp.broadcast_to(slot_mask[:, None], (total_slots, tile_rows * tile_cols)).reshape(blocks, block_rows, 1)
        start_totals = (jnp.zeros((channels,), jnp.float32), jnp.zeros((channels, HID), jnp.float32), jnp.zeros((HID, channels), jnp.float32), jnp.zeros((channels,), jnp.float32))
        totals, outputs = lax.scan(block_step, start_totals, (convolved.reshape(blocks, block_rows, channels), masked.reshape(blocks, block_rows, channels), cell_mask, tangent.reshape(blocks, block_rows, channels)))
        state = outputs[0].reshape(sample_field.shape)
        conv_grad = outputs[1].reshape(sample_field.shape)
        kernel_part = kernel_terms(conv_grad, padded, tile_rows, tile_cols)
        dpadded = spread(conv_grad, kernel_f, tile_rows, tile_cols)
        dmasked = unpad_tiles(dpadded, west_slot, east_slot, partner_slot, half_kernel)
        grad_field = (slot_mask[:, None, None, None] * (tangent.astype(jnp.float32) + dmasked)).astype(jnp.bfloat16)
        return (state, grad_field, kernel_part, totals)
    states, grad_fields, kernel_parts, totals = lax.map(one_sample, (fields, grad_out))
    norm = CELLS ** (-0.5)
    return (states, grad_fields, lax.optimization_barrier(jnp.sum(kernel_parts, axis=0)) * norm, lax.optimization_barrier(jnp.sum(totals[0], axis=0)) * norm, lax.optimization_barrier(jnp.sum(totals[1], axis=0)) * norm, lax.optimization_barrier(jnp.sum(totals[2], axis=0)) * norm, lax.optimization_barrier(jnp.sum(totals[3], axis=0)) * norm)
```

```python
import functools

import jax
import jax.numpy as jnp
from jax import lax
from jax.experimental import pallas as pl
from jax.experimental.pallas import tpu as pltpu
from jax.sharding import PartitionSpec as P

HID = 1024
KSIZE = 7
NX, NZ, NYH = 4, 8, 4
NY = 2 * NYH
GROUP_X, GROUP_Y, GROUP_Z = 1024, 512, 512
HALF = GROUP_X + GROUP_Y + GROUP_Z
SMALL = 64
XR, YR, ZR = GROUP_X // NX, GROUP_Y // NY, GROUP_Z // NZ
XA, XB = XR // 2 // NY, XR // 2 // NZ
YX, ZX = YR // NX, ZR // NX
SR = SMALL // NY
F32, BF16 = jnp.float32, jnp.bfloat16


class Place:
    def __init__(self):
        t = lax.axis_index("tiles")
        self.t = t
        self.lo = lax.axis_index("dp")
        self.core = t % 2
        self.yh = (t // 2) % NYH
        self.z = (t // (2 * NYH)) % NZ
        self.x = t // (2 * NYH * NZ)
        self.y = self.yh * 2 + self.lo

    def along(self, axis, step):
        if axis == "core":
            place = 1 - self.core
            return place, (self.t + place - self.core, self.lo)
        if axis == "x":
            place = (self.x + step) % NX
            return place, (self.t + (place - self.x) * (2 * NYH * NZ), self.lo)
        if axis == "z":
            place = (self.z + step) % NZ
            return place, (self.t + (place - self.z) * (2 * NYH), self.lo)
        place = (self.y + step) % NY
        return place, (self.t + (place // 2 - self.yh) * 2, place % 2)


COUNT = {"x": NX, "y": NY, "z": NZ, "core": 2}


def steps(axis):
    n = COUNT[axis]
    near = []
    for d in range(1, n // 2 + 1):
        near += [d, n - d] if d != n - d else [d]
    return near


def send(src, dst, send_sem, recv_sem, device):
    pltpu.make_async_remote_copy(
        src_ref=src,
        dst_ref=dst,
        send_sem=send_sem,
        recv_sem=recv_sem,
        device_id=device,
        device_id_type=pl.DeviceIdType.MESH,
    ).start()


def await_bytes(like, sem):
    pltpu.make_async_copy(like, like, sem).wait()


def rows(start, size):
    return pl.ds(pl.multiple_of(start, size), size)


def reduce_kernel(
    wide, small, out, small_out, core_out, core_in, held, x_in, y_in, z_in, p_out, xa_in, xb_in,
    w_out, w_in, zz, yy, s_core, s_y, s_z, s_x, s_held, ss, rs
):
    here = Place()
    c, x, y, z = here.core, here.x, here.y, here.z
    me = {"x": x, "y": y, "z": z}
    barrier = pltpu.get_barrier_semaphore()
    greeted = 0
    for axis in ("core", "x", "y", "z"):
        for d in steps(axis):
            pl.semaphore_signal(
                barrier, inc=1, device_id=here.along(axis, d)[1], device_id_type=pl.DeviceIdType.MESH
            )
            greeted += 1
    pl.semaphore_wait(barrier, greeted)
    Y0, Z0 = GROUP_X, GROUP_X + GROUP_Y
    regions = [(0, GROUP_X), (Y0, GROUP_Y), (Z0, GROUP_Z)]
    partner = here.along("core", 1)[1]

    send(small.at[1 - c], s_core, ss.at[3], rs.at[3], partner)
    for i in (1, 2, 0):
        start, size = regions[i]
        core_out[pl.ds(start, size)] = wide[1 - c, pl.ds(start, size)].astype(BF16)
        span = pl.ds(start, size)
        send(core_out.at[span], core_in.at[span], ss.at[i], rs.at[i], partner)

    await_bytes(s_core, rs.at[3])
    s_held[...] = small[c] + s_core[...]
    for d in steps("y"):
        place, device = here.along("y", d)
        send(s_held.at[rows(place * SR, SR)], s_y.at[d - 1], ss.at[7], rs.at[7], device)
    for i, axis, size, landing in ((1, "y", YR, y_in), (2, "z", ZR, z_in), (0, "x", XR, x_in)):
        start, extent = regions[i]
        span = pl.ds(start, extent)
        await_bytes(core_in.at[span], rs.at[i])
        held[span] = (wide[c, span] + core_in[span].astype(F32)).astype(BF16)
        for d in steps(axis):
            place, device = here.along(axis, d)
            send(
                held.at[rows(start + place * size, size)], landing.at[d - 1], ss.at[4 + i], rs.at[4 + i], device
            )

    def own(start, size):
        span = rows(start, size)
        return wide[c, span] + core_in[span].astype(F32)

    def total(first, landing):
        for k in range(landing.shape[0]):
            first = first + landing[k].astype(F32)
        return first

    await_bytes(s_y, rs.at[7])
    s_own = total(s_held[rows(y * SR, SR)], s_y)
    s_z[z] = s_own
    for d in steps("z"):
        send(s_z.at[z], s_z.at[z], ss.at[11], rs.at[11], here.along("z", d)[1])
    await_bytes(y_in, rs.at[5])
    y_own = total(own(Y0 + y * YR, YR), y_in)
    for k in range(NX):
        w_out[k, :YX] = y_own[k * YX : (k + 1) * YX].astype(BF16)
    await_bytes(z_in, rs.at[6])
    z_own = total(own(Z0 + z * ZR, ZR), z_in)
    for k in range(NX):
        w_out[k, YX:] = z_own[k * ZX : (k + 1) * ZX].astype(BF16)
    for d in steps("x"):
        place, device = here.along("x", d)
        send(w_out.at[place], w_in.at[d - 1], ss.at[10], rs.at[10], device)
    await_bytes(x_in, rs.at[4])
    p_own = total(own(x * XR, XR), x_in)
    p_out[...] = p_own.astype(BF16)
    for d in steps("y"):
        place, device = here.along("y", d)
        send(p_out.at[rows(place * XA, XA)], xa_in.at[d - 1], ss.at[8], rs.at[8], device)
    for d in steps("z"):
        place, device = here.along("z", d)
        send(p_out.at[rows(XR // 2 + place * XB, XB)], xb_in.at[d - 1], ss.at[9], rs.at[9], device)

    await_bytes(s_z.at[pl.ds(0, NZ - 1)], rs.at[11])
    s_x[x] = jnp.sum(s_z[...], axis=0)
    for d in steps("x"):
        send(s_x.at[x], s_x.at[x], ss.at[14], rs.at[14], here.along("x", d)[1])

    await_bytes(w_in, rs.at[10])
    mine = w_out[x].astype(F32)
    mine = total(mine, w_in)
    await_bytes(xa_in, rs.at[8])
    zz[z, :XA] = total(p_out[rows(y * XA, XA)].astype(F32), xa_in).astype(BF16)
    zz[z, XA:] = mine[:YX].astype(BF16)
    for d in steps("z"):
        send(zz.at[z], zz.at[z], ss.at[12], rs.at[12], here.along("z", d)[1])
    await_bytes(xb_in, rs.at[9])
    yy[y, :XB] = total(p_out[rows(XR // 2 + z * XB, XB)].astype(F32), xb_in).astype(BF16)
    yy[y, XB:] = mine[YX:].astype(BF16)
    for d in steps("y"):
        send(yy.at[y], yy.at[y], ss.at[13], rs.at[13], here.along("y", d)[1])

    def line_total(landing, count):
        run = landing[0].astype(F32)
        for k in range(1, count):
            run = run + landing[k].astype(F32)
        return run

    await_bytes(s_x.at[pl.ds(0, NX - 1)], rs.at[14])
    small_out[c, rows(y * SR, SR)] = jnp.sum(s_x[...], axis=0)

    def spread_out(ref, axis, sem):
        for d in steps(axis):
            send(ref, ref, ss.at[sem], rs.at[sem], here.along(axis, d)[1])

    spread_out(small_out.at[c, rows(y * SR, SR)], "y", 15)
    await_bytes(zz.at[pl.ds(0, NZ - 1)], rs.at[12])
    zsum = line_total(zz, NZ).astype(BF16)
    out[c, rows(x * XR + y * XA, XA)] = zsum[:XA]
    out[c, rows(Y0 + y * YR + x * YX, YX)] = zsum[XA:]
    spread_out(out.at[c, rows(x * XR + y * XA, XA)], "y", 16)
    spread_out(out.at[c, rows(Y0 + y * YR + x * YX, YX)], "x", 17)
    await_bytes(yy.at[pl.ds(0, NY - 1)], rs.at[13])
    ysum = line_total(yy, NY).astype(BF16)
    out[c, rows(x * XR + XR // 2 + z * XB, XB)] = ysum[:XB]
    out[c, rows(Z0 + z * ZR + x * ZX, ZX)] = ysum[XB:]
    spread_out(out.at[c, rows(x * XR + XR // 2 + z * XB, XB)], "z", 18)
    spread_out(out.at[c, rows(Z0 + z * ZR + x * ZX, ZX)], "x", 19)

    await_bytes(out.at[0, pl.ds(0, (NX - 1) * YX)], rs.at[17])
    spread_out(out.at[c, rows(Y0 + y * YR, YR)], "y", 20)
    await_bytes(out.at[0, pl.ds(0, (NX - 1) * ZX)], rs.at[19])
    spread_out(out.at[c, rows(Z0 + z * ZR, ZR)], "z", 21)
    await_bytes(out.at[0, pl.ds(0, (NY - 1) * XA)], rs.at[16])
    await_bytes(out.at[0, pl.ds(0, (NZ - 1) * XB)], rs.at[18])
    spread_out(out.at[c, rows(x * XR, XR)], "x", 22)

    await_bytes(small_out.at[0, pl.ds(0, (NY - 1) * SR)], rs.at[15])
    send(small_out.at[c], small_out.at[c], ss.at[23], rs.at[23], partner)
    for i, sem, got in ((1, 20, (NY - 1) * YR), (2, 21, (NZ - 1) * ZR), (0, 22, (NX - 1) * XR)):
        await_bytes(out.at[0, pl.ds(0, got)], rs.at[sem])
        ref = out.at[c, pl.ds(*regions[i])]
        send(ref, ref, ss.at[24 + i], rs.at[24 + i], partner)
    await_bytes(small_out.at[0], rs.at[23])
    for i in range(3):
        await_bytes(out.at[0, pl.ds(*regions[i])], rs.at[24 + i])

    for i in range(3):
        await_bytes(core_out.at[pl.ds(*regions[i])], ss.at[i])
        await_bytes(out.at[0, pl.ds(*regions[i])], ss.at[24 + i])
    await_bytes(s_core, ss.at[3])
    await_bytes(x_in, ss.at[4])
    await_bytes(y_in, ss.at[5])
    await_bytes(z_in, ss.at[6])
    await_bytes(s_y, ss.at[7])
    await_bytes(xa_in, ss.at[8])
    await_bytes(xb_in, ss.at[9])
    await_bytes(w_in, ss.at[10])
    await_bytes(s_z.at[pl.ds(0, NZ - 1)], ss.at[11])
    await_bytes(zz.at[pl.ds(0, NZ - 1)], ss.at[12])
    await_bytes(yy.at[pl.ds(0, NY - 1)], ss.at[13])
    await_bytes(s_x.at[pl.ds(0, NX - 1)], ss.at[14])
    await_bytes(small_out.at[0, pl.ds(0, (NY - 1) * SR)], ss.at[15])
    await_bytes(out.at[0, pl.ds(0, (NY - 1) * XA)], ss.at[16])
    await_bytes(out.at[0, pl.ds(0, (NX - 1) * YX)], ss.at[17])
    await_bytes(out.at[0, pl.ds(0, (NZ - 1) * XB)], ss.at[18])
    await_bytes(out.at[0, pl.ds(0, (NX - 1) * ZX)], ss.at[19])
    await_bytes(out.at[0, pl.ds(0, (NY - 1) * YR)], ss.at[20])
    await_bytes(out.at[0, pl.ds(0, (NZ - 1) * ZR)], ss.at[21])
    await_bytes(out.at[0, pl.ds(0, (NX - 1) * XR)], ss.at[22])
    await_bytes(small_out.at[0], ss.at[23])


def reduce_all(wide, small):
    vmem = pl.BlockSpec(memory_space=pltpu.VMEM)
    return pl.pallas_call(
        reduce_kernel,
        out_shape=(
            jax.ShapeDtypeStruct((2, HALF, 128), BF16),
            jax.ShapeDtypeStruct((2, SMALL, 128), F32),
        ),
        in_specs=[vmem, vmem],
        out_specs=(vmem, vmem),
        scratch_shapes=[
            pltpu.VMEM((HALF, 128), BF16),
            pltpu.VMEM((HALF, 128), BF16),
            pltpu.VMEM((HALF, 128), BF16),
            pltpu.VMEM((NX - 1, XR, 128), BF16),
            pltpu.VMEM((NY - 1, YR, 128), BF16),
            pltpu.VMEM((NZ - 1, ZR, 128), BF16),
            pltpu.VMEM((XR, 128), BF16),
            pltpu.VMEM((NY - 1, XA, 128), BF16),
            pltpu.VMEM((NZ - 1, XB, 128), BF16),
            pltpu.VMEM((NX, YX + ZX, 128), BF16),
            pltpu.VMEM((NX - 1, YX + ZX, 128), BF16),
            pltpu.VMEM((NZ, XA + YX, 128), BF16),
            pltpu.VMEM((NY, XB + ZX, 128), BF16),
            pltpu.VMEM((SMALL, 128), F32),
            pltpu.VMEM((NY - 1, SR, 128), F32),
            pltpu.VMEM((NZ, SR, 128), F32),
            pltpu.VMEM((NX, SR, 128), F32),
            pltpu.VMEM((SMALL, 128), F32),
            pltpu.SemaphoreType.DMA((27,)),
            pltpu.SemaphoreType.DMA((27,)),
        ],
        compiler_params=pltpu.CompilerParams(
            collective_id=1, has_side_effects=True, vmem_limit_bytes=32 * 1024 * 1024
        ),
    )(wide, small)


EPS = 1e-06


def passed_along(block, axis, distance):
    devices = range(lax.axis_size(axis))
    route = [(i - distance, i) for i in devices if i - distance in devices]
    return lax.ppermute(block, axis, route)


def from_partner(block, axis, distance):
    count = lax.axis_size(axis)
    route = []
    for low in range(count):
        high = low | 1 << distance
        if high != low and high < count:
            route += [(low, high), (high, low)]
    return lax.ppermute(block, axis, route)


def gelu_tanh(inputs):
    return jax.nn.gelu(inputs, approximate=True)


def depthwise(padded, kernel_f, tile_rows, tile_cols):
    running = jnp.zeros(padded.shape[:-3] + (tile_rows, tile_cols, padded.shape[-1]), jnp.float32)
    for row_shift in range(KSIZE):
        for col_shift in range(KSIZE):
            window = padded[
                ..., row_shift : row_shift + tile_rows, col_shift : col_shift + tile_cols, :
            ]
            running = running + kernel_f[row_shift, col_shift] * window.astype(jnp.float32)
    return running


def kernel_terms(conv_grad, padded, tile_rows, tile_cols):
    grad_f = conv_grad.astype(jnp.float32)
    leading = tuple(range(grad_f.ndim - 1))
    stacked = []
    for row_shift in range(KSIZE):
        taps = []
        for col_shift in range(KSIZE):
            window = padded[
                ..., row_shift : row_shift + tile_rows, col_shift : col_shift + tile_cols, :
            ]
            taps.append(jnp.sum(grad_f * window.astype(jnp.float32), axis=leading))
        stacked.append(jnp.stack(taps))
    return jnp.stack(stacked)


def spread(conv_grad, kernel_f, tile_rows, tile_cols):
    reach = KSIZE - 1
    widths = [(0, 0)] * (conv_grad.ndim - 3) + [(reach, reach), (reach, reach), (0, 0)]
    grad_f = jnp.pad(conv_grad.astype(jnp.float32), widths)
    running = jnp.zeros(
        conv_grad.shape[:-3] + (tile_rows + reach, tile_cols + reach, conv_grad.shape[-1]),
        jnp.float32,
    )
    for row_shift in range(KSIZE):
        for col_shift in range(KSIZE):
            window = grad_f[
                ...,
                reach - row_shift : reach - row_shift + tile_rows + reach,
                reach - col_shift : reach - col_shift + tile_cols + reach,
                :,
            ]
            running = running + kernel_f[row_shift, col_shift] * window
    return running


def make_block(ln_gain, w_in, w_out, layer_scale):

    def block_step(totals, inputs):
        convolved, skip_rows, cell_mask, tangent = inputs
        row_mean = jnp.mean(convolved, axis=-1, keepdims=True)
        centred = convolved - row_mean
        variance = jnp.mean(centred * centred, axis=-1, keepdims=True)
        inverse = lax.rsqrt(variance + EPS)
        yhat = centred * inverse
        normed = (yhat * ln_gain).astype(jnp.bfloat16)
        preact = jnp.dot(normed, w_in, preferred_element_type=jnp.float32)
        activated = gelu_tanh(preact).astype(jnp.bfloat16)
        projected = jnp.dot(activated, w_out, preferred_element_type=jnp.float32)
        tangent_f = tangent.astype(jnp.float32)
        state = (cell_mask * (skip_rows.astype(jnp.float32) + layer_scale * projected)).astype(
            jnp.bfloat16
        )
        dproj = (cell_mask * layer_scale * tangent_f).astype(jnp.bfloat16)
        scale_part = jnp.sum(cell_mask * tangent_f * projected, axis=0)
        w_out_part = lax.dot_general(
            activated, dproj, (((0,), (0,)), ((), ())), preferred_element_type=jnp.float32
        )
        dactivated = lax.dot_general(
            dproj, w_out, (((1,), (1,)), ((), ())), preferred_element_type=jnp.float32
        )
        unused, pullback = jax.vjp(gelu_tanh, preact)
        dpreact = pullback(dactivated)[0].astype(jnp.bfloat16)
        w_in_part = lax.dot_general(
            normed, dpreact, (((0,), (0,)), ((), ())), preferred_element_type=jnp.float32
        )
        dnormed = lax.dot_general(
            dpreact, w_in, (((1,), (1,)), ((), ())), preferred_element_type=jnp.float32
        )
        gain_part = jnp.sum(dnormed * yhat, axis=0)
        dhat = dnormed * ln_gain
        conv_grad = inverse * (
            dhat
            - jnp.mean(dhat, axis=-1, keepdims=True)
            - yhat * jnp.mean(dhat * yhat, axis=-1, keepdims=True)
        )
        totals = (gain_part, w_in_part, w_out_part, scale_part)
        return (totals, (state, conv_grad.astype(jnp.bfloat16)))

    return block_step


def shards(fields, grad_out, block_count, ocean, kernel, ln_gain, w_in, w_out, layer_scale):
    samples, slot_count, tile_rows, tile_cols, channels = fields.shape
    half_kernel = KSIZE // 2
    half_axis = lax.axis_size("tiles") // 2
    top_bit = lax.axis_size("tiles").bit_length() - 2
    here = lax.axis_index("tiles")
    lower_half = here < half_axis
    at_start = here % half_axis == 0
    at_end = here % half_axis == half_axis - 1
    owned = block_count[0]
    strip_width = slot_count * tile_cols
    used_cols = owned * tile_cols
    slot_ids = jnp.arange(slot_count, dtype=jnp.int32)
    slot_mask = jnp.logical_and(slot_ids < owned, ocean > 0).astype(jnp.float32)
    masked = fields * slot_mask.astype(jnp.bfloat16)[None, :, None, None, None]
    strip = jnp.transpose(masked, (0, 2, 1, 3, 4)).reshape(
        samples, tile_rows, strip_width, channels
    )
    tangent = jnp.transpose(grad_out, (0, 2, 1, 3, 4)).reshape(
        samples, tile_rows, strip_width, channels
    )
    mask_strip = jnp.broadcast_to(
        slot_mask[None, None, :, None, None], (samples, tile_rows, slot_count, tile_cols, 1)
    ).reshape(samples, tile_rows, strip_width, 1)
    left_edge = strip[:, :, :half_kernel]
    right_edge = lax.dynamic_slice_in_dim(strip, used_cols - half_kernel, half_kernel, 2)
    up_send = jnp.where(lower_half, right_edge, left_edge)
    down_send = jnp.where(lower_half, left_edge, right_edge)
    from_lower = passed_along(up_send, "tiles", 1)
    from_upper = passed_along(down_send, "tiles", -1)
    far_edges = from_partner(jnp.stack([down_send, up_send]), "tiles", top_bit)
    from_lower = jnp.where(at_start, far_edges[0], from_lower)
    from_upper = jnp.where(at_end, far_edges[1], from_upper)
    from_west = jnp.where(lower_half, from_lower, from_upper)
    from_east = jnp.where(lower_half, from_upper, from_lower)
    blank_cols = jnp.zeros((samples, tile_rows, half_kernel, channels), jnp.bfloat16)
    extended = jnp.concatenate([from_west, strip, blank_cols], axis=2)
    extended = lax.dynamic_update_slice_in_dim(extended, from_east, used_cols + half_kernel, 2)
    mirrored = from_partner(extended[:, tile_rows - half_kernel :], "tiles", top_bit)
    north_rows = jnp.roll(mirrored[:, ::-1, ::-1], used_cols - strip_width, axis=2)
    south_rows = jnp.zeros(
        (samples, half_kernel, strip_width + 2 * half_kernel, channels), jnp.bfloat16
    )
    padded = jnp.concatenate([south_rows, extended, north_rows], axis=1)
    kernel_f = kernel.astype(jnp.float32)
    convolved = depthwise(padded, kernel_f, tile_rows, strip_width)
    block_step = make_block(ln_gain, w_in, w_out, layer_scale)
    start_totals = (
        jnp.zeros((channels,), jnp.float32),
        jnp.zeros((channels, HID), jnp.float32),
        jnp.zeros((HID, channels), jnp.float32),
        jnp.zeros((channels,), jnp.float32),
    )
    totals, outputs = block_step(
        start_totals,
        (
            convolved.reshape(-1, channels),
            strip.reshape(-1, channels),
            mask_strip.reshape(-1, 1),
            tangent.reshape(-1, channels),
        ),
    )
    gain_part, w_in_part, w_out_part, scale_part = totals
    conv_grad = outputs[1].reshape(samples, tile_rows, strip_width, channels)
    kernel_part = kernel_terms(conv_grad, padded, tile_rows, strip_width)
    dpadded = spread(conv_grad, kernel_f, tile_rows, strip_width)
    north_grad = dpadded[:, tile_rows + half_kernel :]
    returned = from_partner(
        jnp.roll(north_grad[:, ::-1, ::-1], used_cols - strip_width, axis=2).astype(jnp.bfloat16),
        "tiles",
        top_bit,
    ).astype(jnp.float32)
    dextended = dpadded[:, half_kernel : tile_rows + half_kernel]
    dextended = dextended.at[:, tile_rows - half_kernel :].add(returned)
    west_grad = dextended[:, :, :half_kernel]
    east_grad = lax.dynamic_slice_in_dim(dextended, used_cols + half_kernel, half_kernel, 2)
    core_grad = dextended[:, :, half_kernel : strip_width + half_kernel]
    up_grad = jnp.where(lower_half, east_grad, west_grad)
    down_grad = jnp.where(lower_half, west_grad, east_grad)
    grad_lower = passed_along(up_grad.astype(jnp.bfloat16), "tiles", 1).astype(up_grad.dtype)
    grad_upper = passed_along(down_grad.astype(jnp.bfloat16), "tiles", -1).astype(down_grad.dtype)
    far_grads = from_partner(
        jnp.stack([down_grad, up_grad]).astype(jnp.bfloat16), "tiles", top_bit
    ).astype(jnp.float32)
    grad_lower = jnp.where(at_start, far_grads[0], grad_lower)
    grad_upper = jnp.where(at_end, far_grads[1], grad_upper)
    to_head = jnp.where(lower_half, grad_lower, grad_upper)
    to_tail = jnp.where(lower_half, grad_upper, grad_lower)
    core_grad = core_grad.at[:, :, :half_kernel].add(to_head)
    tail_cols = (
        lax.dynamic_slice_in_dim(core_grad, used_cols - half_kernel, half_kernel, 2) + to_tail
    )
    core_grad = lax.dynamic_update_slice_in_dim(core_grad, tail_cols, used_cols - half_kernel, 2)
    grad_strip = (mask_strip * (tangent.astype(jnp.float32) + core_grad)).astype(jnp.bfloat16)
    wide = jnp.stack(
        [
            jnp.transpose(w_in_part.reshape(channels, -1, 128), (1, 0, 2)).reshape(HALF, 128),
            jnp.transpose(w_out_part.reshape(-1, channels // 128, 128), (1, 0, 2)).reshape(HALF, 128),
        ]
    )
    taps = KSIZE * KSIZE
    small = jnp.concatenate(
        [
            kernel_part.reshape(taps, channels),
            gain_part[None],
            scale_part[None],
            jnp.zeros((SMALL - taps - 2, channels), F32),
        ]
    )
    small = jnp.stack([small[:, :128], small[:, 128:]])
    wide, small = reduce_all(wide, small)
    w_in_sum = jnp.transpose(
        wide[0].reshape(-1, channels, 128), (1, 0, 2)
    ).reshape(channels, HID).astype(F32)
    w_out_sum = jnp.transpose(
        wide[1].reshape(channels // 128, HID, 128), (1, 0, 2)
    ).reshape(HID, channels).astype(F32)
    small = jnp.concatenate([small[0], small[1]], axis=1)
    kernel_sum = small[:taps].reshape(KSIZE, KSIZE, channels)
    gain_sum, scale_sum = small[taps], small[taps + 1]
    norm = (
        samples * lax.axis_size("dp") * slot_count * lax.axis_size("tiles") * tile_rows * tile_cols
    ) ** (-0.5)
    state_next = jnp.transpose(
        outputs[0].reshape(samples, tile_rows, slot_count, tile_cols, channels), (0, 2, 1, 3, 4)
    )
    grad_fields = jnp.transpose(
        grad_strip.reshape(samples, tile_rows, slot_count, tile_cols, channels), (0, 2, 1, 3, 4)
    )
    return (
        state_next,
        grad_fields,
        kernel_sum * norm,
        gain_sum * norm,
        w_in_sum * norm,
        w_out_sum * norm,
        scale_sum * norm,
    )


def solution(mesh):
    placed = (
        P("dp", "tiles", None, None, None),
        P("dp", "tiles", None, None, None),
        P("tiles"),
        P("tiles"),
        P(),
        P(),
        P(),
        P(),
        P(),
    )
    return jax.shard_map(
        shards,
        mesh=mesh,
        in_specs=placed,
        out_specs=(
            P("dp", "tiles", None, None, None),
            P("dp", "tiles", None, None, None),
            P(),
            P(),
            P(),
            P(),
            P(),
        ),
        check_vma=False,
    )
```

```python
import functools

import jax
import jax.numpy as jnp
from jax import lax
from jax.experimental import pallas as pl
from jax.experimental.pallas import tpu as pltpu
from jax.sharding import PartitionSpec as P

HID = 1024
KSIZE = 7
NX, NZ, NYH = 4, 8, 4
NY = 2 * NYH
GROUP_X, GROUP_Y, GROUP_Z = 1024, 512, 512
HALF = GROUP_X + GROUP_Y + GROUP_Z
Y0, Z0 = GROUP_X, GROUP_X + GROUP_Y
SMALL = 64
XR, YR, ZR = GROUP_X // NX, GROUP_Y // NY, GROUP_Z // NZ
XA, XB = XR // 2 // NY, XR // 2 // NZ
YX, ZX = YR // NX, ZR // NX
SR = SMALL // NY
F32, BF16 = jnp.float32, jnp.bfloat16


class Place:
    def __init__(self):
        t = lax.axis_index("tiles")
        self.t = t
        self.lo = lax.axis_index("dp")
        self.core = t % 2
        self.yh = (t // 2) % NYH
        self.z = (t // (2 * NYH)) % NZ
        self.x = t // (2 * NYH * NZ)
        self.y = self.yh * 2 + self.lo

    def along(self, axis, step):
        if axis == "core":
            place = 1 - self.core
            return place, (self.t + place - self.core, self.lo)
        if axis == "x":
            place = (self.x + step) % NX
            return place, (self.t + (place - self.x) * (2 * NYH * NZ), self.lo)
        if axis == "z":
            place = (self.z + step) % NZ
            return place, (self.t + (place - self.z) * (2 * NYH), self.lo)
        place = (self.y + step) % NY
        return place, (self.t + (place // 2 - self.yh) * 2, place % 2)


COUNT = {"x": NX, "y": NY, "z": NZ, "core": 2}


def steps(axis):
    n = COUNT[axis]
    near = []
    for d in range(1, n // 2 + 1):
        near += [d, n - d] if d != n - d else [d]
    return near


def send(src, dst, send_sem, recv_sem, device):
    pltpu.make_async_remote_copy(
        src_ref=src,
        dst_ref=dst,
        send_sem=send_sem,
        recv_sem=recv_sem,
        device_id=device,
        device_id_type=pl.DeviceIdType.MESH,
    ).start()


def await_bytes(like, sem):
    pltpu.make_async_copy(like, like, sem).wait()


def rows(start, size):
    return pl.ds(pl.multiple_of(start, size), size)


EPS = 1e-06
C = 256
TILE = 16
SLOTS = 3
CELLS = SLOTS * TILE * TILE
WIDE = 64
LEFT = 8
EDGE = KSIZE // 2
BAND = (TILE + 2 * EDGE) * WIDE
GELU_A = 0.7978845608028654
GELU_B = 0.044715


def halo_places(here):
    count = 2 * NX * NZ * NYH
    half = count // 2

    def swap(i):
        return i + (i // half) * (count + half - 1 - 2 * i)

    rank = swap(here.t)
    west = swap((rank + count - 1) % count)
    east = swap((rank + 1) % count)
    across = (here.t + half) % count
    across_west = (west + half) % count
    across_east = (east + half) % count
    return west, east, across, across_west, across_east


class Halo:
    def __init__(self, here, band, edges, top, got, got_top, ss, rs):
        self.here, self.band, self.edges, self.top = here, band, edges, top
        self.got, self.got_top, self.ss, self.rs = got, got_top, ss, rs
        self.west, self.east, self.across, self.across_west, self.across_east = halo_places(here)

    def gather_edges(self, owned):
        for h in range(2):
            lanes = pl.ds(h * 128, 128)
            for j in range(EDGE):
                start = EDGE * WIDE + LEFT + j
                left = self.band[h, pl.ds(start, TILE, WIDE), :]
                self.edges[0, j, :, lanes] = left.astype(BF16)
                ends = [
                    self.band[h, pl.ds(start + TILE * n - EDGE, TILE, WIDE), :]
                    for n in range(1, SLOTS + 1)
                ]
                right = jnp.where(owned == 1, ends[0], jnp.where(owned == 2, ends[1], ends[2]))
                self.edges[1, j, :, lanes] = right.astype(BF16)
            for k in range(EDGE):
                row = self.band[
                    h, pl.ds((TILE + k) * WIDE + LEFT, SLOTS * TILE), :
                ]
                self.top[k, :, lanes] = row.astype(BF16)

    def start(self):
        lo, ss, rs = self.here.lo, self.ss, self.rs
        left, right = self.edges.at[0], self.edges.at[1]
        send(left, self.got.at[1], ss.at[0], rs.at[1], (self.west, lo))
        send(right, self.got.at[0], ss.at[1], rs.at[0], (self.east, lo))
        send(self.top, self.got_top, ss.at[2], rs.at[2], (self.across, lo))
        for block, landing, i, device in (
            (left, self.got.at[2], 3, self.across_west),
            (right, self.got.at[3], 4, self.across_east),
        ):

            @pl.when(device != self.here.t)
            def _():
                send(block, landing, ss.at[i], rs.at[i], (device, lo))

            @pl.when(device == self.here.t)
            def _():
                pltpu.make_async_copy(block, landing, rs.at[i]).start()

    def finish(self, owned):
        edge = self.edges.at[0]
        await_bytes(edge, self.rs.at[0])
        await_bytes(edge, self.rs.at[1])
        for h in range(2):
            lanes = pl.ds(h * 128, 128)
            for j in range(EDGE):
                start = EDGE * WIDE + LEFT + j
                self.band[h, pl.ds(start - EDGE, TILE, WIDE), :] = self.got[0, j, :, lanes].astype(F32)
                east = self.got[1, j, :, lanes].astype(F32)
                for n in range(1, SLOTS):
                    spot = pl.ds(start + TILE * n, TILE, WIDE)
                    self.band[h, spot, :] = jnp.where(owned == n, east, self.band[h, spot, :])
                self.band[h, pl.ds(start + TILE * SLOTS, TILE, WIDE), :] = east
        await_bytes(self.top, self.rs.at[2])
        await_bytes(edge, self.rs.at[3])
        await_bytes(edge, self.rs.at[4])
        used = owned * TILE
        span = SLOTS * TILE
        spot = lax.broadcasted_iota(jnp.int32, (WIDE, 3 * span), 0) - LEFT
        item = lax.broadcasted_iota(jnp.int32, (WIDE, 3 * span), 1)
        inner = jnp.logical_and(jnp.logical_and(spot >= 0, spot < used), item == used - 1 - spot)
        for k in range(1, EDGE + 1):
            row = TILE - k
            west = jnp.logical_and(spot < 0, item == span + (-1 - spot) * TILE + row)
            west = jnp.logical_and(west, spot >= -EDGE)
            past = spot - used
            east = jnp.logical_and(past >= 0, item == 2 * span + (EDGE - 1 - past) * TILE + row)
            east = jnp.logical_and(east, past < EDGE)
            chosen = jnp.logical_or(inner, jnp.logical_or(west, east))
            pick = jnp.where(chosen, 1.0, 0.0).astype(BF16)
            source = jnp.concatenate(
                [
                    self.got_top[EDGE - k],
                    self.got[2].reshape(EDGE * TILE, C),
                    self.got[3].reshape(EDGE * TILE, C),
                ],
                axis=0,
            )
            fold = jnp.dot(pick, source, preferred_element_type=F32)
            place = pl.ds((EDGE + TILE - 1 + k) * WIDE, WIDE)
            self.band[0, place, :] = fold[:, :128]
            self.band[1, place, :] = fold[:, 128:]

    def drain(self):
        edge = self.edges.at[0]
        await_bytes(edge, self.ss.at[0])
        await_bytes(edge, self.ss.at[1])
        await_bytes(self.top, self.ss.at[2])
        for i, device in ((3, self.across_west), (4, self.across_east)):

            @pl.when(device != self.here.t)
            def _():
                await_bytes(edge, self.ss.at[i])


BLOCKS = SLOTS * TILE // 8


def block_start(block):
    return (block // 2) * (TILE * TILE) + (block % 2) * 8


def stencil(band, taps, h, block, backward):
    base = LEFT - EDGE + block * 8
    total = [None] * TILE
    for b in range(KSIZE):
        straight = [taps[h, pl.ds(a * KSIZE + b, 1), :] for a in range(KSIZE)]
        turned = straight
        if backward:
            turned = [
                taps[h, pl.ds((KSIZE - 1 - a) * KSIZE + KSIZE - 1 - b, 1), :] for a in range(KSIZE)
            ]
        for row in range(EDGE, TILE + 2 * EDGE):
            window = band[h, pl.ds(row * WIDE + base + b, 8), :]
            used = straight if row >= TILE + EDGE else turned
            for a in range(KSIZE):
                r = row - a
                if 0 <= r < TILE:
                    term = used[a] * window
                    total[r] = term if total[r] is None else total[r] + term
    return total


def total(first, landing):
    for k in range(landing.shape[0]):
        first = first + landing[k].astype(F32)
    return first


def line_total(landing):
    run = landing[0].astype(F32)
    for k in range(1, landing.shape[0]):
        run = run + landing[k].astype(F32)
    return run


class Reducer:
    def __init__(self, here, refs, ss, rs):
        self.here, self.ss, self.rs = here, ss, rs
        (
            self.wide, self.small, self.out, self.small_out, self.core_out, self.core_in, self.held, self.x_in,
            self.y_in, self.z_in, self.p_out, self.xa_in, self.xb_in, self.w_out, self.w_in, self.zz, self.yy,
            self.s_core, self.s_y, self.s_z, self.s_x, self.s_held,
        ) = refs
        self.partner = here.along("core", 1)[1]

    def gather(self, ref, axis, sem):
        for d in steps(axis):
            send(ref, ref, self.ss.at[sem], self.rs.at[sem], self.here.along(axis, d)[1])

    def scatter(self, ref, offset, size, landing, axis, sem):
        for d in steps(axis):
            place, device = self.here.along(axis, d)
            send(
                ref.at[rows(offset + place * size, size)], landing.at[d - 1], self.ss.at[sem], self.rs.at[sem], device
            )

    def core(self, k):
        span = rows(k * 512, 512)
        self.core_out[span] = self.wide[1 - self.here.core, span].astype(BF16)
        send(self.core_out.at[span], self.core_in.at[span], self.ss.at[k], self.rs.at[k], self.partner)

    def first_axis(self, region):
        axis, start, extent, size, landing, ks, sem = (
            ("x", 0, GROUP_X, XR, self.x_in, (0, 1), 4),
            ("y", Y0, GROUP_Y, YR, self.y_in, (2,), 5),
            ("z", Z0, GROUP_Z, ZR, self.z_in, (3,), 6),
        )[region]
        for k in ks:
            await_bytes(self.core_in.at[pl.ds(0, 512)], self.rs.at[k])
        span = pl.ds(start, extent)
        self.held[span] = (self.wide[self.here.core, span] + self.core_in[span].astype(F32)).astype(BF16)
        self.scatter(self.held, start, size, landing, axis, sem)

    def own(self, start, size):
        span = rows(start, size)
        return self.wide[self.here.core, span] + self.core_in[span].astype(F32)

    def second_axis(self):
        x, y, z = self.here.x, self.here.y, self.here.z
        await_bytes(self.x_in, self.rs.at[4])
        self.p_out[...] = total(self.own(x * XR, XR), self.x_in).astype(BF16)
        self.scatter(self.p_out, 0, XA, self.xa_in, "y", 8)
        self.scatter(self.p_out, XR // 2, XB, self.xb_in, "z", 9)
        await_bytes(self.y_in, self.rs.at[5])
        y_own = total(self.own(Y0 + y * YR, YR), self.y_in)
        for k in range(NX):
            self.w_out[k, :YX] = y_own[k * YX : (k + 1) * YX].astype(BF16)
        await_bytes(self.z_in, self.rs.at[6])
        z_own = total(self.own(Z0 + z * ZR, ZR), self.z_in)
        for k in range(NX):
            self.w_out[k, YX:] = z_own[k * ZX : (k + 1) * ZX].astype(BF16)
        for d in steps("x"):
            place, device = self.here.along("x", d)
            send(self.w_out.at[place], self.w_in.at[d - 1], self.ss.at[10], self.rs.at[10], device)

    def third_axis(self):
        x, y, z = self.here.x, self.here.y, self.here.z
        await_bytes(self.w_in, self.rs.at[10])
        mine = total(self.w_out[x].astype(F32), self.w_in)
        await_bytes(self.xa_in, self.rs.at[8])
        self.zz[z, :XA] = total(self.p_out[rows(y * XA, XA)].astype(F32), self.xa_in).astype(BF16)
        self.zz[z, XA:] = mine[:YX].astype(BF16)
        self.gather(self.zz.at[z], "z", 12)
        await_bytes(self.xb_in, self.rs.at[9])
        self.yy[y, :XB] = total(
            self.p_out[rows(XR // 2 + z * XB, XB)].astype(F32), self.xb_in
        ).astype(BF16)
        self.yy[y, XB:] = mine[YX:].astype(BF16)
        self.gather(self.yy.at[y], "y", 13)

    def second_back(self):
        c, x, y, z = self.here.core, self.here.x, self.here.y, self.here.z
        out = self.out
        await_bytes(self.zz.at[pl.ds(0, NZ - 1)], self.rs.at[12])
        zsum = line_total(self.zz).astype(BF16)
        out[c, rows(x * XR + y * XA, XA)] = zsum[:XA]
        out[c, rows(Y0 + y * YR + x * YX, YX)] = zsum[XA:]
        self.gather(out.at[c, rows(x * XR + y * XA, XA)], "y", 16)
        self.gather(out.at[c, rows(Y0 + y * YR + x * YX, YX)], "x", 17)
        await_bytes(self.yy.at[pl.ds(0, NY - 1)], self.rs.at[13])
        ysum = line_total(self.yy).astype(BF16)
        out[c, rows(x * XR + XR // 2 + z * XB, XB)] = ysum[:XB]
        out[c, rows(Z0 + z * ZR + x * ZX, ZX)] = ysum[XB:]
        self.gather(out.at[c, rows(x * XR + XR // 2 + z * XB, XB)], "z", 18)
        self.gather(out.at[c, rows(Z0 + z * ZR + x * ZX, ZX)], "x", 19)

    def bytes_of(self, count):
        return self.out.at[0, pl.ds(0, count)]

    def first_back(self):
        c, x, y, z = self.here.core, self.here.x, self.here.y, self.here.z
        await_bytes(self.bytes_of((NX - 1) * YX), self.rs.at[17])
        self.gather(self.out.at[c, rows(Y0 + y * YR, YR)], "y", 20)
        await_bytes(self.bytes_of((NX - 1) * ZX), self.rs.at[19])
        self.gather(self.out.at[c, rows(Z0 + z * ZR, ZR)], "z", 21)
        await_bytes(self.bytes_of((NY - 1) * XA), self.rs.at[16])
        await_bytes(self.bytes_of((NZ - 1) * XB), self.rs.at[18])
        self.gather(self.out.at[c, rows(x * XR, XR)], "x", 22)

    def core_back(self):
        c = self.here.core
        for sem, got, start, size, i in (
            (20, (NY - 1) * YR, Y0, GROUP_Y, 25),
            (21, (NZ - 1) * ZR, Z0, GROUP_Z, 26),
            (22, (NX - 1) * XR, 0, GROUP_X, 24),
        ):
            await_bytes(self.bytes_of(got), self.rs.at[sem])
            ref = self.out.at[c, pl.ds(start, size)]
            send(ref, ref, self.ss.at[i], self.rs.at[i], self.partner)

    def core_done(self):
        for i, size in ((25, GROUP_Y), (26, GROUP_Z), (24, GROUP_X)):
            await_bytes(self.bytes_of(size), self.rs.at[i])

    def small_core(self):
        send(self.small.at[1 - self.here.core], self.s_core, self.ss.at[27], self.rs.at[27], self.partner)

    def small_y(self):
        await_bytes(self.s_core, self.rs.at[27])
        self.s_held[...] = self.small[self.here.core] + self.s_core[...]
        self.scatter(self.s_held, 0, SR, self.s_y, "y", 7)

    def small_z(self):
        z = self.here.z
        await_bytes(self.s_y, self.rs.at[7])
        self.s_z[z] = total(self.s_held[rows(self.here.y * SR, SR)], self.s_y)
        self.gather(self.s_z.at[z], "z", 11)

    def small_x(self):
        x = self.here.x
        await_bytes(self.s_z.at[pl.ds(0, NZ - 1)], self.rs.at[11])
        self.s_x[x] = line_total(self.s_z)
        self.gather(self.s_x.at[x], "x", 14)

    def small_back(self):
        place = rows(self.here.y * SR, SR)
        await_bytes(self.s_x.at[pl.ds(0, NX - 1)], self.rs.at[14])
        self.small_out[self.here.core, place] = line_total(self.s_x)
        self.gather(self.small_out.at[self.here.core, place], "y", 15)

    def small_core_back(self):
        await_bytes(self.small_out.at[0, pl.ds(0, (NY - 1) * SR)], self.rs.at[15])
        ref = self.small_out.at[self.here.core]
        send(ref, ref, self.ss.at[23], self.rs.at[23], self.partner)

    def small_done(self):
        await_bytes(self.small_out.at[0], self.rs.at[23])

    def drain(self):
        ss = self.ss
        for k in range(4):
            await_bytes(self.core_out.at[pl.ds(0, 512)], ss.at[k])
        for ref, i in (
            (self.x_in, 4), (self.y_in, 5), (self.z_in, 6), (self.s_y, 7), (self.xa_in, 8), (self.xb_in, 9),
            (self.w_in, 10), (self.s_core, 27), (self.small_out.at[0], 23),
            (self.s_z.at[pl.ds(0, NZ - 1)], 11), (self.zz.at[pl.ds(0, NZ - 1)], 12),
            (self.yy.at[pl.ds(0, NY - 1)], 13), (self.s_x.at[pl.ds(0, NX - 1)], 14),
            (self.small_out.at[0, pl.ds(0, (NY - 1) * SR)], 15),
            (self.bytes_of((NY - 1) * XA), 16), (self.bytes_of((NX - 1) * YX), 17),
            (self.bytes_of((NZ - 1) * XB), 18), (self.bytes_of((NX - 1) * ZX), 19),
            (self.bytes_of((NY - 1) * YR), 20), (self.bytes_of((NZ - 1) * ZR), 21),
            (self.bytes_of((NX - 1) * XR), 22), (self.bytes_of(GROUP_X), 24), (self.bytes_of(GROUP_Y), 25),
            (self.bytes_of(GROUP_Z), 26),
        ):
            await_bytes(ref, ss.at[i])


def greet(here):
    barrier = pltpu.get_barrier_semaphore()
    mesh_id = pl.DeviceIdType.MESH
    greeted = 0
    for axis in ("core", "x", "y", "z"):
        for d in steps(axis):
            pl.semaphore_signal(barrier, inc=1, device_id=here.along(axis, d)[1], device_id_type=mesh_id)
            greeted += 1
    west, east, across, across_west, across_east = halo_places(here)
    for device in (west, east, across):
        pl.semaphore_signal(barrier, inc=1, device_id=(device, here.lo), device_id_type=mesh_id)
        greeted += 1
    for device in (across_west, across_east):

        @pl.when(device != here.t)
        def _():
            pl.semaphore_signal(barrier, inc=1, device_id=(device, here.lo), device_id_type=mesh_id)

    return barrier, greeted, (across_west, across_east)


def block_kernel(
    owned_ref, ocean_ref, fields, grad_out, kernel, ln_gain, w_in_hbm, w_out_hbm, layer_scale,
    state, grad_fields, wide_out, small_out,
    band, gband, taps, conv, inverse, normed, dproj, activated, dpreact, projected, dnormed, rowsum, weight_in,
    weight_out, edges, top, got, got_top, edges2, top2, got2, got_top2, small,
    wide, core_out, core_in, held, x_in, y_in, z_in, p_out, xa_in, xb_in, r_out, r_in, zz, yy,
    s_core, s_y, s_z, s_x, s_held, ss, rs, hs, hr, hs2, hr2, ls
):
    here = Place()
    barrier, greeted, maybe = greet(here)
    load_in = pltpu.make_async_copy(w_in_hbm, weight_in, ls.at[0])
    load_out = pltpu.make_async_copy(w_out_hbm, weight_out, ls.at[1])
    load_in.start()
    load_out.start()
    reducer = Reducer(
        here,
        (
            wide, small, wide_out, small_out, core_out, core_in, held, x_in, y_in, z_in, p_out, xa_in, xb_in,
            r_out, r_in, zz, yy, s_core, s_y, s_z, s_x, s_held,
        ),
        ss,
        rs,
    )
    owned = owned_ref[0]

    def slot_mask(slot):
        live = jnp.logical_and(slot < owned, ocean_ref[slot] > 0)
        return jnp.where(live, 1.0, 0.0).astype(F32)

    def clear(i, carry):
        spot = rows(i * 64, 64)
        for h in range(2):
            band[h, spot, :] = jnp.zeros((64, 128), F32)
            gband[h, spot, :] = jnp.zeros((64, 128), F32)
        return carry

    lax.fori_loop(0, BAND // 64, clear, 0)
    small[...] = jnp.zeros_like(small)
    rowsum[...] = jnp.zeros_like(rowsum)
    for a in range(KSIZE):
        line = kernel[a].astype(F32)
        for h in range(2):
            taps[h, a * KSIZE : (a + 1) * KSIZE, :] = line[:, h * 128 : (h + 1) * 128]

    def fill(i, carry):
        slot, r = i // TILE, i % TILE
        line = fields[rows(i * TILE, TILE), :].astype(F32) * slot_mask(slot)
        place = pl.ds(pl.multiple_of((EDGE + r) * WIDE + LEFT + slot * TILE, 8), TILE)
        band[0, place, :] = line[:, :128]
        band[1, place, :] = line[:, 128:]
        return carry

    lax.fori_loop(0, SLOTS * TILE, fill, 0)
    halo = Halo(here, band, edges, top, got, got_top, hs, hr)
    halo.gather_edges(owned)
    at_seam = jnp.logical_or(maybe[0] == here.t, maybe[1] == here.t)

    @pl.when(at_seam)
    def _():
        pl.semaphore_wait(barrier, greeted + 1)

    @pl.when(jnp.logical_not(at_seam))
    def _():
        pl.semaphore_wait(barrier, greeted + 2)

    halo.start()
    halo.finish(owned)

    def convolve(i, carry):
        h, block = i // BLOCKS, i % BLOCKS
        result = stencil(band, taps, h, block, False)
        for r in range(TILE):
            conv[h, pl.ds(pl.multiple_of(block_start(block) + r * TILE, 8), 8), :] = result[r]
        return carry

    lax.fori_loop(0, 2 * BLOCKS, convolve, 0)

    gain = [ln_gain[:, :128], ln_gain[:, 128:]]
    scale = [layer_scale[:, :128], layer_scale[:, 128:]]
    STEP = 64

    def norm(i, carry):
        span = rows(i * STEP, STEP)
        mask = slot_mask(i // (TILE * TILE // STEP))
        parts = [conv[h, span, :] for h in range(2)]
        mean = jnp.sum(parts[0] + parts[1], axis=1, keepdims=True) * (1.0 / C)
        centred = [part - mean for part in parts]
        variance = jnp.sum(
            centred[0] * centred[0] + centred[1] * centred[1], axis=1, keepdims=True
        ) * (1.0 / C)
        scaled = lax.rsqrt(variance + EPS)
        inverse[span, :] = jnp.broadcast_to(scaled, (STEP, 128))
        for h in range(2):
            lanes = pl.ds(h * 128, 128)
            yhat = centred[h] * scaled
            conv[h, span, :] = yhat
            normed[span, lanes] = (yhat * gain[h]).astype(BF16)
            cotangent = grad_out[span, lanes].astype(F32)
            dproj[span, lanes] = (mask * scale[h] * cotangent).astype(BF16)
        return carry

    lax.fori_loop(0, CELLS // STEP, norm, 0)
    load_in.wait()
    load_out.wait()
    across_rows = (((0,), (0,)), ((), ()))
    across_cols = (((1,), (1,)), ((), ()))

    def quarter(k, carry):
        part_in = weight_in[:, rows(k * 256, 256)]
        part_out = weight_out[rows(k * 256, 256), :]
        for m in range(SLOTS):
            span = pl.ds(m * 256, 256)
            cells, slopes = normed[span, :], dproj[span, :]
            v = jnp.dot(cells, part_in, preferred_element_type=F32)
            dact = lax.dot_general(slopes, part_out, across_cols, preferred_element_type=F32)
            square = v * v
            t = jnp.tanh(v * (GELU_A + (GELU_A * GELU_B) * square))
            half = 0.5 + 0.5 * t
            act = (v * half).astype(BF16)
            slope = half + (v * half) * (1.0 - t) * (GELU_A + (3.0 * GELU_A * GELU_B) * square)
            dpre = (dact * slope).astype(BF16)
            activated[span, :] = act
            dpreact[span, :] = dpre
            forward = jnp.dot(act, part_out, preferred_element_type=F32)
            back = lax.dot_general(dpre, part_in, across_cols, preferred_element_type=F32)
            first = k == 0
            projected[span, :] = jnp.where(first, forward, projected[span, :] + forward)
            dnormed[span, :] = jnp.where(first, back, dnormed[span, :] + back)
        grad_o = lax.dot_general(activated[...], dproj[...], across_rows, preferred_element_type=F32)
        grad_i = lax.dot_general(normed[...], dpreact[...], across_rows, preferred_element_type=F32)
        for h in range(2):
            spot = rows(k * 512 + h * 256, 256)
            wide[0, spot, :] = grad_i[:, h * 128 : (h + 1) * 128]
            wide[1, spot, :] = grad_o[:, h * 128 : (h + 1) * 128]
        reducer.core(k)
        return carry

    projected[...] = jnp.zeros_like(projected)
    dnormed[...] = jnp.zeros_like(dnormed)
    lax.fori_loop(0, HID // 256, quarter, 0)
    for region in range(3):
        reducer.first_axis(region)

    def norm_back(i, carry):
        span = rows(i * STEP, STEP)
        slot, r = i // (TILE * TILE // STEP), (i % (TILE * TILE // STEP)) * (STEP // TILE)
        lanes = [pl.ds(h * 128, 128) for h in range(2)]
        back = [dnormed[span, lanes[h]] for h in range(2)]
        yhat = [conv[h, span, :] for h in range(2)]
        for h in range(2):
            rowsum[h] += jnp.sum((back[h] * yhat[h]).reshape(STEP // 8, 8, 128), axis=0)
        dhat = [back[h] * gain[h] for h in range(2)]
        mean = jnp.sum(dhat[0] + dhat[1], axis=1, keepdims=True) * (1.0 / C)
        tilt = jnp.sum(dhat[0] * yhat[0] + dhat[1] * yhat[1], axis=1, keepdims=True) * (1.0 / C)
        for h in range(2):
            grad = inverse[span, :] * (dhat[h] - mean - yhat[h] * tilt)
            grad = grad.astype(BF16).astype(F32)
            for q in range(STEP // TILE):
                place = pl.ds(
                    pl.multiple_of((EDGE + r + q) * WIDE + LEFT + slot * TILE, 8), TILE
                )
                gband[h, place, :] = grad[q * TILE : (q + 1) * TILE]
        return carry

    lax.fori_loop(0, CELLS // STEP, norm_back, 0)
    halo_back = Halo(here, gband, edges2, top2, got2, got_top2, hs2, hr2)
    halo_back.gather_edges(owned)
    halo_back.start()

    def finish_state(i, carry):
        span = rows(i * STEP, STEP)
        mask = slot_mask(i // (TILE * TILE // STEP))
        for h in range(2):
            lanes = pl.ds(h * 128, 128)
            out = projected[span, lanes]
            rowsum[2 + h] += jnp.sum(
                (mask * grad_out[span, lanes].astype(F32) * out).reshape(STEP // 8, 8, 128), axis=0
            )
            kept = fields[span, lanes].astype(F32)
            state[span, lanes] = (mask * (kept + scale[h] * out)).astype(BF16)
        return carry

    lax.fori_loop(0, CELLS // STEP, finish_state, 0)
    reducer.second_axis()

    def kernel_grad(i, carry):
        h, b = i // KSIZE, i % KSIZE

        def one_block(block, sums):
            sums = list(sums)
            base = LEFT + block * 8
            cots = [gband[h, pl.ds(pl.multiple_of((EDGE + r) * WIDE + base, 8), 8), :] for r in range(TILE)]
            for row in range(EDGE, TILE + 2 * EDGE):
                window = band[h, pl.ds(row * WIDE + base - EDGE + b, 8), :]
                for a in range(KSIZE):
                    if 0 <= row - a < TILE:
                        sums[a] = sums[a] + cots[row - a] * window
            return tuple(sums)

        zero = tuple(jnp.zeros((8, 128), F32) for a in range(KSIZE))
        sums = lax.fori_loop(0, BLOCKS, one_block, zero)
        for a in range(KSIZE):
            small[h, pl.ds(a * KSIZE + b, 1), :] = jnp.sum(sums[a], axis=0, keepdims=True)
        return carry

    lax.fori_loop(0, 2 * KSIZE, kernel_grad, 0)
    for h in range(2):
        small[h, KSIZE * KSIZE : KSIZE * KSIZE + 1, :] = jnp.sum(rowsum[h], axis=0, keepdims=True)
        small[h, KSIZE * KSIZE + 1 : KSIZE * KSIZE + 2, :] = jnp.sum(rowsum[2 + h], axis=0, keepdims=True)
    reducer.small_core()
    reducer.third_axis()
    halo_back.finish(owned)
    reducer.small_y()

    def convolve_back(i, carry):
        h, block = i % 2, i // 2
        result = stencil(gband, taps, h, block, True)
        for r in range(TILE):
            conv[h, pl.ds(pl.multiple_of(block_start(block) + r * TILE, 8), 8), :] = result[r]
        return carry

    def finish_grad(i, carry):
        span = rows(i * STEP, STEP)
        mask = slot_mask(i // (TILE * TILE // STEP))
        for h in range(2):
            lanes = pl.ds(h * 128, 128)
            grad = mask * (grad_out[span, lanes].astype(F32) + conv[h, span, :])
            grad_fields[span, lanes] = grad.astype(BF16)
        return carry

    lax.fori_loop(0, BLOCKS, convolve_back, 0)
    reducer.second_back()
    reducer.small_z()
    lax.fori_loop(BLOCKS, 2 * BLOCKS, convolve_back, 0)
    reducer.first_back()
    reducer.small_x()
    lax.fori_loop(0, CELLS // STEP, finish_grad, 0)
    reducer.small_back()
    reducer.core_back()
    reducer.small_core_back()
    reducer.core_done()
    reducer.small_done()
    reducer.drain()
    halo.drain()
    halo_back.drain()


def block_call(block_count, ocean, fields, grad_out, kernel, ln_gain, w_in, w_out, layer_scale):
    vmem = pl.BlockSpec(memory_space=pltpu.VMEM)
    smem = pl.BlockSpec(memory_space=pltpu.SMEM)
    hbm = pl.BlockSpec(memory_space=pl.ANY)
    edges = pltpu.VMEM((2, EDGE, TILE, C), BF16)
    top = pltpu.VMEM((EDGE, SLOTS * TILE, C), BF16)
    got = pltpu.VMEM((4, EDGE, TILE, C), BF16)
    scratch = [
        pltpu.VMEM((2, BAND, 128), F32),
        pltpu.VMEM((2, BAND, 128), F32),
        pltpu.VMEM((2, 56, 128), F32),
        pltpu.VMEM((2, CELLS, 128), F32),
        pltpu.VMEM((CELLS, 128), F32),
        pltpu.VMEM((CELLS, C), BF16),
        pltpu.VMEM((CELLS, C), BF16),
        pltpu.VMEM((CELLS, 256), BF16),
        pltpu.VMEM((CELLS, 256), BF16),
        pltpu.VMEM((CELLS, C), F32),
        pltpu.VMEM((CELLS, C), F32),
        pltpu.VMEM((4, 8, 128), F32),
        pltpu.VMEM((C, HID), BF16),
        pltpu.VMEM((HID, C), BF16),
        edges, top, got, top, edges, top, got, top,
        pltpu.VMEM((2, SMALL, 128), F32),
        pltpu.VMEM((2, HALF, 128), F32),
        pltpu.VMEM((HALF, 128), BF16),
        pltpu.VMEM((HALF, 128), BF16),
        pltpu.VMEM((HALF, 128), BF16),
        pltpu.VMEM((NX - 1, XR, 128), BF16),
        pltpu.VMEM((NY - 1, YR, 128), BF16),
        pltpu.VMEM((NZ - 1, ZR, 128), BF16),
        pltpu.VMEM((XR, 128), BF16),
        pltpu.VMEM((NY - 1, XA, 128), BF16),
        pltpu.VMEM((NZ - 1, XB, 128), BF16),
        pltpu.VMEM((NX, YX + ZX, 128), BF16),
        pltpu.VMEM((NX - 1, YX + ZX, 128), BF16),
        pltpu.VMEM((NZ, XA + YX, 128), BF16),
        pltpu.VMEM((NY, XB + ZX, 128), BF16),
        pltpu.VMEM((SMALL, 128), F32),
        pltpu.VMEM((NY - 1, SR, 128), F32),
        pltpu.VMEM((NZ, SR, 128), F32),
        pltpu.VMEM((NX, SR, 128), F32),
        pltpu.VMEM((SMALL, 128), F32),
        pltpu.SemaphoreType.DMA((28,)),
        pltpu.SemaphoreType.DMA((28,)),
        pltpu.SemaphoreType.DMA((5,)),
        pltpu.SemaphoreType.DMA((5,)),
        pltpu.SemaphoreType.DMA((5,)),
        pltpu.SemaphoreType.DMA((5,)),
        pltpu.SemaphoreType.DMA((2,)),
    ]
    return pl.pallas_call(
        block_kernel,
        out_shape=(
            jax.ShapeDtypeStruct((CELLS, C), BF16),
            jax.ShapeDtypeStruct((CELLS, C), BF16),
            jax.ShapeDtypeStruct((2, HALF, 128), BF16),
            jax.ShapeDtypeStruct((2, SMALL, 128), F32),
        ),
        in_specs=[smem, smem, vmem, vmem, vmem, vmem, hbm, hbm, vmem],
        out_specs=(vmem, vmem, vmem, vmem),
        scratch_shapes=scratch,
        compiler_params=pltpu.CompilerParams(
            collective_id=1, has_side_effects=True, vmem_limit_bytes=48 * 1024 * 1024
        ),
    )(block_count, ocean, fields, grad_out, kernel, ln_gain, w_in, w_out, layer_scale)


def shards(fields, grad_out, block_count, ocean, kernel, ln_gain, w_in, w_out, layer_scale):
    shape = fields.shape
    samples, slot_count, tile_rows, tile_cols, channels = shape
    state, grad_fields, wide, small = block_call(
        block_count,
        ocean,
        fields.reshape(CELLS, channels),
        grad_out.reshape(CELLS, channels),
        kernel,
        ln_gain.reshape(1, channels),
        w_in,
        w_out,
        layer_scale.reshape(1, channels),
    )
    norm = (
        samples * lax.axis_size("dp") * slot_count * lax.axis_size("tiles") * tile_rows * tile_cols
    ) ** (-0.5)
    taps = KSIZE * KSIZE
    w_in_sum = jnp.transpose(wide[0].reshape(-1, channels, 128), (1, 0, 2)).reshape(channels, HID)
    w_out_sum = jnp.transpose(wide[1].reshape(4, 2, 256, 128), (0, 2, 1, 3)).reshape(HID, channels)
    small = jnp.concatenate([small[0], small[1]], axis=1) * norm
    return (
        state.reshape(shape),
        grad_fields.reshape(shape),
        small[:taps].reshape(KSIZE, KSIZE, channels),
        small[taps],
        w_in_sum.astype(F32) * norm,
        w_out_sum.astype(F32) * norm,
        small[taps + 1],
    )


def solution(mesh):
    placed = (
        P("dp", "tiles", None, None, None),
        P("dp", "tiles", None, None, None),
        P("tiles"),
        P("tiles"),
        P(),
        P(),
        P(),
        P(),
        P(),
    )
    return jax.shard_map(
        shards,
        mesh=mesh,
        in_specs=placed,
        out_specs=(
            P("dp", "tiles", None, None, None),
            P("dp", "tiles", None, None, None),
            P(),
            P(),
            P(),
            P(),
            P(),
        ),
        check_vma=False,
    )
```

```python
import functools

import jax
import jax.numpy as jnp
from jax import lax
from jax.experimental import pallas as pl
from jax.experimental.pallas import tpu as pltpu
from jax.sharding import PartitionSpec as P

HID = 1024
KSIZE = 7
NX, NZ, NYH = 4, 8, 4
NY = 2 * NYH
HALF = 2048
REGION = HALF // 2
SMALL = 64
PR, QR = REGION // (NX * NY), REGION // (NX * NZ)
SR = SMALL // NY
F32, BF16 = jnp.float32, jnp.bfloat16


class Place:
    def __init__(self):
        t = lax.axis_index("tiles")
        self.t = t
        self.lo = lax.axis_index("dp")
        self.core = t % 2
        self.yh = (t // 2) % NYH
        self.z = (t // (2 * NYH)) % NZ
        self.x = t // (2 * NYH * NZ)
        self.y = self.yh * 2 + self.lo

    def device(self, core, x, y, z):
        return (((x * NZ + z) * NYH + y // 2) * 2 + core, y % 2)

    def along(self, axis, step):
        if axis == "core":
            place = 1 - self.core
            return place, (self.t + place - self.core, self.lo)
        if axis == "x":
            place = (self.x + step) % NX
            return place, (self.t + (place - self.x) * (2 * NYH * NZ), self.lo)
        if axis == "z":
            place = (self.z + step) % NZ
            return place, (self.t + (place - self.z) * (2 * NYH), self.lo)
        place = (self.y + step) % NY
        return place, (self.t + (place // 2 - self.yh) * 2, place % 2)


COUNT = {"x": NX, "y": NY, "z": NZ, "core": 2}


def steps(axis):
    n = COUNT[axis]
    near = []
    for d in range(1, n // 2 + 1):
        near += [d, n - d] if d != n - d else [d]
    return near


def offsets(*sizes):
    found = [()]
    for n in sizes:
        found = [step + (d,) for step in found for d in range(n)]
    far = lambda step: -sum(min(d, n - d) for d, n in zip(step, sizes))
    return sorted((step for step in found if any(step)), key=far)


def send(src, dst, send_sem, recv_sem, device):
    pltpu.make_async_remote_copy(
        src_ref=src,
        dst_ref=dst,
        send_sem=send_sem,
        recv_sem=recv_sem,
        device_id=device,
        device_id_type=pl.DeviceIdType.MESH,
    ).start()


def await_bytes(like, sem):
    pltpu.make_async_copy(like, like, sem).wait()


def rows(start, size):
    return pl.ds(pl.multiple_of(start, size), size)


EPS = 1e-06
C = 256
TILE = 16
SLOTS = 3
CELLS = SLOTS * TILE * TILE
WIDE = 64
LEFT = 8
EDGE = KSIZE // 2
BAND = (TILE + 2 * EDGE) * WIDE
GELU_A = 0.7978845608028654
GELU_B = 0.044715


def halo_places(here):
    count = 2 * NX * NZ * NYH
    half = count // 2

    def swap(i):
        return i + (i // half) * (count + half - 1 - 2 * i)

    rank = swap(here.t)
    west = swap((rank + count - 1) % count)
    east = swap((rank + 1) % count)
    across = (here.t + half) % count
    across_west = (west + half) % count
    across_east = (east + half) % count
    return west, east, across, across_west, across_east


class Halo:
    def __init__(self, here, band, edges, top, got, got_top, ss, rs):
        self.here, self.band, self.edges, self.top = here, band, edges, top
        self.got, self.got_top, self.ss, self.rs = got, got_top, ss, rs
        self.west, self.east, self.across, self.across_west, self.across_east = halo_places(here)

    def gather_edges(self, owned):
        for h in range(2):
            lanes = pl.ds(h * 128, 128)
            for j in range(EDGE):
                start = EDGE * WIDE + LEFT + j
                left = self.band[h, pl.ds(start, TILE, WIDE), :]
                self.edges[0, j, :, lanes] = left.astype(BF16)
                ends = [
                    self.band[h, pl.ds(start + TILE * n - EDGE, TILE, WIDE), :]
                    for n in range(1, SLOTS + 1)
                ]
                right = jnp.where(owned == 1, ends[0], jnp.where(owned == 2, ends[1], ends[2]))
                self.edges[1, j, :, lanes] = right.astype(BF16)
            for k in range(EDGE):
                row = self.band[
                    h, pl.ds((TILE + k) * WIDE + LEFT, SLOTS * TILE), :
                ]
                self.top[k, :, lanes] = row.astype(BF16)

    def start(self):
        lo, ss, rs = self.here.lo, self.ss, self.rs
        left, right = self.edges.at[0], self.edges.at[1]
        send(left, self.got.at[1], ss.at[0], rs.at[1], (self.west, lo))
        send(right, self.got.at[0], ss.at[1], rs.at[0], (self.east, lo))
        send(self.top, self.got_top, ss.at[2], rs.at[2], (self.across, lo))
        for block, landing, i, device in (
            (left, self.got.at[2], 3, self.across_west),
            (right, self.got.at[3], 4, self.across_east),
        ):

            @pl.when(device != self.here.t)
            def _():
                send(block, landing, ss.at[i], rs.at[i], (device, lo))

            @pl.when(device == self.here.t)
            def _():
                pltpu.make_async_copy(block, landing, rs.at[i]).start()

    def finish(self, owned):
        edge = self.edges.at[0]
        await_bytes(edge, self.rs.at[0])
        await_bytes(edge, self.rs.at[1])
        for h in range(2):
            lanes = pl.ds(h * 128, 128)
            for j in range(EDGE):
                start = EDGE * WIDE + LEFT + j
                self.band[h, pl.ds(start - EDGE, TILE, WIDE), :] = self.got[0, j, :, lanes].astype(F32)
                east = self.got[1, j, :, lanes].astype(F32)
                for n in range(1, SLOTS):
                    spot = pl.ds(start + TILE * n, TILE, WIDE)
                    self.band[h, spot, :] = jnp.where(owned == n, east, self.band[h, spot, :])
                self.band[h, pl.ds(start + TILE * SLOTS, TILE, WIDE), :] = east
        await_bytes(self.top, self.rs.at[2])
        await_bytes(edge, self.rs.at[3])
        await_bytes(edge, self.rs.at[4])
        used = owned * TILE
        span = SLOTS * TILE
        spot = lax.broadcasted_iota(jnp.int32, (WIDE, 3 * span), 0) - LEFT
        item = lax.broadcasted_iota(jnp.int32, (WIDE, 3 * span), 1)
        inner = jnp.logical_and(jnp.logical_and(spot >= 0, spot < used), item == used - 1 - spot)
        for k in range(1, EDGE + 1):
            row = TILE - k
            west = jnp.logical_and(spot < 0, item == span + (-1 - spot) * TILE + row)
            west = jnp.logical_and(west, spot >= -EDGE)
            past = spot - used
            east = jnp.logical_and(past >= 0, item == 2 * span + (EDGE - 1 - past) * TILE + row)
            east = jnp.logical_and(east, past < EDGE)
            chosen = jnp.logical_or(inner, jnp.logical_or(west, east))
            pick = jnp.where(chosen, 1.0, 0.0).astype(BF16)
            source = jnp.concatenate(
                [
                    self.got_top[EDGE - k],
                    self.got[2].reshape(EDGE * TILE, C),
                    self.got[3].reshape(EDGE * TILE, C),
                ],
                axis=0,
            )
            fold = jnp.dot(pick, source, preferred_element_type=F32)
            place = pl.ds((EDGE + TILE - 1 + k) * WIDE, WIDE)
            self.band[0, place, :] = fold[:, :128]
            self.band[1, place, :] = fold[:, 128:]

    def drain(self):
        edge = self.edges.at[0]
        await_bytes(edge, self.ss.at[0])
        await_bytes(edge, self.ss.at[1])
        await_bytes(self.top, self.ss.at[2])
        for i, device in ((3, self.across_west), (4, self.across_east)):

            @pl.when(device != self.here.t)
            def _():
                await_bytes(edge, self.ss.at[i])


BLOCKS = SLOTS * TILE // 8


def block_start(block):
    return (block // 2) * (TILE * TILE) + (block % 2) * 8


def stencil(band, taps, h, block, backward):
    base = LEFT - EDGE + block * 8
    total = [None] * TILE
    for b in range(KSIZE):
        straight = [taps[h, pl.ds(a * KSIZE + b, 1), :] for a in range(KSIZE)]
        turned = straight
        if backward:
            turned = [
                taps[h, pl.ds((KSIZE - 1 - a) * KSIZE + KSIZE - 1 - b, 1), :] for a in range(KSIZE)
            ]
        for row in range(EDGE, TILE + 2 * EDGE):
            window = band[h, pl.ds(row * WIDE + base + b, 8), :]
            used = straight if row >= TILE + EDGE else turned
            for a in range(KSIZE):
                r = row - a
                if 0 <= r < TILE:
                    term = used[a] * window
                    total[r] = term if total[r] is None else total[r] + term
    return total


def total(first, landing):
    for k in range(landing.shape[0]):
        first = first + landing[k].astype(F32)
    return first


def line_total(landing):
    run = landing[0].astype(F32)
    for k in range(1, landing.shape[0]):
        run = run + landing[k].astype(F32)
    return run


class Reducer:
    def __init__(self, here, refs, ss, rs):
        self.here, self.ss, self.rs = here, ss, rs
        (
            self.wide, self.small, self.out, self.small_out, self.core_out, self.core_in, self.held, self.p_in,
            self.q_in, self.zz, self.yy, self.s_in, self.s_sum,
        ) = refs
        c, x, y, z = here.core, here.x, here.y, here.z
        self.partner = here.device(1 - c, x, y, z)
        self.regions = (
            (0, PR, x * NY + y, self.p_in, self.zz, z, "z"),
            (REGION, QR, x * NZ + z, self.q_in, self.yy, y, "y"),
        )

    def plane(self, region):
        c, x, y, z = self.here.core, self.here.x, self.here.y, self.here.z
        n = NZ if region else NY
        for dx, d in offsets(NX, n):
            px = (x + dx) % NX
            if region:
                pz = (z + d) % NZ
                yield self.here.device(c, px, y, pz), px * NZ + pz, dx * n + d - 1
            else:
                py = (y + d) % NY
                yield self.here.device(c, px, py, z), px * NY + py, dx * n + d - 1

    def core(self, k):
        span = rows(k * 512, 512)
        self.core_out[span] = self.wide[1 - self.here.core, span].astype(BF16)
        send(self.core_out.at[span], self.core_in.at[span], self.ss.at[k], self.rs.at[k], self.partner)

    def scatter(self, region):
        start, size, mine, landing, line, spot, axis = self.regions[region]
        sem = 4 + region
        for k in (2 * region, 2 * region + 1):
            await_bytes(self.core_in.at[pl.ds(0, 512)], self.rs.at[k])
        span = pl.ds(start, REGION)
        self.held[span] = (self.wide[self.here.core, span] + self.core_in[span].astype(F32)).astype(BF16)
        for device, place, slot in self.plane(region):
            send(
                self.held.at[rows(start + place * size, size)], landing.at[slot], self.ss.at[sem], self.rs.at[sem],
                device,
            )

    def line(self, region):
        start, size, mine, landing, line, spot, axis = self.regions[region]
        sem = 6 + region
        await_bytes(landing, self.rs.at[4 + region])
        span = rows(start + mine * size, size)
        own = self.wide[self.here.core, span] + self.core_in[span].astype(F32)
        line[spot] = total(own, landing).astype(BF16)
        for d in steps(axis)[::-1]:
            send(line.at[spot], line.at[spot], self.ss.at[sem], self.rs.at[sem], self.here.along(axis, d)[1])

    def gather(self, region):
        start, size, mine, landing, line, spot, axis = self.regions[region]
        sem = 8 + region
        await_bytes(line.at[pl.ds(0, line.shape[0] - 1)], self.rs.at[6 + region])
        span = rows(start + mine * size, size)
        self.out[self.here.core, span] = line_total(line).astype(BF16)
        ref = self.out.at[self.here.core, span]
        for device, place, slot in self.plane(region):
            send(ref, ref, self.ss.at[sem], self.rs.at[sem], device)

    def core_back(self, region):
        start, size, mine, landing, line, spot, axis = self.regions[region]
        await_bytes(self.bytes_of(REGION - size), self.rs.at[8 + region])
        ref = self.out.at[self.here.core, pl.ds(start, REGION)]
        send(ref, ref, self.ss.at[10 + region], self.rs.at[10 + region], self.partner)

    def core_done(self, region):
        await_bytes(self.bytes_of(REGION), self.rs.at[10 + region])

    def bytes_of(self, count):
        return self.out.at[0, pl.ds(0, count)]

    def small_peers(self):
        c, x, y, z = self.here.core, self.here.x, self.here.y, self.here.z
        for dc, dy in offsets(2, NY):
            pc, py = (c + dc) % 2, (y + dy) % NY
            yield self.here.device(pc, x, py, z), pc, py, dc * NY + dy - 1

    def small_scatter(self):
        for device, pc, py, slot in self.small_peers():
            send(
                self.small.at[pc, rows(py * SR, SR)], self.s_in.at[slot], self.ss.at[12], self.rs.at[12], device
            )

    def small_plane(self):
        c, x, y, z = self.here.core, self.here.x, self.here.y, self.here.z
        await_bytes(self.s_in, self.rs.at[12])
        mine = x * NZ + z
        self.s_sum[mine] = total(self.small[c, rows(y * SR, SR)], self.s_in)
        for device, place, slot in self.plane(1):
            send(self.s_sum.at[mine], self.s_sum.at[mine], self.ss.at[13], self.rs.at[13], device)

    def small_gather(self):
        await_bytes(self.s_sum.at[pl.ds(0, NX * NZ - 1)], self.rs.at[13])
        place = rows(self.here.y * SR, SR)
        self.small_out[self.here.core, place] = line_total(self.s_sum)
        ref = self.small_out.at[self.here.core, place]
        for device, pc, py, slot in self.small_peers():
            send(ref, ref, self.ss.at[14], self.rs.at[14], device)

    def small_done(self):
        await_bytes(self.s_in, self.rs.at[14])

    def drain(self):
        ss = self.ss
        for k in range(4):
            await_bytes(self.core_out.at[pl.ds(0, 512)], ss.at[k])
        for region in range(2):
            start, size, mine, landing, line, spot, axis = self.regions[region]
            await_bytes(landing, ss.at[4 + region])
            await_bytes(line.at[pl.ds(0, line.shape[0] - 1)], ss.at[6 + region])
            await_bytes(self.bytes_of(REGION - size), ss.at[8 + region])
            await_bytes(self.bytes_of(REGION), ss.at[10 + region])
        await_bytes(self.s_in, ss.at[12])
        await_bytes(self.s_sum.at[pl.ds(0, NX * NZ - 1)], ss.at[13])
        await_bytes(self.s_in, ss.at[14])


def greet(here):
    barrier = pltpu.get_barrier_semaphore()
    c, x, y, z = here.core, here.x, here.y, here.z
    west, east, across, across_west, across_east = halo_places(here)
    peers = [(device, here.lo) for device in (west, east, across)]
    for dx, dy in offsets(NX, NY):
        peers.append(here.device(c, (x + dx) % NX, (y + dy) % NY, z))
    for dx, dz in offsets(NX, NZ):
        if dz:
            peers.append(here.device(c, (x + dx) % NX, y, (z + dz) % NZ))
    for dy in range(NY):
        peers.append(here.device(1 - c, x, (y + dy) % NY, z))
    for device in peers:
        pl.semaphore_signal(barrier, inc=1, device_id=device, device_id_type=pl.DeviceIdType.MESH)
    for device in (across_west, across_east):

        @pl.when(device != here.t)
        def _():
            pl.semaphore_signal(
                barrier, inc=1, device_id=(device, here.lo), device_id_type=pl.DeviceIdType.MESH
            )

    return barrier, len(peers), (across_west, across_east)


def block_kernel(
    owned_ref, ocean_ref, fields_hbm, grad_hbm, kernel_hbm, gain_hbm, w_in_hbm, w_out_hbm, scale_hbm,
    state_hbm, grad_fields_hbm, wide_hbm, small_hbm,
    fields, grad_out, kernel, ln_gain, layer_scale, band, gband, taps, conv, inverse, normed, dproj, activated, dpreact, projected, dnormed, rowsum, weight_in,
    weight_out, edges, top, got, got_top, edges2, top2, got2, got_top2, small,
    wide, core_out, core_in, held, p_in, q_in, zz, yy, s_in, s_sum, state, grad_fields, wide_out, small_out,
    ss, rs, hs, hr, hs2, hr2, ls, os
):
    here = Place()
    barrier, greeted, maybe = greet(here)
    loads = [
        pltpu.make_async_copy(source, target, ls.at[i])
        for i, (source, target) in enumerate(
            (
                (fields_hbm, fields), (kernel_hbm, kernel), (gain_hbm, ln_gain), (scale_hbm, layer_scale),
                (grad_hbm, grad_out), (w_in_hbm, weight_in), (w_out_hbm, weight_out),
            )
        )
    ]
    for load in loads:
        load.start()
    reducer = Reducer(
        here,
        (
            wide, small, wide_out, small_out, core_out, core_in, held, p_in, q_in, zz, yy, s_in, s_sum,
        ),
        ss,
        rs,
    )
    owned = owned_ref[0]

    def slot_mask(slot):
        live = jnp.logical_and(slot < owned, ocean_ref[slot] > 0)
        return jnp.where(live, 1.0, 0.0).astype(F32)

    def clear(i, carry):
        spot = rows(i * 64, 64)
        for h in range(2):
            band[h, spot, :] = jnp.zeros((64, 128), F32)
            gband[h, spot, :] = jnp.zeros((64, 128), F32)
        return carry

    lax.fori_loop(0, BAND // 64, clear, 0)
    small[...] = jnp.zeros_like(small)
    rowsum[...] = jnp.zeros_like(rowsum)
    loads[0].wait()
    loads[1].wait()
    for a in range(KSIZE):
        line = kernel[a].astype(F32)
        for h in range(2):
            taps[h, a * KSIZE : (a + 1) * KSIZE, :] = line[:, h * 128 : (h + 1) * 128]

    def fill(i, carry):
        slot, r = i // TILE, i % TILE
        line = fields[rows(i * TILE, TILE), :].astype(F32) * slot_mask(slot)
        place = pl.ds(pl.multiple_of((EDGE + r) * WIDE + LEFT + slot * TILE, 8), TILE)
        band[0, place, :] = line[:, :128]
        band[1, place, :] = line[:, 128:]
        return carry

    lax.fori_loop(0, SLOTS * TILE, fill, 0)
    halo = Halo(here, band, edges, top, got, got_top, hs, hr)
    halo.gather_edges(owned)
    at_seam = jnp.logical_or(maybe[0] == here.t, maybe[1] == here.t)

    @pl.when(at_seam)
    def _():
        pl.semaphore_wait(barrier, greeted + 1)

    @pl.when(jnp.logical_not(at_seam))
    def _():
        pl.semaphore_wait(barrier, greeted + 2)

    halo.start()
    halo.finish(owned)

    def convolve(i, carry):
        h, block = i // BLOCKS, i % BLOCKS
        result = stencil(band, taps, h, block, False)
        for r in range(TILE):
            conv[h, pl.ds(pl.multiple_of(block_start(block) + r * TILE, 8), 8), :] = result[r]
        return carry

    lax.fori_loop(0, 2 * BLOCKS, convolve, 0)

    for load in loads[2:5]:
        load.wait()
    gain = [ln_gain[:, :128], ln_gain[:, 128:]]
    scale = [layer_scale[:, :128], layer_scale[:, 128:]]
    STEP = 128

    def norm(i, carry):
        span = rows(i * STEP, STEP)
        mask = slot_mask(i // (TILE * TILE // STEP))
        parts = [conv[h, span, :] for h in range(2)]
        mean = jnp.sum(parts[0] + parts[1], axis=1, keepdims=True) * (1.0 / C)
        centred = [part - mean for part in parts]
        variance = jnp.sum(
            centred[0] * centred[0] + centred[1] * centred[1], axis=1, keepdims=True
        ) * (1.0 / C)
        scaled = lax.rsqrt(variance + EPS)
        inverse[span, :] = jnp.broadcast_to(scaled, (STEP, 128))
        for h in range(2):
            lanes = pl.ds(h * 128, 128)
            yhat = centred[h] * scaled
            conv[h, span, :] = yhat
            normed[span, lanes] = (yhat * gain[h]).astype(BF16)
            cotangent = grad_out[span, lanes].astype(F32)
            dproj[span, lanes] = (mask * scale[h] * cotangent).astype(BF16)
        return carry

    lax.fori_loop(0, CELLS // STEP, norm, 0)
    loads[5].wait()
    loads[6].wait()
    across_rows = (((0,), (0,)), ((), ()))
    across_cols = (((1,), (1,)), ((), ()))

    def quarter(k, carry):
        part_in = weight_in[:, rows(k * 256, 256)]
        part_out = weight_out[rows(k * 256, 256), :]
        for m in range(SLOTS):
            span = pl.ds(m * 256, 256)
            cells, slopes = normed[span, :], dproj[span, :]
            v = jnp.dot(cells, part_in, preferred_element_type=F32)
            dact = lax.dot_general(slopes, part_out, across_cols, preferred_element_type=F32)
            square = v * v
            t = jnp.tanh(v * (GELU_A + (GELU_A * GELU_B) * square))
            half = 0.5 + 0.5 * t
            act = (v * half).astype(BF16)
            slope = half + (v * half) * (1.0 - t) * (GELU_A + (3.0 * GELU_A * GELU_B) * square)
            dpre = (dact * slope).astype(BF16)
            activated[span, :] = act
            dpreact[span, :] = dpre
            forward = jnp.dot(act, part_out, preferred_element_type=F32)
            back = lax.dot_general(dpre, part_in, across_cols, preferred_element_type=F32)
            first = k == 0
            projected[span, :] = jnp.where(first, forward, projected[span, :] + forward)
            dnormed[span, :] = jnp.where(first, back, dnormed[span, :] + back)
        grad_o = lax.dot_general(activated[...], dproj[...], across_rows, preferred_element_type=F32)
        grad_i = lax.dot_general(normed[...], dpreact[...], across_rows, preferred_element_type=F32)
        for h in range(2):
            spot = rows(k * 512 + h * 256, 256)
            wide[0, spot, :] = grad_i[:, h * 128 : (h + 1) * 128]
            wide[1, spot, :] = grad_o[:, h * 128 : (h + 1) * 128]
        reducer.core(k)

        @pl.when(k == 2)
        def _():
            reducer.scatter(0)

        return carry

    projected[...] = jnp.zeros_like(projected)
    dnormed[...] = jnp.zeros_like(dnormed)
    lax.fori_loop(0, HID // 256, quarter, 0)

    def norm_back(i, carry):
        span = rows(i * STEP, STEP)
        slot, r = i // (TILE * TILE // STEP), (i % (TILE * TILE // STEP)) * (STEP // TILE)
        lanes = [pl.ds(h * 128, 128) for h in range(2)]
        back = [dnormed[span, lanes[h]] for h in range(2)]
        yhat = [conv[h, span, :] for h in range(2)]
        for h in range(2):
            rowsum[h] += jnp.sum((back[h] * yhat[h]).reshape(STEP // 8, 8, 128), axis=0)
        dhat = [back[h] * gain[h] for h in range(2)]
        mean = jnp.sum(dhat[0] + dhat[1], axis=1, keepdims=True) * (1.0 / C)
        tilt = jnp.sum(dhat[0] * yhat[0] + dhat[1] * yhat[1], axis=1, keepdims=True) * (1.0 / C)
        for h in range(2):
            grad = inverse[span, :] * (dhat[h] - mean - yhat[h] * tilt)
            grad = grad.astype(BF16).astype(F32)
            for q in range(STEP // TILE):
                place = pl.ds(
                    pl.multiple_of((EDGE + r + q) * WIDE + LEFT + slot * TILE, 8), TILE
                )
                gband[h, place, :] = grad[q * TILE : (q + 1) * TILE]
        return carry

    lax.fori_loop(0, CELLS // STEP, norm_back, 0)
    halo_back = Halo(here, gband, edges2, top2, got2, got_top2, hs2, hr2)
    halo_back.gather_edges(owned)
    halo_back.start()
    reducer.scatter(1)

    def finish_state(i, carry):
        span = rows(i * STEP, STEP)
        mask = slot_mask(i // (TILE * TILE // STEP))
        for h in range(2):
            lanes = pl.ds(h * 128, 128)
            out = projected[span, lanes]
            rowsum[2 + h] += jnp.sum(
                (mask * grad_out[span, lanes].astype(F32) * out).reshape(STEP // 8, 8, 128), axis=0
            )
            kept = fields[span, lanes].astype(F32)
            state[span, lanes] = (mask * (kept + scale[h] * out)).astype(BF16)
        return carry

    lax.fori_loop(0, CELLS // STEP, finish_state, 0)
    write_state = pltpu.make_async_copy(state, state_hbm, os.at[0])
    write_state.start()

    def kernel_grad(i, carry):
        h, b = i // KSIZE, i % KSIZE

        def one_block(block, sums):
            sums = list(sums)
            base = LEFT + block * 8
            cots = [gband[h, pl.ds(pl.multiple_of((EDGE + r) * WIDE + base, 8), 8), :] for r in range(TILE)]
            for row in range(EDGE, TILE + 2 * EDGE):
                window = band[h, pl.ds(row * WIDE + base - EDGE + b, 8), :]
                for a in range(KSIZE):
                    if 0 <= row - a < TILE:
                        sums[a] = sums[a] + cots[row - a] * window
            return tuple(sums)

        zero = tuple(jnp.zeros((8, 128), F32) for a in range(KSIZE))
        sums = lax.fori_loop(0, BLOCKS, one_block, zero)
        for a in range(KSIZE):
            small[h, pl.ds(a * KSIZE + b, 1), :] = jnp.sum(sums[a], axis=0, keepdims=True)
        return carry

    lax.fori_loop(0, 2 * KSIZE, kernel_grad, 0)
    for h in range(2):
        small[h, KSIZE * KSIZE : KSIZE * KSIZE + 1, :] = jnp.sum(rowsum[h], axis=0, keepdims=True)
        small[h, KSIZE * KSIZE + 1 : KSIZE * KSIZE + 2, :] = jnp.sum(rowsum[2 + h], axis=0, keepdims=True)
    reducer.small_scatter()
    halo_back.finish(owned)

    def convolve_back(i, carry):
        h, block = i % 2, i // 2
        result = stencil(gband, taps, h, block, True)
        for r in range(TILE):
            conv[h, pl.ds(pl.multiple_of(block_start(block) + r * TILE, 8), 8), :] = result[r]
        return carry

    def finish_grad(i, carry):
        span = rows(i * STEP, STEP)
        mask = slot_mask(i // (TILE * TILE // STEP))
        for h in range(2):
            lanes = pl.ds(h * 128, 128)
            grad = mask * (grad_out[span, lanes].astype(F32) + conv[h, span, :])
            grad_fields[span, lanes] = grad.astype(BF16)
        return carry

    lax.fori_loop(0, BLOCKS, convolve_back, 0)
    reducer.line(0)
    lax.fori_loop(BLOCKS, 2 * BLOCKS, convolve_back, 0)
    reducer.line(1)
    reducer.small_plane()
    lax.fori_loop(0, CELLS // STEP, finish_grad, 0)
    write_grad = pltpu.make_async_copy(grad_fields, grad_fields_hbm, os.at[1])
    write_grad.start()
    reducer.gather(0)
    reducer.gather(1)
    reducer.small_gather()
    writes = [write_state, write_grad]
    for region in range(2):
        reducer.core_back(region)
        span = pl.ds(region * REGION, REGION)
        writes.append(
            pltpu.make_async_copy(
                wide_out.at[here.core, span], wide_hbm.at[here.core, span], os.at[2 + region]
            )
        )
        writes[-1].start()
    reducer.small_done()
    writes.append(pltpu.make_async_copy(small_out, small_hbm, os.at[4]))
    writes[-1].start()
    for region in range(2):
        reducer.core_done(region)
        span = pl.ds(region * REGION, REGION)
        writes.append(
            pltpu.make_async_copy(
                wide_out.at[1 - here.core, span], wide_hbm.at[1 - here.core, span], os.at[5 + region]
            )
        )
        writes[-1].start()
    reducer.drain()
    halo.drain()
    halo_back.drain()
    for write in writes:
        write.wait()


def block_call(block_count, ocean, fields, grad_out, kernel, ln_gain, w_in, w_out, layer_scale):
    vmem = pl.BlockSpec(memory_space=pltpu.VMEM)
    smem = pl.BlockSpec(memory_space=pltpu.SMEM)
    hbm = pl.BlockSpec(memory_space=pl.ANY)
    edges = pltpu.VMEM((2, EDGE, TILE, C), BF16)
    top = pltpu.VMEM((EDGE, SLOTS * TILE, C), BF16)
    got = pltpu.VMEM((4, EDGE, TILE, C), BF16)
    scratch = [
        pltpu.VMEM((CELLS, C), BF16),
        pltpu.VMEM((CELLS, C), BF16),
        pltpu.VMEM((KSIZE, KSIZE, C), BF16),
        pltpu.VMEM((1, C), F32),
        pltpu.VMEM((1, C), F32),
        pltpu.VMEM((2, BAND, 128), F32),
        pltpu.VMEM((2, BAND, 128), F32),
        pltpu.VMEM((2, 56, 128), F32),
        pltpu.VMEM((2, CELLS, 128), F32),
        pltpu.VMEM((CELLS, 128), F32),
        pltpu.VMEM((CELLS, C), BF16),
        pltpu.VMEM((CELLS, C), BF16),
        pltpu.VMEM((CELLS, 256), BF16),
        pltpu.VMEM((CELLS, 256), BF16),
        pltpu.VMEM((CELLS, C), F32),
        pltpu.VMEM((CELLS, C), F32),
        pltpu.VMEM((4, 8, 128), F32),
        pltpu.VMEM((C, HID), BF16),
        pltpu.VMEM((HID, C), BF16),
        edges, top, got, top, edges, top, got, top,
        pltpu.VMEM((2, SMALL, 128), F32),
        pltpu.VMEM((2, HALF, 128), F32),
        pltpu.VMEM((HALF, 128), BF16),
        pltpu.VMEM((HALF, 128), BF16),
        pltpu.VMEM((HALF, 128), BF16),
        pltpu.VMEM((NX * NY - 1, PR, 128), BF16),
        pltpu.VMEM((NX * NZ - 1, QR, 128), BF16),
        pltpu.VMEM((NZ, PR, 128), BF16),
        pltpu.VMEM((NY, QR, 128), BF16),
        pltpu.VMEM((2 * NY - 1, SR, 128), F32),
        pltpu.VMEM((NX * NZ, SR, 128), F32),
        pltpu.VMEM((CELLS, C), BF16),
        pltpu.VMEM((CELLS, C), BF16),
        pltpu.VMEM((2, HALF, 128), BF16),
        pltpu.VMEM((2, SMALL, 128), F32),
        pltpu.SemaphoreType.DMA((15,)),
        pltpu.SemaphoreType.DMA((15,)),
        pltpu.SemaphoreType.DMA((5,)),
        pltpu.SemaphoreType.DMA((5,)),
        pltpu.SemaphoreType.DMA((5,)),
        pltpu.SemaphoreType.DMA((5,)),
        pltpu.SemaphoreType.DMA((7,)),
        pltpu.SemaphoreType.DMA((7,)),
    ]
    return pl.pallas_call(
        block_kernel,
        out_shape=(
            jax.ShapeDtypeStruct((CELLS, C), BF16),
            jax.ShapeDtypeStruct((CELLS, C), BF16),
            jax.ShapeDtypeStruct((2, HALF, 128), BF16),
            jax.ShapeDtypeStruct((2, SMALL, 128), F32),
        ),
        in_specs=[smem, smem] + [hbm] * 7,
        out_specs=(hbm,) * 4,
        scratch_shapes=scratch,
        compiler_params=pltpu.CompilerParams(
            collective_id=1, has_side_effects=True, vmem_limit_bytes=56 * 1024 * 1024
        ),
    )(block_count, ocean, fields, grad_out, kernel, ln_gain, w_in, w_out, layer_scale)


def results_kernel(
    norm, state_hbm, fields_hbm, wide_hbm, small_hbm, state_out, fields_out, kernel_out, gain_out, in_out, out_out,
    scale_out, state, grad_fields, wide, small, grad_in, grad_out, grad_kernel, grad_gain, grad_scale, sems, loads
):
    copies = [
        pltpu.make_async_copy(state, state_out, sems.at[0]),
        pltpu.make_async_copy(grad_fields, fields_out, sems.at[1]),
    ]
    through = [
        pltpu.make_async_copy(state_hbm, state, loads.at[9]),
        pltpu.make_async_copy(fields_hbm, grad_fields, loads.at[10]),
    ]
    fetches = [pltpu.make_async_copy(small_hbm, small, loads.at[8])]
    for k in range(4):
        for side in range(2):
            span = pl.ds(k * 512, 512)
            fetches.append(
                pltpu.make_async_copy(
                    wide_hbm.at[side, span], wide.at[side, span], loads.at[2 * k + side]
                )
            )
    for copy in through + fetches:
        copy.start()
    for fetch, copy in zip(through, copies):
        fetch.wait()
        copy.start()
    fetches[0].wait()
    count = KSIZE * KSIZE
    for h in range(2):
        lanes = pl.ds(h * 128, 128)
        for a in range(KSIZE):
            grad_kernel[a, :, lanes] = small[h, pl.ds(a * KSIZE, KSIZE), :] * norm
        grad_gain[:, lanes] = small[h, pl.ds(count, 1), :] * norm
        grad_scale[:, lanes] = small[h, pl.ds(count + 1, 1), :] * norm
    for i, (source, target) in enumerate(
        ((grad_kernel, kernel_out), (grad_gain, gain_out), (grad_scale, scale_out))
    ):
        copies.append(pltpu.make_async_copy(source, target, sems.at[2 + i]))
        copies[-1].start()
    for k in range(4):
        for side in range(2):
            fetches[1 + 2 * k + side].wait()
            for h in range(2):
                part = wide[side, pl.ds(k * 512 + h * 256, 256), :].astype(F32) * norm
                if side:
                    grad_out[pl.ds(k * 256, 256), pl.ds(h * 128, 128)] = part
                else:
                    grad_in[:, pl.ds(k * 256 + h * 128, 128)] = part
            if side:
                spot = (pl.ds(k * 256, 256), slice(None))
                source, target = grad_out, out_out
            else:
                spot = (slice(None), pl.ds(k * 256, 256))
                source, target = grad_in, in_out
            copies.append(
                pltpu.make_async_copy(source.at[spot], target.at[spot], sems.at[5 + 2 * k + side])
            )
            copies[-1].start()
    for copy in copies:
        copy.wait()


def results_call(norm, state, grad_fields, wide, small):
    hbm = pl.BlockSpec(memory_space=pl.ANY)
    sums = [((KSIZE, KSIZE, C), F32), ((1, C), F32), ((C, HID), F32), ((HID, C), F32), ((1, C), F32)]
    return pl.pallas_call(
        functools.partial(results_kernel, norm),
        out_shape=tuple(
            jax.ShapeDtypeStruct(*spec) for spec in [((CELLS, C), BF16), ((CELLS, C), BF16)] + sums
        ),
        in_specs=[hbm] * 4,
        out_specs=(hbm,) * 7,
        scratch_shapes=[
            pltpu.VMEM((CELLS, C), BF16),
            pltpu.VMEM((CELLS, C), BF16),
            pltpu.VMEM((2, HALF, 128), BF16),
            pltpu.VMEM((2, SMALL, 128), F32),
            pltpu.VMEM((C, HID), F32),
            pltpu.VMEM((HID, C), F32),
            pltpu.VMEM((KSIZE, KSIZE, C), F32),
            pltpu.VMEM((1, C), F32),
            pltpu.VMEM((1, C), F32),
            pltpu.SemaphoreType.DMA((13,)),
            pltpu.SemaphoreType.DMA((11,)),
        ],
        compiler_params=pltpu.CompilerParams(vmem_limit_bytes=56 * 1024 * 1024),
    )(state, grad_fields, wide, small)


def shards(fields, grad_out, block_count, ocean, kernel, ln_gain, w_in, w_out, layer_scale):
    shape = fields.shape
    samples, slot_count, tile_rows, tile_cols, channels = shape
    partials = block_call(
        block_count,
        ocean,
        fields.reshape(CELLS, channels),
        grad_out.reshape(CELLS, channels),
        kernel,
        ln_gain.reshape(1, channels),
        w_in,
        w_out,
        layer_scale.reshape(1, channels),
    )
    norm = (
        samples * lax.axis_size("dp") * slot_count * lax.axis_size("tiles") * tile_rows * tile_cols
    ) ** (-0.5)
    state, grad_fields, kernel_sum, gain_sum, w_in_sum, w_out_sum, scale_sum = results_call(norm, *partials)
    return (
        state.reshape(shape),
        grad_fields.reshape(shape),
        kernel_sum,
        gain_sum.reshape(channels),
        w_in_sum,
        w_out_sum,
        scale_sum.reshape(channels),
    )


def solution(mesh):
    placed = (
        P("dp", "tiles", None, None, None),
        P("dp", "tiles", None, None, None),
        P("tiles"),
        P("tiles"),
        P(),
        P(),
        P(),
        P(),
        P(),
    )
    return jax.shard_map(
        shards,
        mesh=mesh,
        in_specs=placed,
        out_specs=(
            P("dp", "tiles", None, None, None),
            P("dp", "tiles", None, None, None),
            P(),
            P(),
            P(),
            P(),
            P(),
        ),
        check_vma=False,
    )
```

```python
import functools

import jax
import jax.numpy as jnp
from jax import lax
from jax.experimental import pallas as pl
from jax.experimental.pallas import tpu as pltpu
from jax.sharding import PartitionSpec as P

HID = 1024
KSIZE = 7
NX, NZ, NYH = 4, 8, 4
NY = 2 * NYH
HALF = 2048
REGION = HALF // 2
SMALL = 64
QUARTER = HALF // 4
PR, QR = QUARTER // (NX * NY), QUARTER // (NX * NZ)
SR = SMALL // NY
F32, BF16 = jnp.float32, jnp.bfloat16


class Place:
    def __init__(self):
        t = lax.axis_index("tiles")
        self.t = t
        self.lo = lax.axis_index("dp")
        self.core = t % 2
        self.yh = (t // 2) % NYH
        self.z = (t // (2 * NYH)) % NZ
        self.x = t // (2 * NYH * NZ)
        self.y = self.yh * 2 + self.lo

    def device(self, core, x, y, z):
        return (((x * NZ + z) * NYH + y // 2) * 2 + core, y % 2)

    def along(self, axis, step):
        if axis == "core":
            place = 1 - self.core
            return place, (self.t + place - self.core, self.lo)
        if axis == "x":
            place = (self.x + step) % NX
            return place, (self.t + (place - self.x) * (2 * NYH * NZ), self.lo)
        if axis == "z":
            place = (self.z + step) % NZ
            return place, (self.t + (place - self.z) * (2 * NYH), self.lo)
        place = (self.y + step) % NY
        return place, (self.t + (place // 2 - self.yh) * 2, place % 2)


COUNT = {"x": NX, "y": NY, "z": NZ, "core": 2}


def steps(axis):
    n = COUNT[axis]
    near = []
    for d in range(1, n // 2 + 1):
        near += [d, n - d] if d != n - d else [d]
    return near


def offsets(*sizes):
    found = [()]
    for n in sizes:
        found = [step + (d,) for step in found for d in range(n)]
    far = lambda step: -sum(min(d, n - d) for d, n in zip(step, sizes))
    return sorted((step for step in found if any(step)), key=far)


def send(src, dst, send_sem, recv_sem, device):
    pltpu.make_async_remote_copy(
        src_ref=src,
        dst_ref=dst,
        send_sem=send_sem,
        recv_sem=recv_sem,
        device_id=device,
        device_id_type=pl.DeviceIdType.MESH,
    ).start()


def await_bytes(like, sem):
    pltpu.make_async_copy(like, like, sem).wait()


def rows(start, size):
    if isinstance(start, int):
        return pl.ds(start, size)
    return pl.ds(pl.multiple_of(start, size), size)


EPS = 1e-06
C = 256
TILE = 16
SLOTS = 3
CELLS = SLOTS * TILE * TILE
WIDE = 64
LEFT = 8
EDGE = KSIZE // 2
BAND = (TILE + 2 * EDGE) * WIDE
GELU_A = 0.7978845608028654
GELU_B = 0.044715


def halo_places(here):
    count = 2 * NX * NZ * NYH
    half = count // 2

    def swap(i):
        return i + (i // half) * (count + half - 1 - 2 * i)

    rank = swap(here.t)
    west = swap((rank + count - 1) % count)
    east = swap((rank + 1) % count)
    across = (here.t + half) % count
    across_west = (west + half) % count
    across_east = (east + half) % count
    return west, east, across, across_west, across_east


class Halo:
    def __init__(self, here, band, edges, top, got, got_top, ss, rs):
        self.here, self.band, self.edges, self.top = here, band, edges, top
        self.got, self.got_top, self.ss, self.rs = got, got_top, ss, rs
        self.west, self.east, self.across, self.across_west, self.across_east = halo_places(here)

    def gather_edges(self, owned):
        for h in range(2):
            lanes = pl.ds(h * 128, 128)
            for j in range(EDGE):
                start = EDGE * WIDE + LEFT + j
                left = self.band[h, pl.ds(start, TILE, WIDE), :]
                self.edges[0, j, :, lanes] = left.astype(BF16)
                ends = [
                    self.band[h, pl.ds(start + TILE * n - EDGE, TILE, WIDE), :]
                    for n in range(1, SLOTS + 1)
                ]
                right = jnp.where(owned == 1, ends[0], jnp.where(owned == 2, ends[1], ends[2]))
                self.edges[1, j, :, lanes] = right.astype(BF16)
            for k in range(EDGE):
                row = self.band[
                    h, pl.ds((TILE + k) * WIDE + LEFT, SLOTS * TILE), :
                ]
                self.top[k, :, lanes] = row.astype(BF16)

    def start(self):
        lo, ss, rs = self.here.lo, self.ss, self.rs
        left, right = self.edges.at[0], self.edges.at[1]
        send(left, self.got.at[1], ss.at[0], rs.at[1], (self.west, lo))
        send(right, self.got.at[0], ss.at[1], rs.at[0], (self.east, lo))
        send(self.top, self.got_top, ss.at[2], rs.at[2], (self.across, lo))
        for block, landing, i, device in (
            (left, self.got.at[2], 3, self.across_west),
            (right, self.got.at[3], 4, self.across_east),
        ):

            @pl.when(device != self.here.t)
            def _():
                send(block, landing, ss.at[i], rs.at[i], (device, lo))

            @pl.when(device == self.here.t)
            def _():
                pltpu.make_async_copy(block, landing, rs.at[i]).start()

    def finish(self, owned):
        edge = self.edges.at[0]
        await_bytes(edge, self.rs.at[0])
        await_bytes(edge, self.rs.at[1])
        for h in range(2):
            lanes = pl.ds(h * 128, 128)
            for j in range(EDGE):
                start = EDGE * WIDE + LEFT + j
                self.band[h, pl.ds(start - EDGE, TILE, WIDE), :] = self.got[0, j, :, lanes].astype(F32)
                east = self.got[1, j, :, lanes].astype(F32)
                for n in range(1, SLOTS):
                    spot = pl.ds(start + TILE * n, TILE, WIDE)
                    self.band[h, spot, :] = jnp.where(owned == n, east, self.band[h, spot, :])
                self.band[h, pl.ds(start + TILE * SLOTS, TILE, WIDE), :] = east
        await_bytes(self.top, self.rs.at[2])
        await_bytes(edge, self.rs.at[3])
        await_bytes(edge, self.rs.at[4])
        used = owned * TILE
        span = SLOTS * TILE
        spot = lax.broadcasted_iota(jnp.int32, (WIDE, 3 * span), 0) - LEFT
        item = lax.broadcasted_iota(jnp.int32, (WIDE, 3 * span), 1)
        inner = jnp.logical_and(jnp.logical_and(spot >= 0, spot < used), item == used - 1 - spot)
        for k in range(1, EDGE + 1):
            row = TILE - k
            west = jnp.logical_and(spot < 0, item == span + (-1 - spot) * TILE + row)
            west = jnp.logical_and(west, spot >= -EDGE)
            past = spot - used
            east = jnp.logical_and(past >= 0, item == 2 * span + (EDGE - 1 - past) * TILE + row)
            east = jnp.logical_and(east, past < EDGE)
            chosen = jnp.logical_or(inner, jnp.logical_or(west, east))
            pick = jnp.where(chosen, 1.0, 0.0).astype(BF16)
            source = jnp.concatenate(
                [
                    self.got_top[EDGE - k],
                    self.got[2].reshape(EDGE * TILE, C),
                    self.got[3].reshape(EDGE * TILE, C),
                ],
                axis=0,
            )
            fold = jnp.dot(pick, source, preferred_element_type=F32)
            place = pl.ds((EDGE + TILE - 1 + k) * WIDE, WIDE)
            self.band[0, place, :] = fold[:, :128]
            self.band[1, place, :] = fold[:, 128:]

    def drain(self):
        edge = self.edges.at[0]
        await_bytes(edge, self.ss.at[0])
        await_bytes(edge, self.ss.at[1])
        await_bytes(self.top, self.ss.at[2])
        for i, device in ((3, self.across_west), (4, self.across_east)):

            @pl.when(device != self.here.t)
            def _():
                await_bytes(edge, self.ss.at[i])


BLOCKS = SLOTS * TILE // 8


def block_start(block):
    return (block // 2) * (TILE * TILE) + (block % 2) * 8


def stencil(band, taps, h, block, backward, last):
    base = LEFT - EDGE + block * 8
    total = [None] * TILE
    for b in range(KSIZE):
        straight = [taps[h, pl.ds(a * KSIZE + b, 1), :] for a in range(KSIZE)]
        turned = straight
        if backward:
            turned = [
                taps[h, pl.ds((KSIZE - 1 - a) * KSIZE + KSIZE - 1 - b, 1), :] for a in range(KSIZE)
            ]
        for row in range(EDGE, last):
            window = band[h, pl.ds(row * WIDE + base + b, 8), :]
            used = straight if row >= TILE + EDGE else turned
            for a in range(KSIZE):
                r = row - a
                if 0 <= r < TILE:
                    term = used[a] * window
                    total[r] = term if total[r] is None else total[r] + term
    return total


def total(first, landing):
    for k in range(landing.shape[0]):
        first = first + landing[k].astype(F32)
    return first


def line_total(landing):
    run = landing[0].astype(F32)
    for k in range(1, landing.shape[0]):
        run = run + landing[k].astype(F32)
    return run


class Reducer:
    def __init__(self, here, refs, ss, rs):
        self.here, self.ss, self.rs = here, ss, rs
        (
            self.wide, self.small, self.out, self.small_out, self.core_out, self.core_in, self.held, self.p_in,
            self.q_in, self.zz, self.yy, self.s_in, self.s_sum,
        ) = refs
        c, x, y, z = here.core, here.x, here.y, here.z
        self.partner = here.device(1 - c, x, y, z)
        self.regions = (
            (0, PR, x * NY + y, self.p_in, self.zz, z, "z"),
            (REGION, QR, x * NZ + z, self.q_in, self.yy, y, "y"),
        )

    def plane(self, region):
        c, x, y, z = self.here.core, self.here.x, self.here.y, self.here.z
        n = NZ if region else NY
        for dx, d in offsets(NX, n):
            px = (x + dx) % NX
            if region:
                pz = (z + d) % NZ
                yield self.here.device(c, px, y, pz), px * NZ + pz, dx * n + d - 1
            else:
                py = (y + d) % NY
                yield self.here.device(c, px, py, z), px * NY + py, dx * n + d - 1

    def core(self, k):
        span = rows(k * 512, 512)
        self.core_out[span] = self.wide[1 - self.here.core, span].astype(BF16)
        send(self.core_out.at[span], self.core_in.at[span], self.ss.at[k], self.rs.at[k], self.partner)

    def scatter(self, k):
        start, size, mine, landing, line, spot, axis = self.regions[k // 2]
        await_bytes(self.core_in.at[pl.ds(0, QUARTER)], self.rs.at[k])
        span = pl.ds(k * QUARTER, QUARTER)
        self.held[span] = (self.wide[self.here.core, span] + self.core_in[span].astype(F32)).astype(BF16)
        for device, place, slot in self.plane(k // 2):
            send(
                self.held.at[rows(k * QUARTER + place * size, size)], landing.at[k % 2, slot], self.ss.at[15 + k],
                self.rs.at[15 + k], device,
            )

    def line(self, region):
        start, size, mine, landing, line, spot, axis = self.regions[region]
        sem = 6 + region
        for i in range(2):
            k = 2 * region + i
            await_bytes(landing.at[i], self.rs.at[15 + k])
            span = rows(k * QUARTER + mine * size, size)
            own = self.wide[self.here.core, span] + self.core_in[span].astype(F32)
            line[spot, i * size : (i + 1) * size] = total(own, landing.at[i]).astype(BF16)
        for d in steps(axis)[::-1]:
            send(line.at[spot], line.at[spot], self.ss.at[sem], self.rs.at[sem], self.here.along(axis, d)[1])

    def gather(self, region):
        start, size, mine, landing, line, spot, axis = self.regions[region]
        sem = 8 + region
        await_bytes(line.at[pl.ds(0, line.shape[0] - 1)], self.rs.at[6 + region])
        span = rows(start + mine * 2 * size, 2 * size)
        self.out[self.here.core, span] = line_total(line).astype(BF16)
        ref = self.out.at[self.here.core, span]
        for device, place, slot in self.plane(region):
            send(ref, ref, self.ss.at[sem], self.rs.at[sem], device)

    def core_back(self, region):
        start, size, mine, landing, line, spot, axis = self.regions[region]
        await_bytes(self.bytes_of(REGION - 2 * size), self.rs.at[8 + region])
        ref = self.out.at[self.here.core, pl.ds(start, REGION)]
        send(ref, ref, self.ss.at[10 + region], self.rs.at[10 + region], self.partner)

    def core_done(self, region):
        await_bytes(self.bytes_of(REGION), self.rs.at[10 + region])

    def bytes_of(self, count):
        return self.out.at[0, pl.ds(0, count)]

    def small_peers(self):
        c, x, y, z = self.here.core, self.here.x, self.here.y, self.here.z
        for dc, dy in offsets(2, NY):
            pc, py = (c + dc) % 2, (y + dy) % NY
            yield self.here.device(pc, x, py, z), pc, py, dc * NY + dy - 1

    def small_scatter(self):
        for device, pc, py, slot in self.small_peers():
            send(
                self.small.at[pc, rows(py * SR, SR)], self.s_in.at[slot], self.ss.at[12], self.rs.at[12], device
            )

    def small_plane(self):
        c, x, y, z = self.here.core, self.here.x, self.here.y, self.here.z
        await_bytes(self.s_in, self.rs.at[12])
        mine = x * NZ + z
        self.s_sum[mine] = total(self.small[c, rows(y * SR, SR)], self.s_in)
        for device, place, slot in self.plane(1):
            send(self.s_sum.at[mine], self.s_sum.at[mine], self.ss.at[13], self.rs.at[13], device)

    def small_gather(self):
        await_bytes(self.s_sum.at[pl.ds(0, NX * NZ - 1)], self.rs.at[13])
        place = rows(self.here.y * SR, SR)
        self.small_out[self.here.core, place] = line_total(self.s_sum)
        ref = self.small_out.at[self.here.core, place]
        for device, pc, py, slot in self.small_peers():
            send(ref, ref, self.ss.at[14], self.rs.at[14], device)

    def small_done(self):
        await_bytes(self.s_in, self.rs.at[14])

    def drain(self):
        ss = self.ss
        for k in range(4):
            await_bytes(self.core_out.at[pl.ds(0, 512)], ss.at[k])
        for region in range(2):
            start, size, mine, landing, line, spot, axis = self.regions[region]
            for i in range(2):
                await_bytes(landing.at[i], ss.at[15 + 2 * region + i])
            await_bytes(line.at[pl.ds(0, line.shape[0] - 1)], ss.at[6 + region])
            await_bytes(self.bytes_of(REGION - 2 * size), ss.at[8 + region])
            await_bytes(self.bytes_of(REGION), ss.at[10 + region])
        await_bytes(self.s_in, ss.at[12])
        await_bytes(self.s_sum.at[pl.ds(0, NX * NZ - 1)], ss.at[13])
        await_bytes(self.s_in, ss.at[14])


def greet(here):
    barrier = pltpu.get_barrier_semaphore()
    c, x, y, z = here.core, here.x, here.y, here.z
    west, east, across, across_west, across_east = halo_places(here)
    peers = [(device, here.lo) for device in (west, east, across)]
    for dx, dy in offsets(NX, NY):
        peers.append(here.device(c, (x + dx) % NX, (y + dy) % NY, z))
    for dx, dz in offsets(NX, NZ):
        if dz:
            peers.append(here.device(c, (x + dx) % NX, y, (z + dz) % NZ))
    for dy in range(NY):
        peers.append(here.device(1 - c, x, (y + dy) % NY, z))
    for device in peers:
        pl.semaphore_signal(barrier, inc=1, device_id=device, device_id_type=pl.DeviceIdType.MESH)
    for device in (across_west, across_east):

        @pl.when(device != here.t)
        def _():
            pl.semaphore_signal(
                barrier, inc=1, device_id=(device, here.lo), device_id_type=pl.DeviceIdType.MESH
            )

    return barrier, len(peers), (across_west, across_east)


def block_kernel(
    owned_ref, ocean_ref, fields_hbm, grad_hbm, kernel_hbm, gain_hbm, w_in_hbm, w_out_hbm, scale_hbm,
    state_hbm, grad_fields_hbm, wide_hbm, small_hbm,
    fields, grad_out, kernel, ln_gain, layer_scale, band, gband, taps, conv, inverse, normed, dproj, activated, dpreact, projected, dnormed, rowsum, weight_in,
    weight_out, edges, top, got, got_top, edges2, top2, got2, got_top2, small,
    wide, core_out, core_in, held, p_in, q_in, zz, yy, s_in, s_sum, state, grad_fields, wide_out, small_out,
    ss, rs, hs, hr, hs2, hr2, ls, os
):
    here = Place()
    barrier, greeted, maybe = greet(here)
    loads = [
        pltpu.make_async_copy(source, target, ls.at[i])
        for i, (source, target) in enumerate(
            (
                (fields_hbm, fields), (kernel_hbm, kernel), (gain_hbm, ln_gain), (scale_hbm, layer_scale),
                (grad_hbm, grad_out), (w_in_hbm, weight_in), (w_out_hbm, weight_out),
            )
        )
    ]
    for load in loads:
        load.start()
    reducer = Reducer(
        here,
        (
            wide, small, wide_out, small_out, core_out, core_in, held, p_in, q_in, zz, yy, s_in, s_sum,
        ),
        ss,
        rs,
    )
    owned = owned_ref[0]

    def slot_mask(slot):
        live = jnp.logical_and(slot < owned, ocean_ref[slot] > 0)
        return jnp.where(live, 1.0, 0.0).astype(F32)

    def clear(i, carry):
        spot = rows(i * 64, 64)
        for h in range(2):
            band[h, spot, :] = jnp.zeros((64, 128), F32)
            gband[h, spot, :] = jnp.zeros((64, 128), F32)
        return carry

    lax.fori_loop(0, BAND // 64, clear, 0)
    small[...] = jnp.zeros_like(small)
    rowsum[...] = jnp.zeros_like(rowsum)
    loads[0].wait()
    loads[1].wait()
    for a in range(KSIZE):
        line = kernel[a].astype(F32)
        for h in range(2):
            taps[h, a * KSIZE : (a + 1) * KSIZE, :] = line[:, h * 128 : (h + 1) * 128]

    def fill(i, carry):
        slot, r = i // TILE, i % TILE
        line = fields[rows(i * TILE, TILE), :].astype(F32) * slot_mask(slot)
        place = pl.ds(pl.multiple_of((EDGE + r) * WIDE + LEFT + slot * TILE, 8), TILE)
        band[0, place, :] = line[:, :128]
        band[1, place, :] = line[:, 128:]
        return carry

    lax.fori_loop(0, SLOTS * TILE, fill, 0, unroll=4)
    halo = Halo(here, band, edges, top, got, got_top, hs, hr)
    halo.gather_edges(owned)
    at_seam = jnp.logical_or(maybe[0] == here.t, maybe[1] == here.t)

    @pl.when(at_seam)
    def _():
        pl.semaphore_wait(barrier, greeted + 1)

    @pl.when(jnp.logical_not(at_seam))
    def _():
        pl.semaphore_wait(barrier, greeted + 2)

    halo.start()

    def convolve(i, carry):
        h, block = i // BLOCKS, i % BLOCKS
        result = stencil(band, taps, h, block, False, TILE + EDGE)
        for r in range(TILE):
            conv[h, pl.ds(pl.multiple_of(block_start(block) + r * TILE, 8), 8), :] = result[r]
        return carry

    lax.fori_loop(0, 2 * BLOCKS, convolve, 0)

    halo.finish(owned)

    def add_fold(i, carry):
        h, block = i // BLOCKS, i % BLOCKS
        base = LEFT - EDGE + block * 8
        sums = [None] * EDGE
        for b in range(KSIZE):
            for row in range(TILE + EDGE, TILE + 2 * EDGE):
                window = band[h, pl.ds(row * WIDE + base + b, 8), :]
                for a in range(row - TILE + 1, KSIZE):
                    term = taps[h, pl.ds(a * KSIZE + b, 1), :] * window
                    r = row - a - TILE + EDGE
                    sums[r] = term if sums[r] is None else sums[r] + term
        for r in range(EDGE):
            place = pl.ds(pl.multiple_of(block_start(block) + (TILE - EDGE + r) * TILE, 8), 8)
            conv[h, place, :] = conv[h, place, :] + sums[r]
        return carry

    lax.fori_loop(0, 2 * BLOCKS, add_fold, 0, unroll=3)
    sub = lax.broadcasted_iota(jnp.int32, (8, 128), 0)

    def edge_sums(h, base, shifts, held):
        sums = [None] * TILE
        for b in shifts:
            weights = [taps[h, pl.ds(a * KSIZE + b, 1), :] for a in range(KSIZE)]
            for row in range(EDGE, TILE + EDGE):
                window = jnp.where(held(b), band[h, pl.ds(row * WIDE + base + b, 8), :], 0.0)
                for a in range(KSIZE):
                    r = row - a
                    if 0 <= r < TILE:
                        term = weights[a] * window
                        sums[r] = term if sums[r] is None else sums[r] + term
        return sums

    def add_edges(h, carry):
        west = edge_sums(h, LEFT - EDGE, range(EDGE), lambda b: sub < EDGE - b)
        for r in range(TILE):
            place = pl.ds(r * TILE, 8)
            conv[h, place, :] = conv[h, place, :] + west[r]
        east = edge_sums(
            h, LEFT - EDGE + owned * TILE - 8, range(EDGE + 1, KSIZE), lambda b: sub >= 8 + EDGE - b
        )
        for n in range(1, SLOTS + 1):
            for r in range(TILE):
                place = pl.ds((n - 1) * TILE * TILE + r * TILE + 8, 8)
                conv[h, place, :] = conv[h, place, :] + jnp.where(owned == n, east[r], 0.0)
        return carry

    lax.fori_loop(0, 2, add_edges, 0, unroll=2)

    for load in loads[2:5]:
        load.wait()
    gain = [ln_gain[:, :128], ln_gain[:, 128:]]
    scale = [layer_scale[:, :128], layer_scale[:, 128:]]
    STEP = 128

    def norm(i, carry):
        span = rows(i * STEP, STEP)
        mask = slot_mask(i // (TILE * TILE // STEP))
        parts = [conv[h, span, :] for h in range(2)]
        mean = jnp.sum(parts[0] + parts[1], axis=1, keepdims=True) * (1.0 / C)
        centred = [part - mean for part in parts]
        variance = jnp.sum(
            centred[0] * centred[0] + centred[1] * centred[1], axis=1, keepdims=True
        ) * (1.0 / C)
        scaled = lax.rsqrt(variance + EPS)
        inverse[span, :] = jnp.broadcast_to(scaled, (STEP, 128))
        for h in range(2):
            lanes = pl.ds(h * 128, 128)
            yhat = centred[h] * scaled
            conv[h, span, :] = yhat
            normed[span, lanes] = (yhat * gain[h]).astype(BF16)
            cotangent = grad_out[span, lanes].astype(F32)
            dproj[span, lanes] = (mask * scale[h] * cotangent).astype(BF16)
        return carry

    lax.fori_loop(0, CELLS // STEP, norm, 0, unroll=2)
    loads[5].wait()
    loads[6].wait()
    across_rows = (((0,), (0,)), ((), ()))
    across_cols = (((1,), (1,)), ((), ()))

    def quarter(k, carry):
        hidden = rows(k * 256, 256)
        part_in = weight_in[:, hidden]
        part_out = weight_out[rows(k * 256, 256), :]
        for m in range(SLOTS):
            span = pl.ds(m * 256, 256)
            cells, slopes = normed[span, :], dproj[span, :]
            v = jnp.dot(cells, part_in, preferred_element_type=F32)
            dact = lax.dot_general(slopes, part_out, across_cols, preferred_element_type=F32)
            square = v * v
            t = jnp.tanh(v * (GELU_A + (GELU_A * GELU_B) * square))
            half = 0.5 + 0.5 * t
            act = (v * half).astype(BF16)
            slope = half + (v * half) * (1.0 - t) * (GELU_A + (3.0 * GELU_A * GELU_B) * square)
            dpre = (dact * slope).astype(BF16)
            activated[span, hidden] = act
            dpreact[span, hidden] = dpre
        grad_o = lax.dot_general(
            activated[:, hidden], dproj[...], across_rows, preferred_element_type=F32
        )
        grad_i = lax.dot_general(
            normed[...], dpreact[:, hidden], across_rows, preferred_element_type=F32
        )
        for h in range(2):
            spot = rows(k * 512 + h * 256, 256)
            wide[0, spot, :] = grad_i[:, h * 128 : (h + 1) * 128]
            wide[1, spot, :] = grad_o[:, h * 128 : (h + 1) * 128]
        reducer.core(k)

        @pl.when(k == 2)
        def _():
            reducer.scatter(0)
            reducer.scatter(1)

        @pl.when(k == 3)
        def _():
            reducer.scatter(2)

        return carry

    for k in range(HID // 256):
        quarter(k, 0)
    for m in range(SLOTS):
        span = pl.ds(m * 256, 256)
        dnormed[span, :] = lax.dot_general(
            dpreact[span, :], weight_in[...], across_cols, preferred_element_type=F32
        )

    def norm_back(i, carry):
        span = rows(i * STEP, STEP)
        slot, r = i // (TILE * TILE // STEP), (i % (TILE * TILE // STEP)) * (STEP // TILE)
        lanes = [pl.ds(h * 128, 128) for h in range(2)]
        back = [dnormed[span, lanes[h]] for h in range(2)]
        yhat = [conv[h, span, :] for h in range(2)]
        for h in range(2):
            rowsum[h] += jnp.sum((back[h] * yhat[h]).reshape(STEP // 8, 8, 128), axis=0)
        dhat = [back[h] * gain[h] for h in range(2)]
        mean = jnp.sum(dhat[0] + dhat[1], axis=1, keepdims=True) * (1.0 / C)
        tilt = jnp.sum(dhat[0] * yhat[0] + dhat[1] * yhat[1], axis=1, keepdims=True) * (1.0 / C)
        for h in range(2):
            grad = inverse[span, :] * (dhat[h] - mean - yhat[h] * tilt)
            grad = grad.astype(BF16).astype(F32)
            for q in range(STEP // TILE):
                place = pl.ds(
                    pl.multiple_of((EDGE + r + q) * WIDE + LEFT + slot * TILE, 8), TILE
                )
                gband[h, place, :] = grad[q * TILE : (q + 1) * TILE]
        return carry

    lax.fori_loop(0, CELLS // STEP, norm_back, 0, unroll=2)
    halo_back = Halo(here, gband, edges2, top2, got2, got_top2, hs2, hr2)
    halo_back.gather_edges(owned)
    halo_back.start()
    reducer.scatter(3)

    for m in range(SLOTS):
        span = pl.ds(m * 256, 256)
        projected[span, :] = jnp.dot(activated[span, :], weight_out[...], preferred_element_type=F32)

    def finish_state(i, carry):
        span = rows(i * STEP, STEP)
        mask = slot_mask(i // (TILE * TILE // STEP))
        for h in range(2):
            lanes = pl.ds(h * 128, 128)
            out = projected[span, lanes]
            rowsum[2 + h] += jnp.sum(
                (mask * grad_out[span, lanes].astype(F32) * out).reshape(STEP // 8, 8, 128), axis=0
            )
            kept = fields[span, lanes].astype(F32)
            state[span, lanes] = (mask * (kept + scale[h] * out)).astype(BF16)
        return carry

    lax.fori_loop(0, CELLS // STEP, finish_state, 0, unroll=2)
    write_state = pltpu.make_async_copy(state, state_hbm, os.at[0])
    write_state.start()

    def kernel_grad(i, carry):
        h, b = i // KSIZE, i % KSIZE

        def one_block(block, sums):
            sums = list(sums)
            base = LEFT + block * 8
            cots = [gband[h, pl.ds(pl.multiple_of((EDGE + r) * WIDE + base, 8), 8), :] for r in range(TILE)]
            for row in range(EDGE, TILE + 2 * EDGE):
                window = band[h, pl.ds(row * WIDE + base - EDGE + b, 8), :]
                for a in range(KSIZE):
                    if 0 <= row - a < TILE:
                        sums[a] = sums[a] + cots[row - a] * window
            return tuple(sums)

        zero = tuple(jnp.zeros((8, 128), F32) for a in range(KSIZE))
        sums = lax.fori_loop(0, BLOCKS, one_block, zero)
        for a in range(KSIZE):
            small[h, pl.ds(a * KSIZE + b, 1), :] = jnp.sum(sums[a], axis=0, keepdims=True)
        return carry

    lax.fori_loop(0, 2 * KSIZE, kernel_grad, 0)
    for h in range(2):
        small[h, KSIZE * KSIZE : KSIZE * KSIZE + 1, :] = jnp.sum(rowsum[h], axis=0, keepdims=True)
        small[h, KSIZE * KSIZE + 1 : KSIZE * KSIZE + 2, :] = jnp.sum(rowsum[2 + h], axis=0, keepdims=True)
    reducer.small_scatter()
    halo_back.finish(owned)

    def convolve_back(i, carry):
        h, block = i % 2, i // 2
        result = stencil(gband, taps, h, block, True, TILE + 2 * EDGE)
        for r in range(TILE):
            conv[h, pl.ds(pl.multiple_of(block_start(block) + r * TILE, 8), 8), :] = result[r]
        return carry

    def finish_grad(i, carry):
        span = rows(i * STEP, STEP)
        mask = slot_mask(i // (TILE * TILE // STEP))
        for h in range(2):
            lanes = pl.ds(h * 128, 128)
            grad = mask * (grad_out[span, lanes].astype(F32) + conv[h, span, :])
            grad_fields[span, lanes] = grad.astype(BF16)
        return carry

    lax.fori_loop(0, 6, convolve_back, 0)
    reducer.line(0)
    lax.fori_loop(6, 8, convolve_back, 0)
    reducer.line(1)
    lax.fori_loop(8, 2 * BLOCKS, convolve_back, 0)
    reducer.small_plane()
    lax.fori_loop(0, CELLS // STEP, finish_grad, 0)
    write_grad = pltpu.make_async_copy(grad_fields, grad_fields_hbm, os.at[1])
    write_grad.start()
    reducer.gather(0)
    reducer.gather(1)
    reducer.small_gather()
    writes = [write_state, write_grad]
    for region in range(2):
        reducer.core_back(region)
        span = pl.ds(region * REGION, REGION)
        writes.append(
            pltpu.make_async_copy(
                wide_out.at[here.core, span], wide_hbm.at[here.core, span], os.at[2 + region]
            )
        )
        writes[-1].start()
    reducer.small_done()
    writes.append(pltpu.make_async_copy(small_out, small_hbm, os.at[4]))
    writes[-1].start()
    for region in range(2):
        reducer.core_done(region)
        span = pl.ds(region * REGION, REGION)
        writes.append(
            pltpu.make_async_copy(
                wide_out.at[1 - here.core, span], wide_hbm.at[1 - here.core, span], os.at[5 + region]
            )
        )
        writes[-1].start()
    reducer.drain()
    halo.drain()
    halo_back.drain()
    for write in writes:
        write.wait()


def block_call(block_count, ocean, fields, grad_out, kernel, ln_gain, w_in, w_out, layer_scale):
    vmem = pl.BlockSpec(memory_space=pltpu.VMEM)
    smem = pl.BlockSpec(memory_space=pltpu.SMEM)
    hbm = pl.BlockSpec(memory_space=pl.ANY)
    edges = pltpu.VMEM((2, EDGE, TILE, C), BF16)
    top = pltpu.VMEM((EDGE, SLOTS * TILE, C), BF16)
    got = pltpu.VMEM((4, EDGE, TILE, C), BF16)
    scratch = [
        pltpu.VMEM((CELLS, C), BF16),
        pltpu.VMEM((CELLS, C), BF16),
        pltpu.VMEM((KSIZE, KSIZE, C), BF16),
        pltpu.VMEM((1, C), F32),
        pltpu.VMEM((1, C), F32),
        pltpu.VMEM((2, BAND, 128), F32),
        pltpu.VMEM((2, BAND, 128), F32),
        pltpu.VMEM((2, 56, 128), F32),
        pltpu.VMEM((2, CELLS, 128), F32),
        pltpu.VMEM((CELLS, 128), F32),
        pltpu.VMEM((CELLS, C), BF16),
        pltpu.VMEM((CELLS, C), BF16),
        pltpu.VMEM((CELLS, HID), BF16),
        pltpu.VMEM((CELLS, HID), BF16),
        pltpu.VMEM((CELLS, C), F32),
        pltpu.VMEM((CELLS, C), F32),
        pltpu.VMEM((4, 8, 128), F32),
        pltpu.VMEM((C, HID), BF16),
        pltpu.VMEM((HID, C), BF16),
        edges, top, got, top, edges, top, got, top,
        pltpu.VMEM((2, SMALL, 128), F32),
        pltpu.VMEM((2, HALF, 128), F32),
        pltpu.VMEM((HALF, 128), BF16),
        pltpu.VMEM((HALF, 128), BF16),
        pltpu.VMEM((HALF, 128), BF16),
        pltpu.VMEM((2, NX * NY - 1, PR, 128), BF16),
        pltpu.VMEM((2, NX * NZ - 1, QR, 128), BF16),
        pltpu.VMEM((NZ, 2 * PR, 128), BF16),
        pltpu.VMEM((NY, 2 * QR, 128), BF16),
        pltpu.VMEM((2 * NY - 1, SR, 128), F32),
        pltpu.VMEM((NX * NZ, SR, 128), F32),
        pltpu.VMEM((CELLS, C), BF16),
        pltpu.VMEM((CELLS, C), BF16),
        pltpu.VMEM((2, HALF, 128), BF16),
        pltpu.VMEM((2, SMALL, 128), F32),
        pltpu.SemaphoreType.DMA((19,)),
        pltpu.SemaphoreType.DMA((19,)),
        pltpu.SemaphoreType.DMA((5,)),
        pltpu.SemaphoreType.DMA((5,)),
        pltpu.SemaphoreType.DMA((5,)),
        pltpu.SemaphoreType.DMA((5,)),
        pltpu.SemaphoreType.DMA((7,)),
        pltpu.SemaphoreType.DMA((7,)),
    ]
    return pl.pallas_call(
        block_kernel,
        out_shape=(
            jax.ShapeDtypeStruct((CELLS, C), BF16),
            jax.ShapeDtypeStruct((CELLS, C), BF16),
            jax.ShapeDtypeStruct((2, HALF, 128), BF16),
            jax.ShapeDtypeStruct((2, SMALL, 128), F32),
        ),
        in_specs=[smem, smem] + [hbm] * 7,
        out_specs=(hbm,) * 4,
        scratch_shapes=scratch,
        compiler_params=pltpu.CompilerParams(
            collective_id=1, has_side_effects=True, vmem_limit_bytes=56 * 1024 * 1024
        ),
    )(block_count, ocean, fields, grad_out, kernel, ln_gain, w_in, w_out, layer_scale)


def quarter_rows(wide, side, k):
    size = QR if k // 2 else PR
    start = (k // 2) * REGION + (k % 2) * size
    return jnp.concatenate(
        [wide[side, pl.ds(start + i * 2 * size, size), :] for i in range(QUARTER // size)], axis=0
    )


def results_kernel(
    norm, state_hbm, fields_hbm, wide_hbm, small_hbm, state_out, fields_out, kernel_out, gain_out, in_out, out_out,
    scale_out, state, grad_fields, wide, small, grad_in, grad_out, grad_kernel, grad_gain, grad_scale, sems, loads
):
    copies = [
        pltpu.make_async_copy(state, state_out, sems.at[0]),
        pltpu.make_async_copy(grad_fields, fields_out, sems.at[1]),
    ]
    through = [
        pltpu.make_async_copy(state_hbm, state, loads.at[9]),
        pltpu.make_async_copy(fields_hbm, grad_fields, loads.at[10]),
    ]
    fetches = [pltpu.make_async_copy(small_hbm, small, loads.at[8])]
    for k in range(4):
        for side in range(2):
            if k % 2 == 0:
                span = pl.ds(k * QUARTER, REGION)
                fetches.append(
                    pltpu.make_async_copy(
                        wide_hbm.at[side, span], wide.at[side, span], loads.at[k + side]
                    )
                )
    for copy in through + fetches:
        copy.start()
    for fetch, copy in zip(through, copies):
        fetch.wait()
        copy.start()
    fetches[0].wait()
    count = KSIZE * KSIZE
    for h in range(2):
        lanes = pl.ds(h * 128, 128)
        for a in range(KSIZE):
            grad_kernel[a, :, lanes] = small[h, pl.ds(a * KSIZE, KSIZE), :] * norm
        grad_gain[:, lanes] = small[h, pl.ds(count, 1), :] * norm
        grad_scale[:, lanes] = small[h, pl.ds(count + 1, 1), :] * norm
    for i, (source, target) in enumerate(
        ((grad_kernel, kernel_out), (grad_gain, gain_out), (grad_scale, scale_out))
    ):
        copies.append(pltpu.make_async_copy(source, target, sems.at[2 + i]))
        copies[-1].start()
    for k in range(4):
        for side in range(2):
            if k % 2 == 0:
                fetches[1 + k + side].wait()
            for h in range(2):
                part = quarter_rows(wide, side, k)[h * 256 : (h + 1) * 256].astype(F32) * norm
                if side:
                    grad_out[pl.ds(k * 256, 256), pl.ds(h * 128, 128)] = part
                else:
                    grad_in[:, pl.ds(k * 256 + h * 128, 128)] = part
            if side:
                spot = (pl.ds(k * 256, 256), slice(None))
                source, target = grad_out, out_out
            else:
                spot = (slice(None), pl.ds(k * 256, 256))
                source, target = grad_in, in_out
            copies.append(
                pltpu.make_async_copy(source.at[spot], target.at[spot], sems.at[5 + 2 * k + side])
            )
            copies[-1].start()
    for copy in copies:
        copy.wait()


def results_call(norm, state, grad_fields, wide, small):
    hbm = pl.BlockSpec(memory_space=pl.ANY)
    sums = [((KSIZE, KSIZE, C), F32), ((1, C), F32), ((C, HID), F32), ((HID, C), F32), ((1, C), F32)]
    return pl.pallas_call(
        functools.partial(results_kernel, norm),
        out_shape=tuple(
            jax.ShapeDtypeStruct(*spec) for spec in [((CELLS, C), BF16), ((CELLS, C), BF16)] + sums
        ),
        in_specs=[hbm] * 4,
        out_specs=(hbm,) * 7,
        scratch_shapes=[
            pltpu.VMEM((CELLS, C), BF16),
            pltpu.VMEM((CELLS, C), BF16),
            pltpu.VMEM((2, HALF, 128), BF16),
            pltpu.VMEM((2, SMALL, 128), F32),
            pltpu.VMEM((C, HID), F32),
            pltpu.VMEM((HID, C), F32),
            pltpu.VMEM((KSIZE, KSIZE, C), F32),
            pltpu.VMEM((1, C), F32),
            pltpu.VMEM((1, C), F32),
            pltpu.SemaphoreType.DMA((13,)),
            pltpu.SemaphoreType.DMA((11,)),
        ],
        compiler_params=pltpu.CompilerParams(vmem_limit_bytes=56 * 1024 * 1024),
    )(state, grad_fields, wide, small)


def shards(fields, grad_out, block_count, ocean, kernel, ln_gain, w_in, w_out, layer_scale):
    shape = fields.shape
    samples, slot_count, tile_rows, tile_cols, channels = shape
    partials = block_call(
        block_count,
        ocean,
        fields.reshape(CELLS, channels),
        grad_out.reshape(CELLS, channels),
        kernel,
        ln_gain.reshape(1, channels),
        w_in,
        w_out,
        layer_scale.reshape(1, channels),
    )
    norm = (
        samples * lax.axis_size("dp") * slot_count * lax.axis_size("tiles") * tile_rows * tile_cols
    ) ** (-0.5)
    state, grad_fields, kernel_sum, gain_sum, w_in_sum, w_out_sum, scale_sum = results_call(norm, *partials)
    return (
        state.reshape(shape),
        grad_fields.reshape(shape),
        kernel_sum,
        gain_sum.reshape(channels),
        w_in_sum,
        w_out_sum,
        scale_sum.reshape(channels),
    )


def solution(mesh):
    placed = (
        P("dp", "tiles", None, None, None),
        P("dp", "tiles", None, None, None),
        P("tiles"),
        P("tiles"),
        P(),
        P(),
        P(),
        P(),
        P(),
    )
    return jax.shard_map(
        shards,
        mesh=mesh,
        in_specs=placed,
        out_specs=(
            P("dp", "tiles", None, None, None),
            P("dp", "tiles", None, None, None),
            P(),
            P(),
            P(),
            P(),
            P(),
        ),
        check_vma=False,
    )
```

```python
import functools

import jax
import jax.numpy as jnp
from jax import lax
from jax.experimental import pallas as pl
from jax.experimental.pallas import tpu as pltpu
from jax.sharding import PartitionSpec as P

HID = 1024
KSIZE = 7
NX, NZ, NYH = 4, 8, 4
NY = 2 * NYH
HALF = 2048
SMALL = 64
QUARTER = HALF // 4
PR, QR = QUARTER // (NX * NY), QUARTER // (NX * NZ)
SR = SMALL // NY
F32, BF16 = jnp.float32, jnp.bfloat16


class Place:
    def __init__(self):
        t = lax.axis_index("tiles")
        self.t = t
        self.lo = lax.axis_index("dp")
        self.core = t % 2
        self.yh = (t // 2) % NYH
        self.z = (t // (2 * NYH)) % NZ
        self.x = t // (2 * NYH * NZ)
        self.y = self.yh * 2 + self.lo

    def device(self, core, x, y, z):
        return (((x * NZ + z) * NYH + y // 2) * 2 + core, y % 2)

    def along(self, axis, step):
        if axis == "core":
            place = 1 - self.core
            return place, (self.t + place - self.core, self.lo)
        if axis == "x":
            place = (self.x + step) % NX
            return place, (self.t + (place - self.x) * (2 * NYH * NZ), self.lo)
        if axis == "z":
            place = (self.z + step) % NZ
            return place, (self.t + (place - self.z) * (2 * NYH), self.lo)
        place = (self.y + step) % NY
        return place, (self.t + (place // 2 - self.yh) * 2, place % 2)


COUNT = {"x": NX, "y": NY, "z": NZ, "core": 2}


def steps(axis):
    n = COUNT[axis]
    near = []
    for d in range(1, n // 2 + 1):
        near += [d, n - d] if d != n - d else [d]
    return near


def offsets(*sizes):
    found = [()]
    for n in sizes:
        found = [step + (d,) for step in found for d in range(n)]
    far = lambda step: -sum(min(d, n - d) for d, n in zip(step, sizes))
    return sorted((step for step in found if any(step)), key=far)


def send(src, dst, send_sem, recv_sem, device):
    pltpu.make_async_remote_copy(
        src_ref=src,
        dst_ref=dst,
        send_sem=send_sem,
        recv_sem=recv_sem,
        device_id=device,
        device_id_type=pl.DeviceIdType.MESH,
    ).start()


def await_bytes(like, sem):
    pltpu.make_async_copy(like, like, sem).wait()


def rows(start, size):
    if isinstance(start, int):
        return pl.ds(start, size)
    return pl.ds(pl.multiple_of(start, size), size)


EPS = 1e-06
C = 256
TILE = 16
SLOTS = 3
CELLS = SLOTS * TILE * TILE
WIDE = 64
LEFT = 8
EDGE = KSIZE // 2
BAND = (TILE + 2 * EDGE) * WIDE
GELU_A = 0.7978845608028654
GELU_B = 0.044715


def halo_places(here):
    count = 2 * NX * NZ * NYH
    half = count // 2

    def swap(i):
        return i + (i // half) * (count + half - 1 - 2 * i)

    rank = swap(here.t)
    west = swap((rank + count - 1) % count)
    east = swap((rank + 1) % count)
    across = (here.t + half) % count
    across_west = (west + half) % count
    across_east = (east + half) % count
    return west, east, across, across_west, across_east


class Halo:
    def __init__(self, here, band, edges, top, got, got_top, ss, rs):
        self.here, self.band, self.edges, self.top = here, band, edges, top
        self.got, self.got_top, self.ss, self.rs = got, got_top, ss, rs
        self.west, self.east, self.across, self.across_west, self.across_east = halo_places(here)

    def gather_edges(self, owned):
        for h in range(2):
            lanes = pl.ds(h * 128, 128)
            for j in range(EDGE):
                start = EDGE * WIDE + LEFT + j
                left = self.band[h, pl.ds(start, TILE, WIDE), :]
                self.edges[0, j, :, lanes] = left.astype(BF16)
                ends = [
                    self.band[h, pl.ds(start + TILE * n - EDGE, TILE, WIDE), :]
                    for n in range(1, SLOTS + 1)
                ]
                right = jnp.where(owned == 1, ends[0], jnp.where(owned == 2, ends[1], ends[2]))
                self.edges[1, j, :, lanes] = right.astype(BF16)
            for k in range(EDGE):
                row = self.band[
                    h, pl.ds((TILE + k) * WIDE + LEFT, SLOTS * TILE), :
                ]
                self.top[k, :, lanes] = row.astype(BF16)

    def start(self):
        lo, ss, rs = self.here.lo, self.ss, self.rs
        left, right = self.edges.at[0], self.edges.at[1]
        send(left, self.got.at[1], ss.at[0], rs.at[1], (self.west, lo))
        send(right, self.got.at[0], ss.at[1], rs.at[0], (self.east, lo))
        send(self.top, self.got_top, ss.at[2], rs.at[2], (self.across, lo))
        for block, landing, i, device in (
            (left, self.got.at[2], 3, self.across_west),
            (right, self.got.at[3], 4, self.across_east),
        ):

            @pl.when(device != self.here.t)
            def _():
                send(block, landing, ss.at[i], rs.at[i], (device, lo))

            @pl.when(device == self.here.t)
            def _():
                pltpu.make_async_copy(block, landing, rs.at[i]).start()

    def finish(self, owned):
        edge = self.edges.at[0]
        await_bytes(edge, self.rs.at[0])
        await_bytes(edge, self.rs.at[1])
        for h in range(2):
            lanes = pl.ds(h * 128, 128)
            for j in range(EDGE):
                start = EDGE * WIDE + LEFT + j
                self.band[h, pl.ds(start - EDGE, TILE, WIDE), :] = self.got[0, j, :, lanes].astype(F32)
                east = self.got[1, j, :, lanes].astype(F32)
                for n in range(1, SLOTS):
                    spot = pl.ds(start + TILE * n, TILE, WIDE)
                    self.band[h, spot, :] = jnp.where(owned == n, east, self.band[h, spot, :])
                self.band[h, pl.ds(start + TILE * SLOTS, TILE, WIDE), :] = east
        await_bytes(self.top, self.rs.at[2])
        await_bytes(edge, self.rs.at[3])
        await_bytes(edge, self.rs.at[4])
        used = owned * TILE
        span = SLOTS * TILE
        spot = lax.broadcasted_iota(jnp.int32, (WIDE, 3 * span), 0) - LEFT
        item = lax.broadcasted_iota(jnp.int32, (WIDE, 3 * span), 1)
        inner = jnp.logical_and(jnp.logical_and(spot >= 0, spot < used), item == used - 1 - spot)
        for k in range(1, EDGE + 1):
            row = TILE - k
            west = jnp.logical_and(spot < 0, item == span + (-1 - spot) * TILE + row)
            west = jnp.logical_and(west, spot >= -EDGE)
            past = spot - used
            east = jnp.logical_and(past >= 0, item == 2 * span + (EDGE - 1 - past) * TILE + row)
            east = jnp.logical_and(east, past < EDGE)
            chosen = jnp.logical_or(inner, jnp.logical_or(west, east))
            pick = jnp.where(chosen, 1.0, 0.0).astype(BF16)
            source = jnp.concatenate(
                [
                    self.got_top[EDGE - k],
                    self.got[2].reshape(EDGE * TILE, C),
                    self.got[3].reshape(EDGE * TILE, C),
                ],
                axis=0,
            )
            fold = jnp.dot(pick, source, preferred_element_type=F32)
            place = pl.ds((EDGE + TILE - 1 + k) * WIDE, WIDE)
            self.band[0, place, :] = fold[:, :128]
            self.band[1, place, :] = fold[:, 128:]

    def drain(self):
        edge = self.edges.at[0]
        await_bytes(edge, self.ss.at[0])
        await_bytes(edge, self.ss.at[1])
        await_bytes(self.top, self.ss.at[2])
        for i, device in ((3, self.across_west), (4, self.across_east)):

            @pl.when(device != self.here.t)
            def _():
                await_bytes(edge, self.ss.at[i])


BLOCKS = SLOTS * TILE // 8


def block_start(block):
    return (block // 2) * (TILE * TILE) + (block % 2) * 8


def stencil(band, taps, h, block, backward, last):
    base = LEFT - EDGE + block * 8
    total = [None] * TILE
    for b in range(KSIZE):
        straight = [taps[h, pl.ds(a * KSIZE + b, 1), :] for a in range(KSIZE)]
        turned = straight
        if backward:
            turned = [
                taps[h, pl.ds((KSIZE - 1 - a) * KSIZE + KSIZE - 1 - b, 1), :] for a in range(KSIZE)
            ]
        for row in range(EDGE, last):
            window = band[h, pl.ds(row * WIDE + base + b, 8), :]
            used = straight if row >= TILE + EDGE else turned
            for a in range(KSIZE):
                r = row - a
                if 0 <= r < TILE:
                    term = used[a] * window
                    total[r] = term if total[r] is None else total[r] + term
    return total


def total(first, landing):
    for k in range(landing.shape[0]):
        first = first + landing[k].astype(F32)
    return first


def line_total(landing):
    run = landing[0].astype(F32)
    for k in range(1, landing.shape[0]):
        run = run + landing[k].astype(F32)
    return run


class Reducer:
    def __init__(self, here, refs, ss, rs):
        self.here, self.ss, self.rs = here, ss, rs
        (
            self.wide, self.small, self.out, self.small_out, self.core_out, self.core_in, self.held, self.p_in,
            self.q_in, self.zz, self.yy, self.s_in, self.s_sum,
        ) = refs
        c, x, y, z = here.core, here.x, here.y, here.z
        self.partner = here.device(1 - c, x, y, z)
        self.quarters = tuple(
            (PR, x * NY + y, self.p_in, self.zz, z, "z") if k % 2 == 0 else (QR, x * NZ + z, self.q_in, self.yy, y, "y")
            for k in range(4)
        )

    def plane(self, side):
        c, x, y, z = self.here.core, self.here.x, self.here.y, self.here.z
        n = NZ if side else NY
        for dx, d in offsets(NX, n):
            px = (x + dx) % NX
            if side:
                pz = (z + d) % NZ
                yield self.here.device(c, px, y, pz), px * NZ + pz, dx * n + d - 1
            else:
                py = (y + d) % NY
                yield self.here.device(c, px, py, z), px * NY + py, dx * n + d - 1

    def core(self, k):
        span = rows(k * QUARTER, QUARTER)
        self.core_out[span] = self.wide[1 - self.here.core, span].astype(BF16)
        send(self.core_out.at[span], self.core_in.at[span], self.ss.at[k], self.rs.at[k], self.partner)

    def scatter(self, k):
        size, mine, landing, line, spot, axis = self.quarters[k]
        await_bytes(self.core_in.at[pl.ds(0, QUARTER)], self.rs.at[k])
        span = pl.ds(k * QUARTER, QUARTER)
        self.held[span] = (self.wide[self.here.core, span] + self.core_in[span].astype(F32)).astype(BF16)
        for device, place, slot in self.plane(k % 2):
            send(
                self.held.at[rows(k * QUARTER + place * size, size)], landing.at[k // 2, slot], self.ss.at[4 + k],
                self.rs.at[4 + k], device,
            )

    def line(self, k):
        size, mine, landing, line, spot, axis = self.quarters[k]
        await_bytes(landing.at[k // 2], self.rs.at[4 + k])
        span = rows(k * QUARTER + mine * size, size)
        own = self.wide[self.here.core, span] + self.core_in[span].astype(F32)
        line[k // 2, spot] = total(own, landing.at[k // 2]).astype(BF16)
        ref = line.at[k // 2, spot]
        for d in steps(axis)[::-1]:
            send(ref, ref, self.ss.at[8 + k], self.rs.at[8 + k], self.here.along(axis, d)[1])

    def gather(self, k):
        size, mine, landing, line, spot, axis = self.quarters[k]
        await_bytes(line.at[0, pl.ds(0, line.shape[1] - 1)], self.rs.at[8 + k])
        span = rows(k * QUARTER + mine * size, size)
        self.out[self.here.core, span] = line_total(line.at[k // 2]).astype(BF16)
        ref = self.out.at[self.here.core, span]
        for device, place, slot in self.plane(k % 2):
            send(ref, ref, self.ss.at[12 + k], self.rs.at[12 + k], device)

    def core_back(self, k):
        size = self.quarters[k][0]
        await_bytes(self.bytes_of(QUARTER - size), self.rs.at[12 + k])
        ref = self.out.at[self.here.core, pl.ds(k * QUARTER, QUARTER)]
        send(ref, ref, self.ss.at[16 + k], self.rs.at[16 + k], self.partner)

    def core_done(self, k):
        await_bytes(self.bytes_of(QUARTER), self.rs.at[16 + k])

    def bytes_of(self, count):
        return self.out.at[0, pl.ds(0, count)]

    def small_peers(self):
        c, x, y, z = self.here.core, self.here.x, self.here.y, self.here.z
        for dc, dy in offsets(2, NY):
            pc, py = (c + dc) % 2, (y + dy) % NY
            yield self.here.device(pc, x, py, z), pc, py, dc * NY + dy - 1

    def small_scatter(self):
        for device, pc, py, slot in self.small_peers():
            send(
                self.small.at[pc, rows(py * SR, SR)], self.s_in.at[slot], self.ss.at[20], self.rs.at[20], device
            )

    def small_plane(self):
        c, x, y, z = self.here.core, self.here.x, self.here.y, self.here.z
        await_bytes(self.s_in, self.rs.at[20])
        mine = x * NZ + z
        self.s_sum[mine] = total(self.small[c, rows(y * SR, SR)], self.s_in)
        for device, place, slot in self.plane(1):
            send(self.s_sum.at[mine], self.s_sum.at[mine], self.ss.at[21], self.rs.at[21], device)

    def small_gather(self):
        await_bytes(self.s_sum.at[pl.ds(0, NX * NZ - 1)], self.rs.at[21])
        place = rows(self.here.y * SR, SR)
        self.small_out[self.here.core, place] = line_total(self.s_sum)
        ref = self.small_out.at[self.here.core, place]
        for device, pc, py, slot in self.small_peers():
            send(ref, ref, self.ss.at[22], self.rs.at[22], device)

    def small_done(self):
        await_bytes(self.s_in, self.rs.at[22])

    def drain(self):
        ss = self.ss
        for k in range(4):
            size, mine, landing, line, spot, axis = self.quarters[k]
            await_bytes(self.core_out.at[pl.ds(0, QUARTER)], ss.at[k])
            await_bytes(landing.at[k // 2], ss.at[4 + k])
            await_bytes(line.at[0, pl.ds(0, line.shape[1] - 1)], ss.at[8 + k])
            await_bytes(self.bytes_of(QUARTER - size), ss.at[12 + k])
            await_bytes(self.bytes_of(QUARTER), ss.at[16 + k])
        await_bytes(self.s_in, ss.at[20])
        await_bytes(self.s_sum.at[pl.ds(0, NX * NZ - 1)], ss.at[21])
        await_bytes(self.s_in, ss.at[22])


def greet(here):
    barrier = pltpu.get_barrier_semaphore()
    c, x, y, z = here.core, here.x, here.y, here.z
    west, east, across, across_west, across_east = halo_places(here)
    peers = [(device, here.lo) for device in (west, east, across)]
    for dx, dy in offsets(NX, NY):
        peers.append(here.device(c, (x + dx) % NX, (y + dy) % NY, z))
    for dx, dz in offsets(NX, NZ):
        if dz:
            peers.append(here.device(c, (x + dx) % NX, y, (z + dz) % NZ))
    for dy in range(NY):
        peers.append(here.device(1 - c, x, (y + dy) % NY, z))
    for device in peers:
        pl.semaphore_signal(barrier, inc=1, device_id=device, device_id_type=pl.DeviceIdType.MESH)
    for device in (across_west, across_east):

        @pl.when(device != here.t)
        def _():
            pl.semaphore_signal(
                barrier, inc=1, device_id=(device, here.lo), device_id_type=pl.DeviceIdType.MESH
            )

    return barrier, len(peers), (across_west, across_east)


def block_kernel(
    owned_ref, ocean_ref, fields_hbm, grad_hbm, kernel_hbm, gain_hbm, w_in_hbm, w_out_hbm, scale_hbm,
    state_hbm, grad_fields_hbm, wide_hbm, small_hbm,
    fields, grad_out, kernel, ln_gain, layer_scale, band, gband, taps, conv, inverse, normed, dproj, activated, dpreact, projected, dnormed, rowsum, weight_in,
    weight_out, edges, top, got, got_top, edges2, top2, got2, got_top2, small,
    wide, core_out, core_in, held, p_in, q_in, zz, yy, s_in, s_sum, state, grad_fields, wide_out, small_out,
    ss, rs, hs, hr, hs2, hr2, ls, os
):
    here = Place()
    barrier, greeted, maybe = greet(here)
    loads = [
        pltpu.make_async_copy(source, target, ls.at[i])
        for i, (source, target) in enumerate(
            (
                (fields_hbm, fields), (kernel_hbm, kernel), (gain_hbm, ln_gain), (scale_hbm, layer_scale),
                (grad_hbm, grad_out), (w_in_hbm, weight_in), (w_out_hbm, weight_out),
            )
        )
    ]
    for load in loads:
        load.start()
    reducer = Reducer(
        here,
        (
            wide, small, wide_out, small_out, core_out, core_in, held, p_in, q_in, zz, yy, s_in, s_sum,
        ),
        ss,
        rs,
    )
    owned = owned_ref[0]

    def slot_mask(slot):
        live = jnp.logical_and(slot < owned, ocean_ref[slot] > 0)
        return jnp.where(live, 1.0, 0.0).astype(F32)

    def clear(i, carry):
        spot = rows(i * 64, 64)
        for h in range(2):
            band[h, spot, :] = jnp.zeros((64, 128), F32)
            gband[h, spot, :] = jnp.zeros((64, 128), F32)
        return carry

    lax.fori_loop(0, BAND // 64, clear, 0)
    small[...] = jnp.zeros_like(small)
    rowsum[...] = jnp.zeros_like(rowsum)
    loads[0].wait()
    loads[1].wait()
    for a in range(KSIZE):
        line = kernel[a].astype(F32)
        for h in range(2):
            taps[h, a * KSIZE : (a + 1) * KSIZE, :] = line[:, h * 128 : (h + 1) * 128]

    def fill(i, carry):
        slot, r = i // TILE, i % TILE
        line = fields[rows(i * TILE, TILE), :].astype(F32) * slot_mask(slot)
        place = pl.ds(pl.multiple_of((EDGE + r) * WIDE + LEFT + slot * TILE, 8), TILE)
        band[0, place, :] = line[:, :128]
        band[1, place, :] = line[:, 128:]
        return carry

    lax.fori_loop(0, SLOTS * TILE, fill, 0, unroll=4)
    halo = Halo(here, band, edges, top, got, got_top, hs, hr)
    halo.gather_edges(owned)
    at_seam = jnp.logical_or(maybe[0] == here.t, maybe[1] == here.t)

    @pl.when(at_seam)
    def _():
        pl.semaphore_wait(barrier, greeted + 1)

    @pl.when(jnp.logical_not(at_seam))
    def _():
        pl.semaphore_wait(barrier, greeted + 2)

    halo.start()

    def convolve(i, carry):
        h, block = i // BLOCKS, i % BLOCKS
        result = stencil(band, taps, h, block, False, TILE + EDGE)
        for r in range(TILE):
            conv[h, pl.ds(pl.multiple_of(block_start(block) + r * TILE, 8), 8), :] = result[r]
        return carry

    lax.fori_loop(0, 2 * BLOCKS, convolve, 0)

    halo.finish(owned)

    def add_fold(i, carry):
        h, block = i // BLOCKS, i % BLOCKS
        base = LEFT - EDGE + block * 8
        sums = [None] * EDGE
        for b in range(KSIZE):
            for row in range(TILE + EDGE, TILE + 2 * EDGE):
                window = band[h, pl.ds(row * WIDE + base + b, 8), :]
                for a in range(row - TILE + 1, KSIZE):
                    term = taps[h, pl.ds(a * KSIZE + b, 1), :] * window
                    r = row - a - TILE + EDGE
                    sums[r] = term if sums[r] is None else sums[r] + term
        for r in range(EDGE):
            place = pl.ds(pl.multiple_of(block_start(block) + (TILE - EDGE + r) * TILE, 8), 8)
            conv[h, place, :] = conv[h, place, :] + sums[r]
        return carry

    lax.fori_loop(0, 2 * BLOCKS, add_fold, 0, unroll=3)
    sub = lax.broadcasted_iota(jnp.int32, (8, 128), 0)

    def edge_sums(h, base, shifts, held):
        sums = [None] * TILE
        for b in shifts:
            weights = [taps[h, pl.ds(a * KSIZE + b, 1), :] for a in range(KSIZE)]
            for row in range(EDGE, TILE + EDGE):
                window = jnp.where(held(b), band[h, pl.ds(row * WIDE + base + b, 8), :], 0.0)
                for a in range(KSIZE):
                    r = row - a
                    if 0 <= r < TILE:
                        term = weights[a] * window
                        sums[r] = term if sums[r] is None else sums[r] + term
        return sums

    def add_edges(h, carry):
        west = edge_sums(h, LEFT - EDGE, range(EDGE), lambda b: sub < EDGE - b)
        for r in range(TILE):
            place = pl.ds(r * TILE, 8)
            conv[h, place, :] = conv[h, place, :] + west[r]
        east = edge_sums(
            h, LEFT - EDGE + owned * TILE - 8, range(EDGE + 1, KSIZE), lambda b: sub >= 8 + EDGE - b
        )
        for n in range(1, SLOTS + 1):
            for r in range(TILE):
                place = pl.ds((n - 1) * TILE * TILE + r * TILE + 8, 8)
                conv[h, place, :] = conv[h, place, :] + jnp.where(owned == n, east[r], 0.0)
        return carry

    lax.fori_loop(0, 2, add_edges, 0, unroll=2)

    for load in loads[2:5]:
        load.wait()
    gain = [ln_gain[:, :128], ln_gain[:, 128:]]
    scale = [layer_scale[:, :128], layer_scale[:, 128:]]
    STEP = 128

    def norm(i, carry):
        span = rows(i * STEP, STEP)
        mask = slot_mask(i // (TILE * TILE // STEP))
        parts = [conv[h, span, :] for h in range(2)]
        mean = jnp.sum(parts[0] + parts[1], axis=1, keepdims=True) * (1.0 / C)
        centred = [part - mean for part in parts]
        variance = jnp.sum(
            centred[0] * centred[0] + centred[1] * centred[1], axis=1, keepdims=True
        ) * (1.0 / C)
        scaled = lax.rsqrt(variance + EPS)
        inverse[span, :] = jnp.broadcast_to(scaled, (STEP, 128))
        for h in range(2):
            lanes = pl.ds(h * 128, 128)
            yhat = centred[h] * scaled
            conv[h, span, :] = yhat
            normed[span, lanes] = (yhat * gain[h]).astype(BF16)
            cotangent = grad_out[span, lanes].astype(F32)
            dproj[span, lanes] = (mask * scale[h] * cotangent).astype(BF16)
        return carry

    lax.fori_loop(0, CELLS // STEP, norm, 0, unroll=2)
    loads[5].wait()
    loads[6].wait()
    across_rows = (((0,), (0,)), ((), ()))
    across_cols = (((1,), (1,)), ((), ()))

    def quarter(k, carry):
        hidden = rows(k * 256, 256)
        part_in = weight_in[:, hidden]
        part_out = weight_out[rows(k * 256, 256), :]
        for m in range(SLOTS):
            span = pl.ds(m * 256, 256)
            cells, slopes = normed[span, :], dproj[span, :]
            v = jnp.dot(cells, part_in, preferred_element_type=F32)
            dact = lax.dot_general(slopes, part_out, across_cols, preferred_element_type=F32)
            square = v * v
            t = jnp.tanh(v * (GELU_A + (GELU_A * GELU_B) * square))
            half = 0.5 + 0.5 * t
            act = (v * half).astype(BF16)
            slope = half + (v * half) * (1.0 - t) * (GELU_A + (3.0 * GELU_A * GELU_B) * square)
            dpre = (dact * slope).astype(BF16)
            activated[span, hidden] = act
            dpreact[span, hidden] = dpre
        grad_o = lax.dot_general(
            activated[:, hidden], dproj[...], across_rows, preferred_element_type=F32
        )
        grad_i = lax.dot_general(
            normed[...], dpreact[:, hidden], across_rows, preferred_element_type=F32
        )
        for h in range(2):
            spot = rows(k * 512 + h * 256, 256)
            wide[0, spot, :] = grad_i[:, h * 128 : (h + 1) * 128]
            wide[1, spot, :] = grad_o[:, h * 128 : (h + 1) * 128]
        reducer.core(k)

        if k >= 2:
            reducer.scatter(k - 2)

        return carry

    for k in range(HID // 256):
        quarter(k, 0)
    for m in range(SLOTS):
        span = pl.ds(m * 256, 256)
        dnormed[span, :] = lax.dot_general(
            dpreact[span, :], weight_in[...], across_cols, preferred_element_type=F32
        )

    reducer.scatter(2)

    def norm_back(i, carry):
        span = rows(i * STEP, STEP)
        slot, r = i // (TILE * TILE // STEP), (i % (TILE * TILE // STEP)) * (STEP // TILE)
        lanes = [pl.ds(h * 128, 128) for h in range(2)]
        back = [dnormed[span, lanes[h]] for h in range(2)]
        yhat = [conv[h, span, :] for h in range(2)]
        for h in range(2):
            rowsum[h] += jnp.sum((back[h] * yhat[h]).reshape(STEP // 8, 8, 128), axis=0)
        dhat = [back[h] * gain[h] for h in range(2)]
        mean = jnp.sum(dhat[0] + dhat[1], axis=1, keepdims=True) * (1.0 / C)
        tilt = jnp.sum(dhat[0] * yhat[0] + dhat[1] * yhat[1], axis=1, keepdims=True) * (1.0 / C)
        for h in range(2):
            grad = inverse[span, :] * (dhat[h] - mean - yhat[h] * tilt)
            grad = grad.astype(BF16).astype(F32)
            for q in range(STEP // TILE):
                place = pl.ds(
                    pl.multiple_of((EDGE + r + q) * WIDE + LEFT + slot * TILE, 8), TILE
                )
                gband[h, place, :] = grad[q * TILE : (q + 1) * TILE]
        return carry

    lax.fori_loop(0, CELLS // STEP, norm_back, 0, unroll=2)
    halo_back = Halo(here, gband, edges2, top2, got2, got_top2, hs2, hr2)
    reducer.scatter(3)
    halo_back.gather_edges(owned)
    halo_back.start()

    for m in range(SLOTS):
        span = pl.ds(m * 256, 256)
        projected[span, :] = jnp.dot(activated[span, :], weight_out[...], preferred_element_type=F32)

    def finish_state(i, carry):
        span = rows(i * STEP, STEP)
        mask = slot_mask(i // (TILE * TILE // STEP))
        for h in range(2):
            lanes = pl.ds(h * 128, 128)
            out = projected[span, lanes]
            rowsum[2 + h] += jnp.sum(
                (mask * grad_out[span, lanes].astype(F32) * out).reshape(STEP // 8, 8, 128), axis=0
            )
            kept = fields[span, lanes].astype(F32)
            state[span, lanes] = (mask * (kept + scale[h] * out)).astype(BF16)
        return carry

    lax.fori_loop(0, CELLS // STEP, finish_state, 0, unroll=2)
    write_state = pltpu.make_async_copy(state, state_hbm, os.at[0])
    write_state.start()

    def kernel_grad(i, carry):
        h, b = i // KSIZE, i % KSIZE

        def one_block(block, sums):
            sums = list(sums)
            base = LEFT + block * 8
            cots = [gband[h, pl.ds(pl.multiple_of((EDGE + r) * WIDE + base, 8), 8), :] for r in range(TILE)]
            for row in range(EDGE, TILE + 2 * EDGE):
                window = band[h, pl.ds(row * WIDE + base - EDGE + b, 8), :]
                for a in range(KSIZE):
                    if 0 <= row - a < TILE:
                        sums[a] = sums[a] + cots[row - a] * window
            return tuple(sums)

        zero = tuple(jnp.zeros((8, 128), F32) for a in range(KSIZE))
        sums = lax.fori_loop(0, BLOCKS, one_block, zero, unroll=3)
        for a in range(KSIZE):
            small[h, pl.ds(a * KSIZE + b, 1), :] = jnp.sum(sums[a], axis=0, keepdims=True)
        return carry

    lax.fori_loop(0, 2 * KSIZE, kernel_grad, 0)
    for h in range(2):
        small[h, KSIZE * KSIZE : KSIZE * KSIZE + 1, :] = jnp.sum(rowsum[h], axis=0, keepdims=True)
        small[h, KSIZE * KSIZE + 1 : KSIZE * KSIZE + 2, :] = jnp.sum(rowsum[2 + h], axis=0, keepdims=True)
    reducer.small_scatter()
    for k in range(3):
        reducer.line(k)
    halo_back.finish(owned)

    def convolve_back(i, carry):
        h, block = i % 2, i // 2
        result = stencil(gband, taps, h, block, True, TILE + 2 * EDGE)
        for r in range(TILE):
            conv[h, pl.ds(pl.multiple_of(block_start(block) + r * TILE, 8), 8), :] = result[r]
        return carry

    def finish_grad(i, carry):
        span = rows(i * STEP, STEP)
        mask = slot_mask(i // (TILE * TILE // STEP))
        for h in range(2):
            lanes = pl.ds(h * 128, 128)
            grad = mask * (grad_out[span, lanes].astype(F32) + conv[h, span, :])
            grad_fields[span, lanes] = grad.astype(BF16)
        return carry

    lax.fori_loop(0, 2, convolve_back, 0)
    reducer.line(3)
    lax.fori_loop(2, 2 * BLOCKS, convolve_back, 0)
    reducer.small_plane()
    for k in range(4):
        reducer.gather(k)
    lax.fori_loop(0, CELLS // STEP, finish_grad, 0)
    write_grad = pltpu.make_async_copy(grad_fields, grad_fields_hbm, os.at[1])
    write_grad.start()
    reducer.small_gather()
    writes = [write_state, write_grad]
    for k in range(4):
        reducer.core_back(k)
        span = pl.ds(k * QUARTER, QUARTER)
        writes.append(
            pltpu.make_async_copy(wide_out.at[here.core, span], wide_hbm.at[here.core, span], os.at[2 + k])
        )
        writes[-1].start()
    for k in range(4):
        reducer.core_done(k)
        span = pl.ds(k * QUARTER, QUARTER)
        writes.append(
            pltpu.make_async_copy(
                wide_out.at[1 - here.core, span], wide_hbm.at[1 - here.core, span], os.at[7 + k]
            )
        )
        writes[-1].start()
    reducer.small_done()
    writes.append(pltpu.make_async_copy(small_out, small_hbm, os.at[6]))
    writes[-1].start()
    reducer.drain()
    halo.drain()
    halo_back.drain()
    for write in writes:
        write.wait()


def block_call(block_count, ocean, fields, grad_out, kernel, ln_gain, w_in, w_out, layer_scale):
    vmem = pl.BlockSpec(memory_space=pltpu.VMEM)
    smem = pl.BlockSpec(memory_space=pltpu.SMEM)
    hbm = pl.BlockSpec(memory_space=pl.ANY)
    edges = pltpu.VMEM((2, EDGE, TILE, C), BF16)
    top = pltpu.VMEM((EDGE, SLOTS * TILE, C), BF16)
    got = pltpu.VMEM((4, EDGE, TILE, C), BF16)
    scratch = [
        pltpu.VMEM((CELLS, C), BF16),
        pltpu.VMEM((CELLS, C), BF16),
        pltpu.VMEM((KSIZE, KSIZE, C), BF16),
        pltpu.VMEM((1, C), F32),
        pltpu.VMEM((1, C), F32),
        pltpu.VMEM((2, BAND, 128), F32),
        pltpu.VMEM((2, BAND, 128), F32),
        pltpu.VMEM((2, 56, 128), F32),
        pltpu.VMEM((2, CELLS, 128), F32),
        pltpu.VMEM((CELLS, 128), F32),
        pltpu.VMEM((CELLS, C), BF16),
        pltpu.VMEM((CELLS, C), BF16),
        pltpu.VMEM((CELLS, HID), BF16),
        pltpu.VMEM((CELLS, HID), BF16),
        pltpu.VMEM((CELLS, C), F32),
        pltpu.VMEM((CELLS, C), F32),
        pltpu.VMEM((4, 8, 128), F32),
        pltpu.VMEM((C, HID), BF16),
        pltpu.VMEM((HID, C), BF16),
        edges, top, got, top, edges, top, got, top,
        pltpu.VMEM((2, SMALL, 128), F32),
        pltpu.VMEM((2, HALF, 128), F32),
        pltpu.VMEM((HALF, 128), BF16),
        pltpu.VMEM((HALF, 128), BF16),
        pltpu.VMEM((HALF, 128), BF16),
        pltpu.VMEM((2, NX * NY - 1, PR, 128), BF16),
        pltpu.VMEM((2, NX * NZ - 1, QR, 128), BF16),
        pltpu.VMEM((2, NZ, PR, 128), BF16),
        pltpu.VMEM((2, NY, QR, 128), BF16),
        pltpu.VMEM((2 * NY - 1, SR, 128), F32),
        pltpu.VMEM((NX * NZ, SR, 128), F32),
        pltpu.VMEM((CELLS, C), BF16),
        pltpu.VMEM((CELLS, C), BF16),
        pltpu.VMEM((2, HALF, 128), BF16),
        pltpu.VMEM((2, SMALL, 128), F32),
        pltpu.SemaphoreType.DMA((23,)),
        pltpu.SemaphoreType.DMA((23,)),
        pltpu.SemaphoreType.DMA((5,)),
        pltpu.SemaphoreType.DMA((5,)),
        pltpu.SemaphoreType.DMA((5,)),
        pltpu.SemaphoreType.DMA((5,)),
        pltpu.SemaphoreType.DMA((7,)),
        pltpu.SemaphoreType.DMA((11,)),
    ]
    return pl.pallas_call(
        block_kernel,
        out_shape=(
            jax.ShapeDtypeStruct((CELLS, C), BF16),
            jax.ShapeDtypeStruct((CELLS, C), BF16),
            jax.ShapeDtypeStruct((2, HALF, 128), BF16),
            jax.ShapeDtypeStruct((2, SMALL, 128), F32),
        ),
        in_specs=[smem, smem] + [hbm] * 7,
        out_specs=(hbm,) * 4,
        scratch_shapes=scratch,
        compiler_params=pltpu.CompilerParams(
            collective_id=1, has_side_effects=True, vmem_limit_bytes=56 * 1024 * 1024
        ),
    )(block_count, ocean, fields, grad_out, kernel, ln_gain, w_in, w_out, layer_scale)


def results_kernel(
    norm, state_hbm, fields_hbm, wide_hbm, small_hbm, state_out, fields_out, kernel_out, gain_out, in_out, out_out,
    scale_out, state, grad_fields, wide, small, grad_in, grad_out, grad_kernel, grad_gain, grad_scale, sems, loads
):
    copies = [
        pltpu.make_async_copy(state, state_out, sems.at[0]),
        pltpu.make_async_copy(grad_fields, fields_out, sems.at[1]),
    ]
    through = [
        pltpu.make_async_copy(state_hbm, state, loads.at[9]),
        pltpu.make_async_copy(fields_hbm, grad_fields, loads.at[10]),
    ]
    fetches = [pltpu.make_async_copy(small_hbm, small, loads.at[8])]
    for k in range(4):
        for side in range(2):
            span = pl.ds(k * QUARTER, QUARTER)
            fetches.append(
                pltpu.make_async_copy(
                    wide_hbm.at[side, span], wide.at[side, span], loads.at[2 * k + side]
                )
            )
    for copy in through + fetches:
        copy.start()
    for fetch, copy in zip(through, copies):
        fetch.wait()
        copy.start()
    fetches[0].wait()
    count = KSIZE * KSIZE
    for h in range(2):
        lanes = pl.ds(h * 128, 128)
        for a in range(KSIZE):
            grad_kernel[a, :, lanes] = small[h, pl.ds(a * KSIZE, KSIZE), :] * norm
        grad_gain[:, lanes] = small[h, pl.ds(count, 1), :] * norm
        grad_scale[:, lanes] = small[h, pl.ds(count + 1, 1), :] * norm
    for i, (source, target) in enumerate(
        ((grad_kernel, kernel_out), (grad_gain, gain_out), (grad_scale, scale_out))
    ):
        copies.append(pltpu.make_async_copy(source, target, sems.at[2 + i]))
        copies[-1].start()
    for k in range(4):
        for side in range(2):
            fetches[1 + 2 * k + side].wait()
            for h in range(2):
                part = wide[side, pl.ds(k * 512 + h * 256, 256), :].astype(F32) * norm
                if side:
                    grad_out[pl.ds(k * 256, 256), pl.ds(h * 128, 128)] = part
                else:
                    grad_in[:, pl.ds(k * 256 + h * 128, 128)] = part
            if side:
                spot = (pl.ds(k * 256, 256), slice(None))
                source, target = grad_out, out_out
            else:
                spot = (slice(None), pl.ds(k * 256, 256))
                source, target = grad_in, in_out
            copies.append(
                pltpu.make_async_copy(source.at[spot], target.at[spot], sems.at[5 + 2 * k + side])
            )
            copies[-1].start()
    for copy in copies:
        copy.wait()


def results_call(norm, state, grad_fields, wide, small):
    hbm = pl.BlockSpec(memory_space=pl.ANY)
    sums = [((KSIZE, KSIZE, C), F32), ((1, C), F32), ((C, HID), F32), ((HID, C), F32), ((1, C), F32)]
    return pl.pallas_call(
        functools.partial(results_kernel, norm),
        out_shape=tuple(
            jax.ShapeDtypeStruct(*spec) for spec in [((CELLS, C), BF16), ((CELLS, C), BF16)] + sums
        ),
        in_specs=[hbm] * 4,
        out_specs=(hbm,) * 7,
        scratch_shapes=[
            pltpu.VMEM((CELLS, C), BF16),
            pltpu.VMEM((CELLS, C), BF16),
            pltpu.VMEM((2, HALF, 128), BF16),
            pltpu.VMEM((2, SMALL, 128), F32),
            pltpu.VMEM((C, HID), F32),
            pltpu.VMEM((HID, C), F32),
            pltpu.VMEM((KSIZE, KSIZE, C), F32),
            pltpu.VMEM((1, C), F32),
            pltpu.VMEM((1, C), F32),
            pltpu.SemaphoreType.DMA((13,)),
            pltpu.SemaphoreType.DMA((11,)),
        ],
        compiler_params=pltpu.CompilerParams(vmem_limit_bytes=56 * 1024 * 1024),
    )(state, grad_fields, wide, small)


def shards(fields, grad_out, block_count, ocean, kernel, ln_gain, w_in, w_out, layer_scale):
    shape = fields.shape
    samples, slot_count, tile_rows, tile_cols, channels = shape
    partials = block_call(
        block_count,
        ocean,
        fields.reshape(CELLS, channels),
        grad_out.reshape(CELLS, channels),
        kernel,
        ln_gain.reshape(1, channels),
        w_in,
        w_out,
        layer_scale.reshape(1, channels),
    )
    norm = (
        samples * lax.axis_size("dp") * slot_count * lax.axis_size("tiles") * tile_rows * tile_cols
    ) ** (-0.5)
    state, grad_fields, kernel_sum, gain_sum, w_in_sum, w_out_sum, scale_sum = results_call(norm, *partials)
    return (
        state.reshape(shape),
        grad_fields.reshape(shape),
        kernel_sum,
        gain_sum.reshape(channels),
        w_in_sum,
        w_out_sum,
        scale_sum.reshape(channels),
    )


def solution(mesh):
    placed = (
        P("dp", "tiles", None, None, None),
        P("dp", "tiles", None, None, None),
        P("tiles"),
        P("tiles"),
        P(),
        P(),
        P(),
        P(),
        P(),
    )
    return jax.shard_map(
        shards,
        mesh=mesh,
        in_specs=placed,
        out_specs=(
            P("dp", "tiles", None, None, None),
            P("dp", "tiles", None, None, None),
            P(),
            P(),
            P(),
            P(),
            P(),
        ),
        check_vma=False,
    )
```

```python
import functools

import jax
import jax.numpy as jnp
from jax import lax
from jax.experimental import pallas as pl
from jax.experimental.pallas import tpu as pltpu
from jax.sharding import PartitionSpec as P

HID = 1024
KSIZE = 7
NX, NZ, NYH = 4, 8, 4
NY = 2 * NYH
HALF = 2048
SMALL = 64
QUARTER = HALF // 4
PR, QR = QUARTER // (NX * NY), QUARTER // (NX * NZ)
SR = SMALL // NY
F32, BF16 = jnp.float32, jnp.bfloat16


class Place:
    def __init__(self):
        t = lax.axis_index("tiles")
        self.t = t
        self.lo = lax.axis_index("dp")
        self.core = t % 2
        self.yh = (t // 2) % NYH
        self.z = (t // (2 * NYH)) % NZ
        self.x = t // (2 * NYH * NZ)
        self.y = self.yh * 2 + self.lo

    def device(self, core, x, y, z):
        return (((x * NZ + z) * NYH + y // 2) * 2 + core, y % 2)

    def along(self, axis, step):
        if axis == "core":
            place = 1 - self.core
            return place, (self.t + place - self.core, self.lo)
        if axis == "x":
            place = (self.x + step) % NX
            return place, (self.t + (place - self.x) * (2 * NYH * NZ), self.lo)
        if axis == "z":
            place = (self.z + step) % NZ
            return place, (self.t + (place - self.z) * (2 * NYH), self.lo)
        place = (self.y + step) % NY
        return place, (self.t + (place // 2 - self.yh) * 2, place % 2)


COUNT = {"x": NX, "y": NY, "z": NZ, "core": 2}


def steps(axis):
    n = COUNT[axis]
    near = []
    for d in range(1, n // 2 + 1):
        near += [d, n - d] if d != n - d else [d]
    return near


def offsets(*sizes):
    found = [()]
    for n in sizes:
        found = [step + (d,) for step in found for d in range(n)]
    far = lambda step: -sum(min(d, n - d) for d, n in zip(step, sizes))
    return sorted((step for step in found if any(step)), key=far)


def send(src, dst, send_sem, recv_sem, device):
    pltpu.make_async_remote_copy(
        src_ref=src,
        dst_ref=dst,
        send_sem=send_sem,
        recv_sem=recv_sem,
        device_id=device,
        device_id_type=pl.DeviceIdType.MESH,
    ).start()


def await_bytes(like, sem):
    pltpu.make_async_copy(like, like, sem).wait()


def rows(start, size):
    if isinstance(start, int):
        return pl.ds(start, size)
    return pl.ds(pl.multiple_of(start, size), size)


EPS = 1e-06
C = 256
TILE = 16
SLOTS = 3
CELLS = SLOTS * TILE * TILE
WIDE = 64
LEFT = 8
EDGE = KSIZE // 2
BAND = (TILE + 2 * EDGE) * WIDE
GELU_A = 0.7978845608028654
GELU_B = 0.044715


def halo_places(here):
    count = 2 * NX * NZ * NYH
    half = count // 2

    def swap(i):
        return i + (i // half) * (count + half - 1 - 2 * i)

    rank = swap(here.t)
    west = swap((rank + count - 1) % count)
    east = swap((rank + 1) % count)
    across = (here.t + half) % count
    across_west = (west + half) % count
    across_east = (east + half) % count
    return west, east, across, across_west, across_east


class Halo:
    def __init__(self, here, band, edges, top, got, got_top, ss, rs):
        self.here, self.band, self.edges, self.top = here, band, edges, top
        self.got, self.got_top, self.ss, self.rs = got, got_top, ss, rs
        self.west, self.east, self.across, self.across_west, self.across_east = halo_places(here)

    def gather_edges(self, owned):
        for h in range(2):
            lanes = pl.ds(h * 128, 128)
            for j in range(EDGE):
                start = EDGE * WIDE + LEFT + j
                left = self.band[h, pl.ds(start, TILE, WIDE), :]
                self.edges[0, j, :, lanes] = left.astype(BF16)
                ends = [
                    self.band[h, pl.ds(start + TILE * n - EDGE, TILE, WIDE), :]
                    for n in range(1, SLOTS + 1)
                ]
                right = jnp.where(owned == 1, ends[0], jnp.where(owned == 2, ends[1], ends[2]))
                self.edges[1, j, :, lanes] = right.astype(BF16)
            for k in range(EDGE):
                row = self.band[
                    h, pl.ds((TILE + k) * WIDE + LEFT, SLOTS * TILE), :
                ]
                self.top[k, :, lanes] = row.astype(BF16)

    def start(self):
        lo, ss, rs = self.here.lo, self.ss, self.rs
        left, right = self.edges.at[0], self.edges.at[1]
        send(left, self.got.at[1], ss.at[0], rs.at[1], (self.west, lo))
        send(right, self.got.at[0], ss.at[1], rs.at[0], (self.east, lo))
        send(self.top, self.got_top, ss.at[2], rs.at[2], (self.across, lo))
        for block, landing, i, device in (
            (left, self.got.at[2], 3, self.across_west),
            (right, self.got.at[3], 4, self.across_east),
        ):

            @pl.when(device != self.here.t)
            def _():
                send(block, landing, ss.at[i], rs.at[i], (device, lo))

            @pl.when(device == self.here.t)
            def _():
                pltpu.make_async_copy(block, landing, rs.at[i]).start()

    def finish(self, owned):
        edge = self.edges.at[0]
        await_bytes(edge, self.rs.at[0])
        await_bytes(edge, self.rs.at[1])
        for h in range(2):
            lanes = pl.ds(h * 128, 128)
            for j in range(EDGE):
                start = EDGE * WIDE + LEFT + j
                self.band[h, pl.ds(start - EDGE, TILE, WIDE), :] = self.got[0, j, :, lanes].astype(F32)
                east = self.got[1, j, :, lanes].astype(F32)
                for n in range(1, SLOTS):
                    spot = pl.ds(start + TILE * n, TILE, WIDE)
                    self.band[h, spot, :] = jnp.where(owned == n, east, self.band[h, spot, :])
                self.band[h, pl.ds(start + TILE * SLOTS, TILE, WIDE), :] = east
        await_bytes(self.top, self.rs.at[2])
        await_bytes(edge, self.rs.at[3])
        await_bytes(edge, self.rs.at[4])
        used = owned * TILE
        span = SLOTS * TILE
        spot = lax.broadcasted_iota(jnp.int32, (WIDE, 3 * span), 0) - LEFT
        item = lax.broadcasted_iota(jnp.int32, (WIDE, 3 * span), 1)
        inner = jnp.logical_and(jnp.logical_and(spot >= 0, spot < used), item == used - 1 - spot)
        for k in range(1, EDGE + 1):
            row = TILE - k
            west = jnp.logical_and(spot < 0, item == span + (-1 - spot) * TILE + row)
            west = jnp.logical_and(west, spot >= -EDGE)
            past = spot - used
            east = jnp.logical_and(past >= 0, item == 2 * span + (EDGE - 1 - past) * TILE + row)
            east = jnp.logical_and(east, past < EDGE)
            chosen = jnp.logical_or(inner, jnp.logical_or(west, east))
            pick = jnp.where(chosen, 1.0, 0.0).astype(BF16)
            source = jnp.concatenate(
                [
                    self.got_top[EDGE - k],
                    self.got[2].reshape(EDGE * TILE, C),
                    self.got[3].reshape(EDGE * TILE, C),
                ],
                axis=0,
            )
            fold = jnp.dot(pick, source, preferred_element_type=F32)
            place = pl.ds((EDGE + TILE - 1 + k) * WIDE, WIDE)
            self.band[0, place, :] = fold[:, :128]
            self.band[1, place, :] = fold[:, 128:]

    def drain(self):
        edge = self.edges.at[0]
        await_bytes(edge, self.ss.at[0])
        await_bytes(edge, self.ss.at[1])
        await_bytes(self.top, self.ss.at[2])
        for i, device in ((3, self.across_west), (4, self.across_east)):

            @pl.when(device != self.here.t)
            def _():
                await_bytes(edge, self.ss.at[i])


BLOCKS = SLOTS * TILE // 8


def block_start(block):
    return (block // 2) * (TILE * TILE) + (block % 2) * 8


def stencil(band, taps, h, block, backward, last):
    base = LEFT - EDGE + block * 8
    total = [None] * TILE
    for b in range(KSIZE):
        straight = [taps[h, pl.ds(a * KSIZE + b, 1), :] for a in range(KSIZE)]
        turned = straight
        if backward:
            turned = [
                taps[h, pl.ds((KSIZE - 1 - a) * KSIZE + KSIZE - 1 - b, 1), :] for a in range(KSIZE)
            ]
        for row in range(EDGE, last):
            window = band[h, pl.ds(row * WIDE + base + b, 8), :]
            used = straight if row >= TILE + EDGE else turned
            for a in range(KSIZE):
                r = row - a
                if 0 <= r < TILE:
                    term = used[a] * window
                    total[r] = term if total[r] is None else total[r] + term
    return total


def total(first, landing):
    for k in range(landing.shape[0]):
        first = first + landing[k].astype(F32)
    return first


def line_total(landing):
    run = landing[0].astype(F32)
    for k in range(1, landing.shape[0]):
        run = run + landing[k].astype(F32)
    return run


class Reducer:
    def __init__(self, here, refs, ss, rs):
        self.here, self.ss, self.rs = here, ss, rs
        (
            self.wide, self.small, self.out, self.small_out, self.core_out, self.core_in, self.held, self.p_in,
            self.q_in, self.zz, self.yy, self.s_in, self.s_sum,
        ) = refs
        c, x, y, z = here.core, here.x, here.y, here.z
        self.partner = here.device(1 - c, x, y, z)
        self.quarters = tuple(
            (PR, x * NY + y, self.p_in, self.zz, z, "z") if k % 2 == 0 else (QR, x * NZ + z, self.q_in, self.yy, y, "y")
            for k in range(4)
        )

    def plane(self, side):
        c, x, y, z = self.here.core, self.here.x, self.here.y, self.here.z
        n = NZ if side else NY
        for dx, d in offsets(NX, n):
            px = (x + dx) % NX
            if side:
                pz = (z + d) % NZ
                yield self.here.device(c, px, y, pz), px * NZ + pz, dx * n + d - 1
            else:
                py = (y + d) % NY
                yield self.here.device(c, px, py, z), px * NY + py, dx * n + d - 1

    def core(self, k):
        span = rows(k * QUARTER, QUARTER)
        self.core_out[span] = self.wide[1 - self.here.core, span].astype(BF16)
        send(self.core_out.at[span], self.core_in.at[span], self.ss.at[k], self.rs.at[k], self.partner)

    def scatter(self, k):
        size, mine, landing, line, spot, axis = self.quarters[k]
        await_bytes(self.core_in.at[pl.ds(0, QUARTER)], self.rs.at[k])
        span = pl.ds(k * QUARTER, QUARTER)
        self.held[span] = (self.wide[self.here.core, span] + self.core_in[span].astype(F32)).astype(BF16)
        for device, place, slot in self.plane(k % 2):
            send(
                self.held.at[rows(k * QUARTER + place * size, size)], landing.at[k // 2, slot], self.ss.at[4 + k],
                self.rs.at[4 + k], device,
            )

    def line(self, k):
        size, mine, landing, line, spot, axis = self.quarters[k]
        await_bytes(landing.at[k // 2], self.rs.at[4 + k])
        span = rows(k * QUARTER + mine * size, size)
        own = self.wide[self.here.core, span] + self.core_in[span].astype(F32)
        line[k // 2, spot] = total(own, landing.at[k // 2]).astype(BF16)
        ref = line.at[k // 2, spot]
        for d in steps(axis)[::-1]:
            send(ref, ref, self.ss.at[8 + k], self.rs.at[8 + k], self.here.along(axis, d)[1])

    def gather(self, k):
        size, mine, landing, line, spot, axis = self.quarters[k]
        await_bytes(line.at[0, pl.ds(0, line.shape[1] - 1)], self.rs.at[8 + k])
        span = rows(k * QUARTER + mine * size, size)
        self.out[self.here.core, span] = line_total(line.at[k // 2]).astype(BF16)
        ref = self.out.at[self.here.core, span]
        for device, place, slot in self.plane(k % 2):
            send(ref, ref, self.ss.at[12 + k], self.rs.at[12 + k], device)

    def core_back(self, k):
        size = self.quarters[k][0]
        await_bytes(self.bytes_of(QUARTER - size), self.rs.at[12 + k])
        ref = self.out.at[self.here.core, pl.ds(k * QUARTER, QUARTER)]
        send(ref, ref, self.ss.at[16 + k], self.rs.at[16 + k], self.partner)

    def core_done(self, k):
        await_bytes(self.bytes_of(QUARTER), self.rs.at[16 + k])

    def bytes_of(self, count):
        return self.out.at[0, pl.ds(0, count)]

    def small_peers(self):
        c, x, y, z = self.here.core, self.here.x, self.here.y, self.here.z
        for dc, dy in offsets(2, NY):
            pc, py = (c + dc) % 2, (y + dy) % NY
            yield self.here.device(pc, x, py, z), pc, py, dc * NY + dy - 1

    def small_scatter(self):
        for device, pc, py, slot in self.small_peers():
            send(
                self.small.at[pc, rows(py * SR, SR)], self.s_in.at[slot], self.ss.at[20], self.rs.at[20], device
            )

    def small_plane(self):
        c, x, y, z = self.here.core, self.here.x, self.here.y, self.here.z
        await_bytes(self.s_in, self.rs.at[20])
        mine = x * NZ + z
        self.s_sum[mine] = total(self.small[c, rows(y * SR, SR)], self.s_in)
        for device, place, slot in self.plane(1):
            send(self.s_sum.at[mine], self.s_sum.at[mine], self.ss.at[21], self.rs.at[21], device)

    def small_gather(self):
        await_bytes(self.s_sum.at[pl.ds(0, NX * NZ - 1)], self.rs.at[21])
        place = rows(self.here.y * SR, SR)
        self.small_out[self.here.core, place] = line_total(self.s_sum)
        ref = self.small_out.at[self.here.core, place]
        for device, pc, py, slot in self.small_peers():
            send(ref, ref, self.ss.at[22], self.rs.at[22], device)

    def small_done(self):
        await_bytes(self.s_in, self.rs.at[22])

    def drain(self):
        ss = self.ss
        for k in range(4):
            size, mine, landing, line, spot, axis = self.quarters[k]
            await_bytes(self.core_out.at[pl.ds(0, QUARTER)], ss.at[k])
            await_bytes(landing.at[k // 2], ss.at[4 + k])
            await_bytes(line.at[0, pl.ds(0, line.shape[1] - 1)], ss.at[8 + k])
            await_bytes(self.bytes_of(QUARTER - size), ss.at[12 + k])
            await_bytes(self.bytes_of(QUARTER), ss.at[16 + k])
        await_bytes(self.s_in, ss.at[20])
        await_bytes(self.s_sum.at[pl.ds(0, NX * NZ - 1)], ss.at[21])
        await_bytes(self.s_in, ss.at[22])


def greet(here):
    barrier = pltpu.get_barrier_semaphore()
    c, x, y, z = here.core, here.x, here.y, here.z
    west, east, across, across_west, across_east = halo_places(here)
    peers = [(device, here.lo) for device in (west, east, across)]
    for dx, dy in offsets(NX, NY):
        peers.append(here.device(c, (x + dx) % NX, (y + dy) % NY, z))
    for dx, dz in offsets(NX, NZ):
        if dz:
            peers.append(here.device(c, (x + dx) % NX, y, (z + dz) % NZ))
    for dy in range(NY):
        peers.append(here.device(1 - c, x, (y + dy) % NY, z))
    for device in peers:
        pl.semaphore_signal(barrier, inc=1, device_id=device, device_id_type=pl.DeviceIdType.MESH)
    for device in (across_west, across_east):

        @pl.when(device != here.t)
        def _():
            pl.semaphore_signal(
                barrier, inc=1, device_id=(device, here.lo), device_id_type=pl.DeviceIdType.MESH
            )

    return barrier, len(peers), (across_west, across_east)


def block_kernel(
    owned_ref, ocean_ref, fields_hbm, grad_hbm, kernel_hbm, gain_hbm, w_in_hbm, w_out_hbm, scale_hbm,
    state_hbm, grad_fields_hbm, wide_hbm, small_hbm,
    fields, grad_out, kernel, ln_gain, layer_scale, band, gband, taps, conv, inverse, normed, dproj, activated, dpreact, projected, dnormed, rowsum, weight_in,
    weight_out, edges, top, got, got_top, edges2, top2, got2, got_top2, small,
    wide, core_out, core_in, held, p_in, q_in, zz, yy, s_in, s_sum, state, grad_fields, wide_out, small_out,
    ss, rs, hs, hr, hs2, hr2, ls, os
):
    here = Place()
    barrier, greeted, maybe = greet(here)
    loads = [
        pltpu.make_async_copy(source, target, ls.at[i])
        for i, (source, target) in enumerate(
            (
                (fields_hbm, fields), (kernel_hbm, kernel), (gain_hbm, ln_gain), (scale_hbm, layer_scale),
                (grad_hbm, grad_out), (w_in_hbm, weight_in), (w_out_hbm, weight_out),
            )
        )
    ]
    for load in loads:
        load.start()
    reducer = Reducer(
        here,
        (
            wide, small, wide_out, small_out, core_out, core_in, held, p_in, q_in, zz, yy, s_in, s_sum,
        ),
        ss,
        rs,
    )
    owned = owned_ref[0]

    def slot_mask(slot):
        live = jnp.logical_and(slot < owned, ocean_ref[slot] > 0)
        return jnp.where(live, 1.0, 0.0).astype(F32)

    def clear(i, carry):
        spot = rows(i * 64, 64)
        for h in range(2):
            band[h, spot, :] = jnp.zeros((64, 128), F32)
            gband[h, spot, :] = jnp.zeros((64, 128), F32)
        return carry

    lax.fori_loop(0, BAND // 64, clear, 0)
    small[...] = jnp.zeros_like(small)
    rowsum[...] = jnp.zeros_like(rowsum)
    loads[0].wait()
    loads[1].wait()
    for a in range(KSIZE):
        line = kernel[a].astype(F32)
        for h in range(2):
            taps[h, a * KSIZE : (a + 1) * KSIZE, :] = line[:, h * 128 : (h + 1) * 128]

    def fill(i, carry):
        slot, r = i // TILE, i % TILE
        line = fields[rows(i * TILE, TILE), :].astype(F32) * slot_mask(slot)
        place = pl.ds(pl.multiple_of((EDGE + r) * WIDE + LEFT + slot * TILE, 8), TILE)
        band[0, place, :] = line[:, :128]
        band[1, place, :] = line[:, 128:]
        return carry

    lax.fori_loop(0, SLOTS * TILE, fill, 0, unroll=4)
    halo = Halo(here, band, edges, top, got, got_top, hs, hr)
    halo.gather_edges(owned)
    at_seam = jnp.logical_or(maybe[0] == here.t, maybe[1] == here.t)

    @pl.when(at_seam)
    def _():
        pl.semaphore_wait(barrier, greeted + 1)

    @pl.when(jnp.logical_not(at_seam))
    def _():
        pl.semaphore_wait(barrier, greeted + 2)

    halo.start()

    def convolve(i, carry):
        h, block = i // BLOCKS, i % BLOCKS
        result = stencil(band, taps, h, block, False, TILE + EDGE)
        for r in range(TILE):
            conv[h, pl.ds(pl.multiple_of(block_start(block) + r * TILE, 8), 8), :] = result[r]
        return carry

    lax.fori_loop(0, 2 * BLOCKS, convolve, 0)

    halo.finish(owned)

    def add_fold(i, carry):
        h, block = i // BLOCKS, i % BLOCKS
        base = LEFT - EDGE + block * 8
        sums = [None] * EDGE
        for b in range(KSIZE):
            for row in range(TILE + EDGE, TILE + 2 * EDGE):
                window = band[h, pl.ds(row * WIDE + base + b, 8), :]
                for a in range(row - TILE + 1, KSIZE):
                    term = taps[h, pl.ds(a * KSIZE + b, 1), :] * window
                    r = row - a - TILE + EDGE
                    sums[r] = term if sums[r] is None else sums[r] + term
        for r in range(EDGE):
            place = pl.ds(pl.multiple_of(block_start(block) + (TILE - EDGE + r) * TILE, 8), 8)
            conv[h, place, :] = conv[h, place, :] + sums[r]
        return carry

    lax.fori_loop(0, 2 * BLOCKS, add_fold, 0, unroll=3)
    sub = lax.broadcasted_iota(jnp.int32, (8, 128), 0)

    def edge_sums(h, base, shifts, held):
        sums = [None] * TILE
        for b in shifts:
            weights = [taps[h, pl.ds(a * KSIZE + b, 1), :] for a in range(KSIZE)]
            for row in range(EDGE, TILE + EDGE):
                window = jnp.where(held(b), band[h, pl.ds(row * WIDE + base + b, 8), :], 0.0)
                for a in range(KSIZE):
                    r = row - a
                    if 0 <= r < TILE:
                        term = weights[a] * window
                        sums[r] = term if sums[r] is None else sums[r] + term
        return sums

    def add_edges(h, carry):
        west = edge_sums(h, LEFT - EDGE, range(EDGE), lambda b: sub < EDGE - b)
        for r in range(TILE):
            place = pl.ds(r * TILE, 8)
            conv[h, place, :] = conv[h, place, :] + west[r]
        east = edge_sums(
            h, LEFT - EDGE + owned * TILE - 8, range(EDGE + 1, KSIZE), lambda b: sub >= 8 + EDGE - b
        )
        for n in range(1, SLOTS + 1):
            for r in range(TILE):
                place = pl.ds((n - 1) * TILE * TILE + r * TILE + 8, 8)
                conv[h, place, :] = conv[h, place, :] + jnp.where(owned == n, east[r], 0.0)
        return carry

    lax.fori_loop(0, 2, add_edges, 0, unroll=2)

    for load in loads[2:5]:
        load.wait()
    gain = [ln_gain[:, :128], ln_gain[:, 128:]]
    scale = [layer_scale[:, :128], layer_scale[:, 128:]]
    STEP = 128

    def norm(i, carry):
        span = rows(i * STEP, STEP)
        mask = slot_mask(i // (TILE * TILE // STEP))
        parts = [conv[h, span, :] for h in range(2)]
        mean = jnp.sum(parts[0] + parts[1], axis=1, keepdims=True) * (1.0 / C)
        centred = [part - mean for part in parts]
        variance = jnp.sum(
            centred[0] * centred[0] + centred[1] * centred[1], axis=1, keepdims=True
        ) * (1.0 / C)
        scaled = lax.rsqrt(variance + EPS)
        inverse[span, :] = jnp.broadcast_to(scaled, (STEP, 128))
        for h in range(2):
            lanes = pl.ds(h * 128, 128)
            yhat = centred[h] * scaled
            conv[h, span, :] = yhat
            normed[span, lanes] = (yhat * gain[h]).astype(BF16)
            cotangent = grad_out[span, lanes].astype(F32)
            dproj[span, lanes] = (mask * scale[h] * cotangent).astype(BF16)
        return carry

    lax.fori_loop(0, CELLS // STEP, norm, 0, unroll=2)
    loads[5].wait()
    loads[6].wait()
    across_rows = (((0,), (0,)), ((), ()))
    across_cols = (((1,), (1,)), ((), ()))

    def quarter(k, carry):
        hidden = rows(k * 256, 256)
        part_in = weight_in[:, hidden]
        part_out = weight_out[rows(k * 256, 256), :]
        for m in range(SLOTS):
            span = pl.ds(m * 256, 256)
            cells, slopes = normed[span, :], dproj[span, :]
            v = jnp.dot(cells, part_in, preferred_element_type=F32)
            dact = lax.dot_general(slopes, part_out, across_cols, preferred_element_type=F32)
            square = v * v
            t = jnp.tanh(v * (GELU_A + (GELU_A * GELU_B) * square))
            half = 0.5 + 0.5 * t
            act = (v * half).astype(BF16)
            slope = half + (v * half) * (1.0 - t) * (GELU_A + (3.0 * GELU_A * GELU_B) * square)
            dpre = (dact * slope).astype(BF16)
            activated[span, hidden] = act
            dpreact[span, hidden] = dpre
        grad_o = lax.dot_general(
            activated[:, hidden], dproj[...], across_rows, preferred_element_type=F32
        )
        grad_i = lax.dot_general(
            normed[...], dpreact[:, hidden], across_rows, preferred_element_type=F32
        )
        for h in range(2):
            spot = rows(k * 512 + h * 256, 256)
            wide[0, spot, :] = grad_i[:, h * 128 : (h + 1) * 128]
            wide[1, spot, :] = grad_o[:, h * 128 : (h + 1) * 128]
        reducer.core(k)

        if k >= 2:
            reducer.scatter(k - 2)

        return carry

    for k in range(HID // 256):
        quarter(k, 0)
    reducer.scatter(2)
    for m in range(SLOTS):
        span = pl.ds(m * 256, 256)
        dnormed[span, :] = lax.dot_general(
            dpreact[span, :], weight_in[...], across_cols, preferred_element_type=F32
        )

    reducer.scatter(3)

    def norm_back(i, carry):
        span = rows(i * STEP, STEP)
        slot, r = i // (TILE * TILE // STEP), (i % (TILE * TILE // STEP)) * (STEP // TILE)
        lanes = [pl.ds(h * 128, 128) for h in range(2)]
        back = [dnormed[span, lanes[h]] for h in range(2)]
        yhat = [conv[h, span, :] for h in range(2)]
        for h in range(2):
            rowsum[h] += jnp.sum((back[h] * yhat[h]).reshape(STEP // 8, 8, 128), axis=0)
        dhat = [back[h] * gain[h] for h in range(2)]
        mean = jnp.sum(dhat[0] + dhat[1], axis=1, keepdims=True) * (1.0 / C)
        tilt = jnp.sum(dhat[0] * yhat[0] + dhat[1] * yhat[1], axis=1, keepdims=True) * (1.0 / C)
        for h in range(2):
            grad = inverse[span, :] * (dhat[h] - mean - yhat[h] * tilt)
            grad = grad.astype(BF16).astype(F32)
            for q in range(STEP // TILE):
                place = pl.ds(
                    pl.multiple_of((EDGE + r + q) * WIDE + LEFT + slot * TILE, 8), TILE
                )
                gband[h, place, :] = grad[q * TILE : (q + 1) * TILE]
        return carry

    lax.fori_loop(0, CELLS // STEP, norm_back, 0, unroll=2)
    halo_back = Halo(here, gband, edges2, top2, got2, got_top2, hs2, hr2)
    halo_back.gather_edges(owned)
    halo_back.start()

    for m in range(SLOTS):
        span = pl.ds(m * 256, 256)
        projected[span, :] = jnp.dot(activated[span, :], weight_out[...], preferred_element_type=F32)

    def finish_state(i, carry):
        span = rows(i * STEP, STEP)
        mask = slot_mask(i // (TILE * TILE // STEP))
        for h in range(2):
            lanes = pl.ds(h * 128, 128)
            out = projected[span, lanes]
            rowsum[2 + h] += jnp.sum(
                (mask * grad_out[span, lanes].astype(F32) * out).reshape(STEP // 8, 8, 128), axis=0
            )
            kept = fields[span, lanes].astype(F32)
            state[span, lanes] = (mask * (kept + scale[h] * out)).astype(BF16)
        return carry

    lax.fori_loop(0, CELLS // STEP, finish_state, 0, unroll=2)
    write_state = pltpu.make_async_copy(state, state_hbm, os.at[0])
    write_state.start()

    def kernel_grad(i, carry):
        h, b = i // KSIZE, i % KSIZE

        def one_block(block, sums):
            sums = list(sums)
            base = LEFT + block * 8
            cots = [gband[h, pl.ds(pl.multiple_of((EDGE + r) * WIDE + base, 8), 8), :] for r in range(TILE)]
            for row in range(EDGE, TILE + 2 * EDGE):
                window = band[h, pl.ds(row * WIDE + base - EDGE + b, 8), :]
                for a in range(KSIZE):
                    if 0 <= row - a < TILE:
                        sums[a] = sums[a] + cots[row - a] * window
            return tuple(sums)

        zero = tuple(jnp.zeros((8, 128), F32) for a in range(KSIZE))
        sums = lax.fori_loop(0, BLOCKS, one_block, zero, unroll=3)
        for a in range(KSIZE):
            small[h, pl.ds(a * KSIZE + b, 1), :] = jnp.sum(sums[a], axis=0, keepdims=True)
        return carry

    lax.fori_loop(0, 2 * KSIZE, kernel_grad, 0)
    for h in range(2):
        small[h, KSIZE * KSIZE : KSIZE * KSIZE + 1, :] = jnp.sum(rowsum[h], axis=0, keepdims=True)
        small[h, KSIZE * KSIZE + 1 : KSIZE * KSIZE + 2, :] = jnp.sum(rowsum[2 + h], axis=0, keepdims=True)
    reducer.small_scatter()
    for k in range(3):
        reducer.line(k)
    halo_back.finish(owned)

    def convolve_back(i, carry):
        h, block = i % 2, i // 2
        result = stencil(gband, taps, h, block, True, TILE + 2 * EDGE)
        for r in range(TILE):
            conv[h, pl.ds(pl.multiple_of(block_start(block) + r * TILE, 8), 8), :] = result[r]
        return carry

    def finish_grad(i, carry):
        span = rows(i * STEP, STEP)
        mask = slot_mask(i // (TILE * TILE // STEP))
        for h in range(2):
            lanes = pl.ds(h * 128, 128)
            grad = mask * (grad_out[span, lanes].astype(F32) + conv[h, span, :])
            grad_fields[span, lanes] = grad.astype(BF16)
        return carry

    lax.fori_loop(0, 2, convolve_back, 0)
    reducer.line(3)
    lax.fori_loop(2, 2 * BLOCKS, convolve_back, 0)
    reducer.small_plane()
    for k in range(4):
        reducer.gather(k)
    lax.fori_loop(0, CELLS // STEP, finish_grad, 0)
    write_grad = pltpu.make_async_copy(grad_fields, grad_fields_hbm, os.at[1])
    write_grad.start()
    reducer.small_gather()
    writes = [write_state, write_grad]
    for k in range(4):
        reducer.core_back(k)
        span = pl.ds(k * QUARTER, QUARTER)
        writes.append(
            pltpu.make_async_copy(wide_out.at[here.core, span], wide_hbm.at[here.core, span], os.at[2 + k])
        )
        writes[-1].start()
    for k in range(4):
        reducer.core_done(k)
        span = pl.ds(k * QUARTER, QUARTER)
        writes.append(
            pltpu.make_async_copy(
                wide_out.at[1 - here.core, span], wide_hbm.at[1 - here.core, span], os.at[7 + k]
            )
        )
        writes[-1].start()
    reducer.small_done()
    writes.append(pltpu.make_async_copy(small_out, small_hbm, os.at[6]))
    writes[-1].start()
    reducer.drain()
    halo.drain()
    halo_back.drain()
    for write in writes:
        write.wait()


def block_call(block_count, ocean, fields, grad_out, kernel, ln_gain, w_in, w_out, layer_scale):
    vmem = pl.BlockSpec(memory_space=pltpu.VMEM)
    smem = pl.BlockSpec(memory_space=pltpu.SMEM)
    hbm = pl.BlockSpec(memory_space=pl.ANY)
    edges = pltpu.VMEM((2, EDGE, TILE, C), BF16)
    top = pltpu.VMEM((EDGE, SLOTS * TILE, C), BF16)
    got = pltpu.VMEM((4, EDGE, TILE, C), BF16)
    scratch = [
        pltpu.VMEM((CELLS, C), BF16),
        pltpu.VMEM((CELLS, C), BF16),
        pltpu.VMEM((KSIZE, KSIZE, C), BF16),
        pltpu.VMEM((1, C), F32),
        pltpu.VMEM((1, C), F32),
        pltpu.VMEM((2, BAND, 128), F32),
        pltpu.VMEM((2, BAND, 128), F32),
        pltpu.VMEM((2, 56, 128), F32),
        pltpu.VMEM((2, CELLS, 128), F32),
        pltpu.VMEM((CELLS, 128), F32),
        pltpu.VMEM((CELLS, C), BF16),
        pltpu.VMEM((CELLS, C), BF16),
        pltpu.VMEM((CELLS, HID), BF16),
        pltpu.VMEM((CELLS, HID), BF16),
        pltpu.VMEM((CELLS, C), F32),
        pltpu.VMEM((CELLS, C), F32),
        pltpu.VMEM((4, 8, 128), F32),
        pltpu.VMEM((C, HID), BF16),
        pltpu.VMEM((HID, C), BF16),
        edges, top, got, top, edges, top, got, top,
        pltpu.VMEM((2, SMALL, 128), F32),
        pltpu.VMEM((2, HALF, 128), F32),
        pltpu.VMEM((HALF, 128), BF16),
        pltpu.VMEM((HALF, 128), BF16),
        pltpu.VMEM((HALF, 128), BF16),
        pltpu.VMEM((2, NX * NY - 1, PR, 128), BF16),
        pltpu.VMEM((2, NX * NZ - 1, QR, 128), BF16),
        pltpu.VMEM((2, NZ, PR, 128), BF16),
        pltpu.VMEM((2, NY, QR, 128), BF16),
        pltpu.VMEM((2 * NY - 1, SR, 128), F32),
        pltpu.VMEM((NX * NZ, SR, 128), F32),
        pltpu.VMEM((CELLS, C), BF16),
        pltpu.VMEM((CELLS, C), BF16),
        pltpu.VMEM((2, HALF, 128), BF16),
        pltpu.VMEM((2, SMALL, 128), F32),
        pltpu.SemaphoreType.DMA((23,)),
        pltpu.SemaphoreType.DMA((23,)),
        pltpu.SemaphoreType.DMA((5,)),
        pltpu.SemaphoreType.DMA((5,)),
        pltpu.SemaphoreType.DMA((5,)),
        pltpu.SemaphoreType.DMA((5,)),
        pltpu.SemaphoreType.DMA((7,)),
        pltpu.SemaphoreType.DMA((11,)),
    ]
    return pl.pallas_call(
        block_kernel,
        out_shape=(
            jax.ShapeDtypeStruct((CELLS, C), BF16),
            jax.ShapeDtypeStruct((CELLS, C), BF16),
            jax.ShapeDtypeStruct((2, HALF, 128), BF16),
            jax.ShapeDtypeStruct((2, SMALL, 128), F32),
        ),
        in_specs=[smem, smem] + [hbm] * 7,
        out_specs=(hbm,) * 4,
        scratch_shapes=scratch,
        compiler_params=pltpu.CompilerParams(
            collective_id=1, has_side_effects=True, vmem_limit_bytes=56 * 1024 * 1024
        ),
    )(block_count, ocean, fields, grad_out, kernel, ln_gain, w_in, w_out, layer_scale)


def results_kernel(
    norm, state_hbm, fields_hbm, wide_hbm, small_hbm, state_out, fields_out, kernel_out, gain_out, in_out, out_out,
    scale_out, state, grad_fields, wide, small, grad_in, grad_out, grad_kernel, grad_gain, grad_scale, sems, loads
):
    copies = [
        pltpu.make_async_copy(state, state_out, sems.at[0]),
        pltpu.make_async_copy(grad_fields, fields_out, sems.at[1]),
    ]
    through = [
        pltpu.make_async_copy(state_hbm, state, loads.at[9]),
        pltpu.make_async_copy(fields_hbm, grad_fields, loads.at[10]),
    ]
    fetches = [pltpu.make_async_copy(small_hbm, small, loads.at[8])]
    for k in range(4):
        for side in range(2):
            span = pl.ds(k * QUARTER, QUARTER)
            fetches.append(
                pltpu.make_async_copy(
                    wide_hbm.at[side, span], wide.at[side, span], loads.at[2 * k + side]
                )
            )
    for copy in through + fetches:
        copy.start()
    for fetch, copy in zip(through, copies):
        fetch.wait()
        copy.start()
    fetches[0].wait()
    count = KSIZE * KSIZE
    for h in range(2):
        lanes = pl.ds(h * 128, 128)
        for a in range(KSIZE):
            grad_kernel[a, :, lanes] = small[h, pl.ds(a * KSIZE, KSIZE), :] * norm
        grad_gain[:, lanes] = small[h, pl.ds(count, 1), :] * norm
        grad_scale[:, lanes] = small[h, pl.ds(count + 1, 1), :] * norm
    for i, (source, target) in enumerate(
        ((grad_kernel, kernel_out), (grad_gain, gain_out), (grad_scale, scale_out))
    ):
        copies.append(pltpu.make_async_copy(source, target, sems.at[2 + i]))
        copies[-1].start()
    for k in range(4):
        for side in range(2):
            fetches[1 + 2 * k + side].wait()
            for h in range(2):
                part = wide[side, pl.ds(k * 512 + h * 256, 256), :].astype(F32) * norm
                if side:
                    grad_out[pl.ds(k * 256, 256), pl.ds(h * 128, 128)] = part
                else:
                    grad_in[:, pl.ds(k * 256 + h * 128, 128)] = part
            if side:
                spot = (pl.ds(k * 256, 256), slice(None))
                source, target = grad_out, out_out
            else:
                spot = (slice(None), pl.ds(k * 256, 256))
                source, target = grad_in, in_out
            copies.append(
                pltpu.make_async_copy(source.at[spot], target.at[spot], sems.at[5 + 2 * k + side])
            )
            copies[-1].start()
    for copy in copies:
        copy.wait()


def results_call(norm, state, grad_fields, wide, small):
    hbm = pl.BlockSpec(memory_space=pl.ANY)
    sums = [((KSIZE, KSIZE, C), F32), ((1, C), F32), ((C, HID), F32), ((HID, C), F32), ((1, C), F32)]
    return pl.pallas_call(
        functools.partial(results_kernel, norm),
        out_shape=tuple(
            jax.ShapeDtypeStruct(*spec) for spec in [((CELLS, C), BF16), ((CELLS, C), BF16)] + sums
        ),
        in_specs=[hbm] * 4,
        out_specs=(hbm,) * 7,
        scratch_shapes=[
            pltpu.VMEM((CELLS, C), BF16),
            pltpu.VMEM((CELLS, C), BF16),
            pltpu.VMEM((2, HALF, 128), BF16),
            pltpu.VMEM((2, SMALL, 128), F32),
            pltpu.VMEM((C, HID), F32),
            pltpu.VMEM((HID, C), F32),
            pltpu.VMEM((KSIZE, KSIZE, C), F32),
            pltpu.VMEM((1, C), F32),
            pltpu.VMEM((1, C), F32),
            pltpu.SemaphoreType.DMA((13,)),
            pltpu.SemaphoreType.DMA((11,)),
        ],
        compiler_params=pltpu.CompilerParams(vmem_limit_bytes=56 * 1024 * 1024),
    )(state, grad_fields, wide, small)


def shards(fields, grad_out, block_count, ocean, kernel, ln_gain, w_in, w_out, layer_scale):
    shape = fields.shape
    samples, slot_count, tile_rows, tile_cols, channels = shape
    partials = block_call(
        block_count,
        ocean,
        fields.reshape(CELLS, channels),
        grad_out.reshape(CELLS, channels),
        kernel,
        ln_gain.reshape(1, channels),
        w_in,
        w_out,
        layer_scale.reshape(1, channels),
    )
    norm = (
        samples * lax.axis_size("dp") * slot_count * lax.axis_size("tiles") * tile_rows * tile_cols
    ) ** (-0.5)
    state, grad_fields, kernel_sum, gain_sum, w_in_sum, w_out_sum, scale_sum = results_call(norm, *partials)
    return (
        state.reshape(shape),
        grad_fields.reshape(shape),
        kernel_sum,
        gain_sum.reshape(channels),
        w_in_sum,
        w_out_sum,
        scale_sum.reshape(channels),
    )


def solution(mesh):
    placed = (
        P("dp", "tiles", None, None, None),
        P("dp", "tiles", None, None, None),
        P("tiles"),
        P("tiles"),
        P(),
        P(),
        P(),
        P(),
        P(),
    )
    return jax.shard_map(
        shards,
        mesh=mesh,
        in_specs=placed,
        out_specs=(
            P("dp", "tiles", None, None, None),
            P("dp", "tiles", None, None, None),
            P(),
            P(),
            P(),
            P(),
            P(),
        ),
        check_vma=False,
    )
```
